256 devices in a mesh: role: 4 (over z_hi), grp: 2 (over z_lo), tp: 32 (over x, y, core).
Axes of the slice: x: 4, y: 4, z: 8 (z_hi: 4, z_lo: 2; z = z_hi * 2 + z_lo), core: 2. Of those that a mesh axis runs over, the one named last changes fastest.
Arguments:
- x_pre: bfloat16 [4096, 7168], P(('role', 'grp'), 'tp'), may hold values from -6 to 6
- x_dec: bfloat16 [128, 7168], P(('role', 'grp'), 'tp'), may hold values from -6 to 6
- wq_a: bfloat16 [7168, 1536], P('tp'), may hold values from -0.0625 to 0.0625
- wkv_a: bfloat16 [7168, 576], P('tp'), may hold values from -0.0625 to 0.0625
- q_gain: float32 [1536], replicated, may hold values from 0.5 to 80, as said below
- kv_gain: float32 [512], replicated, may hold values from 0.25 to 1.75
- wq_b: bfloat16 [1536, 24576], P(None, 'tp'), may hold values from -0.15625 to 0.15625
- wkv_b: bfloat16 [512, 32768], P(None, 'tp'), may hold values from -0.25 to 0.25
- wo: bfloat16 [16384, 7168], P('tp'), may hold values from -0.046875 to 0.046875
- doc_len: int32 [8, 16], replicated, may hold values from 1 to 64, 512 in all within a row
- request_docs: int32 [128], replicated, may hold values from 0 to 127, each once
Outputs:
- out_pre: bfloat16 [4096, 7168], P(('role', 'grp'), 'tp')
- out_dec: bfloat16 [128, 7168], P(('role', 'grp'), 'tp')
The draws below stay inside these ranges and needn't reach their ends.
Inputs may be any that keep to these rules, and one draw needn't show every extreme that they name: `doc_len`: row g lists the lengths of the 16 prompts packed in order into prefill group g's 512 tokens; each row sums to 512 and its longest is exactly 64. `request_docs`: prompt m is the (m % 16)-th prompt of prefill group m // 16; every prompt is continued by exactly one request. `q_gain`: positive.
All inputs are finite; a program needn't handle non-finite values.
Results may differ from the reference program's by a relative error of at most 0.03.
The reference program's roundings to bfloat16 on the way count: a program that leaves them out, or rounds other values in their place, can miss the bound.
Values may be sent and summed in bfloat16 or wider, within the bound.
A program may use at most 128 MiB of HBM per device.

```python
import math
import jax
import jax.numpy as jnp
import numpy as np
from jax import lax

D = 7168
QL = 1536
KL = 512
RD = 64
NOPE = 128
VD = 128
HEADS = 128
PTOK = 512
NDOC = 16
LMAX = 64
NG = 8
TOKENS = 4096
REQS = 128


def draw_q_gain(key, part):
    key = jax.random.fold_in(key, 11)
    low = jnp.log(jnp.float32(0.5))
    high = jnp.log(jnp.float32(2.0))
    return jnp.exp(jax.random.uniform(key, (QL,), jnp.float32, low, high))


def level_of(stream_key, extent, shards, smallest, largest):
    level, own = 1.0, jax.random.fold_in(stream_key, 6)
    for dim, parts in shards:
        draws = jnp.exp(jax.random.uniform(jax.random.fold_in(own, dim), (parts,), jnp.float32, smallest / len(shards), largest / len(shards)))
        level = level * jnp.repeat(draws, extent[dim] // parts).reshape([-1 if axis == dim else 1 for axis in range(len(extent))])
    return level


def split_up(count, total, reach, skew):
    weights = [(1 << 20) // math.isqrt(grade ** skew) + 1 for grade in range(2, count + 1)]
    rest, holding = total - reach - (count - 1), [1] * (count - 1)
    while rest > 0:
        candidates = [i for i in range(count - 1) if holding[i] < reach]
        mass, remaining = sum([weights[i] for i in candidates]), rest
        for i in candidates:
            more = min(reach - holding[i], max(1, remaining * weights[i] // mass), rest)
            holding[i] = holding[i] + more
            rest = rest - more
    return np.array([reach] + holding)


def ragged_sizes(rng, amount, total, most, slope):
    if amount == 2:
        one = jax.random.randint(rng, (), max(1, total - most), min(most, total - 1) + 1)
        return jnp.stack([one, total - one])
    sizes = jnp.asarray(split_up(amount, total, most, slope), jnp.int32)
    twos = (amount - 1) // 2
    donor, sink = sizes[1:1 + 2 * twos:2], sizes[2:2 + 2 * twos:2]
    room = jnp.minimum(donor - 1, most - sink)
    shifted = jax.random.randint(jax.random.fold_in(rng, 1), (twos,), 0, 1 << 20) % (room + 1)
    sizes = sizes.at[1:1 + 2 * twos:2].set(donor - shifted).at[2:2 + 2 * twos:2].set(sink + shifted)
    return sizes[jax.random.permutation(jax.random.fold_in(rng, 2), amount)]


def normal_values(rng, extent, scale, reach, shards=(), held_as=jnp.bfloat16):
    drawn = scale * jax.random.normal(rng, extent, jnp.float32)
    if shards:
        drawn = drawn * level_of(rng, extent, shards, -0.22, 0.18)
    return jnp.clip(drawn, -reach, reach).astype(held_as)


def setup_inputs(seed: int = 0) -> dict:
    arg_keys = jax.random.split(jax.random.key(seed), 12)
    x_pre = normal_values(arg_keys[0], (TOKENS, D), 1.0, 6.0, ((0, 8), (1, 32)))
    x_dec = normal_values(arg_keys[1], (REQS, D), 1.0, 6.0, ((0, 8), (1, 32)))
    wq_a = normal_values(arg_keys[2], (D, QL), D ** -0.5, 0.0625, ((0, 32),))
    wkv_a = normal_values(arg_keys[3], (D, KL + RD), D ** -0.5, 0.0625, ((0, 32),))
    q_gain = draw_q_gain(jax.random.fold_in(arg_keys[11], 71), 0)
    kv_gain = jnp.clip(1.0 + 0.15 * jax.random.normal(arg_keys[5], (KL,), jnp.float32), 0.25, 1.75)
    wq_b = normal_values(arg_keys[6], (QL, HEADS * (NOPE + RD)), QL ** -0.5, 0.15625, ((1, 32),))
    wkv_b = normal_values(arg_keys[7], (KL, HEADS * (NOPE + VD)), KL ** -0.5, 0.25, ((1, 32),))
    wo = normal_values(arg_keys[8], (HEADS * VD, D), (HEADS * VD) ** -0.5, 0.046875, ((0, 32),))
    doc_len = jax.vmap(lambda own: ragged_sizes(own, NDOC, PTOK, LMAX, 2))(jax.random.split(arg_keys[9], NG)).reshape((NG, NDOC)).astype(jnp.int32)
    request_docs = jax.random.permutation(arg_keys[10], REQS).astype(jnp.int32)
    return dict(x_pre=x_pre, x_dec=x_dec, wq_a=wq_a, wkv_a=wkv_a, q_gain=q_gain, kv_gain=kv_gain, wq_b=wq_b, wkv_b=wkv_b, wo=wo, doc_len=doc_len, request_docs=request_docs)


eps = 1e-06

def rms_scale(values, gain):
    return values * lax.rsqrt(lax.optimization_barrier(jnp.mean(values * values, axis=-1, keepdims=True)) + eps) * gain

def angles(positions, width):
    half = width // 2
    freq = 10000.0 ** (-jnp.arange(half, dtype=jnp.float32) / half)
    turn = positions.astype(jnp.float32)[:, None] * freq[None, :]
    return (jnp.cos(turn), jnp.sin(turn))

def rotate(values, cosine, sine):
    half = values.shape[-1] // 2
    first = values[..., :half]
    second = values[..., half:]
    return jnp.concatenate([first * cosine - second * sine, second * cosine + first * sine], axis=-1)

def layout(lengths):
    ends = jnp.cumsum(lengths).astype(jnp.int32)
    starts = ends - lengths
    rows = jnp.arange(PTOK, dtype=jnp.int32)
    seg = lax.optimization_barrier(jnp.sum((rows[:, None] >= ends[None, :]).astype(jnp.int32), axis=1))
    onehot = (seg[:, None] == jnp.arange(NDOC, dtype=jnp.int32)[None, :]).astype(jnp.int32)
    pos = rows - lax.optimization_barrier(jnp.sum(onehot * starts[None, :], axis=1))
    return (seg, pos)

def prepare(lat_q, lat_kv, positions, q_gain, kv_gain, wq_b):
    count = lat_q.shape[0]
    q_lat = rms_scale(lat_q, q_gain).astype(jnp.bfloat16)
    kv_c = rms_scale(lat_kv[:, :KL], kv_gain).astype(jnp.bfloat16)
    cosine, sine = angles(positions, RD)
    k_rope = rotate(lat_kv[:, KL:], cosine, sine).astype(jnp.bfloat16)
    query = jnp.dot(q_lat, wq_b, preferred_element_type=jnp.float32).reshape(count, -1, NOPE + RD)
    q_nope = query[..., :NOPE].astype(jnp.bfloat16)
    q_rope = rotate(query[..., NOPE:], cosine[:, None, :], sine[:, None, :]).astype(jnp.bfloat16)
    return (q_nope, q_rope, jnp.concatenate([kv_c, k_rope], axis=1))

def math_sqrt(value):
    return float(value) ** 0.5

def prefill_attend(q_nope, q_rope, kv_row, wkv_b, seg):
    count = kv_row.shape[0]
    kv = jnp.dot(kv_row[:, :KL], wkv_b, preferred_element_type=jnp.float32).astype(jnp.bfloat16)
    kv = kv.reshape(count, -1, NOPE + VD)
    k_nope = kv[..., :NOPE].astype(jnp.float32)
    values = kv[..., NOPE:].astype(jnp.float32)
    scale = 1.0 / math_sqrt(NOPE + RD)
    scores = jnp.einsum('qhd,khd->hqk', q_nope.astype(jnp.float32), k_nope)
    scores = scores + jnp.einsum('qhd,kd->hqk', q_rope.astype(jnp.float32), kv_row[:, KL:].astype(jnp.float32))
    scores = scores * scale
    rows = jnp.arange(count, dtype=jnp.int32)
    keep = (seg[:, None] == seg[None, :]) & (rows[None, :] <= rows[:, None])
    scores = jnp.where(keep[None], scores, -1e+30)
    top = lax.optimization_barrier(jnp.max(scores, axis=-1, keepdims=True))
    weights = jnp.exp(scores - top)
    probs = (weights / lax.optimization_barrier(jnp.sum(weights, axis=-1, keepdims=True))).astype(jnp.bfloat16)
    out = jnp.einsum('hqk,khd->qhd', probs.astype(jnp.float32), values).astype(jnp.bfloat16)
    return out.reshape(count, -1)

def decode_attend(dq_nope, dq_rope, own_row, cache, valid, wkv_b):
    count, heads = (dq_nope.shape[0], dq_nope.shape[1])
    table = wkv_b.reshape(KL, heads, NOPE + VD).astype(jnp.float32)
    q_abs = jnp.einsum('rhd,chd->rhc', dq_nope.astype(jnp.float32), table[..., :NOPE]).astype(jnp.bfloat16)
    latent = cache[..., :KL].astype(jnp.float32)
    rotary = cache[..., KL:].astype(jnp.float32)
    scale = 1.0 / math_sqrt(NOPE + RD)
    q_abs_f = q_abs.astype(jnp.float32)
    q_rope_f = dq_rope.astype(jnp.float32)
    scores = (jnp.einsum('rhc,rpc->rhp', q_abs_f, latent) + jnp.einsum('rhd,rpd->rhp', q_rope_f, rotary)) * scale
    scores = jnp.where(valid[:, None, :], scores, -1e+30)
    own_lat = own_row[:, :KL].astype(jnp.float32)
    own = (jnp.einsum('rhc,rc->rh', q_abs_f, own_lat) + jnp.einsum('rhd,rd->rh', q_rope_f, own_row[:, KL:].astype(jnp.float32))) * scale
    top = jnp.maximum(lax.optimization_barrier(jnp.max(scores, axis=-1)), own)
    weights = jnp.exp(scores - top[..., None])
    own_weight = jnp.exp(own - top)
    total = lax.optimization_barrier(jnp.sum(weights, axis=-1)) + own_weight
    probs = (weights / total[..., None]).astype(jnp.bfloat16)
    own_prob = (own_weight / total).astype(jnp.bfloat16)
    lat_out = jnp.einsum('rhp,rpc->rhc', probs.astype(jnp.float32), latent)
    lat_out = (lat_out + own_prob.astype(jnp.float32)[..., None] * own_lat[:, None, :]).astype(jnp.bfloat16)
    out = jnp.einsum('rhc,chd->rhd', lat_out.astype(jnp.float32), table[..., NOPE:]).astype(jnp.bfloat16)
    return out.reshape(count, -1)

def reference(x_pre, x_dec, wq_a, wkv_a, q_gain, kv_gain, wq_b, wkv_b, wo, doc_len, request_docs):
    lat_q = jnp.dot(x_pre, wq_a, preferred_element_type=jnp.float32)
    lat_kv = jnp.dot(x_pre, wkv_a, preferred_element_type=jnp.float32)
    seg, pos = jax.vmap(layout)(doc_len)
    q_nope, q_rope, kv_row = prepare(lat_q, lat_kv, pos.reshape(-1), q_gain, kv_gain, wq_b)

    def one_group(items):
        return prefill_attend(items[0], items[1], items[2], wkv_b, items[3])
    o_pre = lax.map(one_group, (q_nope.reshape(NG, PTOK, HEADS, NOPE), q_rope.reshape(NG, PTOK, HEADS, RD), kv_row.reshape(NG, PTOK, KL + RD), seg))
    o_pre = o_pre.reshape(TOKENS, HEADS * VD)
    out_pre = jnp.dot(o_pre, wo, preferred_element_type=jnp.float32).astype(jnp.bfloat16)
    ends = jnp.cumsum(doc_len, axis=1).astype(jnp.int32)
    starts = (ends - doc_len).reshape(-1)
    flat_len = doc_len.reshape(-1)
    source = request_docs // NDOC
    first_row = source * PTOK + starts[request_docs]
    length = flat_len[request_docs]
    steps = jnp.arange(LMAX, dtype=jnp.int32)
    index = jnp.minimum(first_row[:, None] + steps[None, :], TOKENS - 1)
    valid = steps[None, :] < length[:, None]
    cache = kv_row[index]
    dlat_q = jnp.dot(x_dec, wq_a, preferred_element_type=jnp.float32)
    dlat_kv = jnp.dot(x_dec, wkv_a, preferred_element_type=jnp.float32)
    dq_nope, dq_rope, own_row = prepare(dlat_q, dlat_kv, length, q_gain, kv_gain, wq_b)
    o_dec = decode_attend(dq_nope, dq_rope, own_row, cache, valid, wkv_b)
    out_dec = jnp.dot(o_dec, wo, preferred_element_type=jnp.float32).astype(jnp.bfloat16)
    return (out_pre, out_dec)
```

```python
import functools

import jax
import jax.numpy as jnp
from jax import lax
from jax.experimental import pallas as pl
from jax.experimental.pallas import tpu as pltpu
from jax.sharding import PartitionSpec as P

QL = 1536
KL = 512
RD = 64
NOPE = 128
VD = 128
NX = 4
NY = 4
W = QL + KL + 128
SPLIT = 1152
EPS = 1e-06
F32 = jnp.float32
BF16 = jnp.bfloat16
MESH = pl.DeviceIdType.MESH
VMEM_LIMIT = 58 * 2**20


def place():
    tp = lax.axis_index("tp")
    return tp, tp // 8, lax.rem(tp // 2, NY), lax.rem(tp, 2)


def tp_of(x, y, c):
    return x * 8 + y * 2 + c


def next_of(p, step):
    return lax.rem(p + step + 4, 4)


def z_peer(step):
    z = lax.axis_index("role") * 2 + lax.axis_index("grp")
    other = lax.rem(z + step, 8)
    return z, other, {"role": other // 2, "grp": lax.rem(other, 2)}


def remote(src, dst, send, recv, device):
    return pltpu.make_async_remote_copy(
        src_ref=src, dst_ref=dst, send_sem=send, recv_sem=recv, device_id=device, device_id_type=MESH
    )


def chip_peer(x, y, c, step):
    other = lax.rem(x * 4 + y + step, 16)
    return other, {"tp": tp_of(other // 4, lax.rem(other, 4), c)}


def greet(x, y, c):
    barrier = pltpu.get_barrier_semaphore()
    pl.semaphore_signal(barrier, inc=1, device_id={"tp": tp_of(x, y, 1 - c)}, device_id_type=MESH)

    def chips(step, carry):
        _, device = chip_peer(x, y, c, step)
        pl.semaphore_signal(barrier, inc=1, device_id=device, device_id_type=MESH)
        return carry

    lax.fori_loop(1, 16, chips, 0)

    def planes(step, carry):
        _, _, device = z_peer(step)
        pl.semaphore_signal(barrier, inc=1, device_id=device, device_id_type=MESH)
        return carry

    lax.fori_loop(1, 8, planes, 0)
    pl.semaphore_wait(barrier, 1 + 15 + 7)


class Ring:
    def __init__(self, data, near, far, part, pos, plus, minus, send, recv, base):
        self.data, self.near, self.far, self.part = data, near, far, part
        self.pos, self.plus, self.minus = pos, plus, minus
        self.send, self.recv, self.base = send, recv, base
        self.copies = {}

    def cut(self, ref, side):
        return ref.at[(Ellipsis, self.part[side])]

    def go(self, key, number, src, dst, device):
        copy = remote(src, dst, self.send.at[self.base + number], self.recv.at[self.base + number], device)
        copy.start()
        self.copies[key] = copy

    def start_far(self):
        chunk = self.data.at[next_of(self.pos, 2)]
        self.go("far0", 0, self.cut(chunk, 0), self.cut(self.far, 0), self.plus)
        self.go("far1", 1, self.cut(chunk, 1), self.cut(self.far, 1), self.minus)

    def start_near(self):
        up, down = self.data.at[next_of(self.pos, 1)], self.data.at[next_of(self.pos, -1)]
        self.go("up1", 2, self.cut(up, 1), self.cut(self.near.at[0], 1), self.plus)
        self.go("down0", 3, self.cut(down, 0), self.cut(self.near.at[1], 0), self.minus)

    def add(self, chunk, side):
        ref, extra = self.cut(chunk, side), self.cut(self.far, side)
        ref[...] = (ref[...].astype(F32) + extra[...].astype(F32)).astype(ref.dtype)

    def pass_on(self):
        up, down = self.data.at[next_of(self.pos, 1)], self.data.at[next_of(self.pos, -1)]
        self.copies["far0"].wait_recv()
        self.add(up, 0)
        self.go("up0", 4, self.cut(up, 0), self.cut(self.near.at[0], 0), self.plus)
        self.copies["far1"].wait_recv()
        self.add(down, 1)
        self.go("down1", 5, self.cut(down, 1), self.cut(self.near.at[1], 1), self.minus)

    def result(self, side):
        for key in ("up%d" % side, "down%d" % side):
            self.copies[key].wait_recv()
        own = self.cut(self.data.at[self.pos], side)[...].astype(F32)
        left = self.cut(self.near.at[0], side)[...].astype(F32)
        right = self.cut(self.near.at[1], side)[...].astype(F32)
        return own + (left + right)

    def close(self):
        for copy in self.copies.values():
            copy.wait_send()


def latent_rows(rows, q_gain, kv_gain, cosine, sine):
    q = rows[:, :QL]
    kv = rows[:, QL : QL + KL]
    turn = rows[:, QL + KL :]
    q = q * lax.rsqrt(jnp.mean(q * q, axis=-1, keepdims=True) + EPS) * q_gain
    kv = kv * lax.rsqrt(jnp.mean(kv * kv, axis=-1, keepdims=True) + EPS) * kv_gain
    turn = rope_tile(turn, cosine, sine)
    lane = lax.broadcasted_iota(jnp.int32, turn.shape, 1)
    turn = jnp.where(lane < RD, turn, 0.0)
    return q, kv, turn


def rope_tile(tile, cosine, sine):
    lane = lax.broadcasted_iota(jnp.int32, tile.shape, 1)
    swapped = jnp.where(lane % RD < RD // 2, pltpu.roll(tile, 96, 1), pltpu.roll(tile, 32, 1))
    return tile * cosine + swapped * sine


def down_kernel(
    xt_ref, xd_ref, wqa_ref, wkva_ref, sel_ref, qg_ref, kvg_ref, cos_ref, sin_ref, cosd_ref, sind_ref,
    out_ref, outd_ref,
    wkv_s, p0, p1, c0, c1, near0, near1, far0, far1, q0, q1, qnear0, qnear1, qfar0, qfar1,
    xd_all, dec, dec_in, tiles, tiles_in, sums_in, rows_in,
    zs, zr, cs, cr, rs, rr, ds, dr, es, er, gs, gr, ks, kr, ms, mr,
):
    tp, x, y, c = place()
    peer = {"tp": tp_of(x, y, 1 - c)}
    xp, xm = {"tp": tp_of(next_of(x, 1), y, c)}, {"tp": tp_of(next_of(x, -1), y, c)}
    yp, ym = {"tp": tp_of(x, next_of(y, 1), c)}, {"tp": tp_of(x, next_of(y, -1), c)}
    greet(x, y, c)

    z, _, _ = z_peer(0)
    xd_all[z] = xd_ref[...]

    def send_z(step, carry):
        zz, _, device = z_peer(step)
        remote(xd_ref, xd_all.at[zz], zs.at[step], zr.at[step], device).start()
        return carry

    lax.fori_loop(1, 8, send_z, 0)

    wkv_s[...] = jnp.zeros_like(wkv_s)
    wkv_s[:, : KL + RD] = wkva_ref[...]

    dims = (((0,), (0,)), ((), ()))
    order = (2, 1, 3, 0)
    core0, core1 = [], []
    for i, d in enumerate(order):
        xx = next_of(x, d)
        rows = xt_ref[:, pl.ds(pl.multiple_of(xx * 128, 128), 128)]
        for w_ref, lo, wide in ((wqa_ref, 0, QL), (wkv_s, QL, W - QL)):
            val = lax.dot_general(rows, w_ref[...], dims, preferred_element_type=F32)
            val = val.reshape(NY, 2, 2, 8, wide)
            for cc in range(2):
                p0[cc, xx, :, :, lo : lo + wide] = val[:, cc, 0]
                for yy in range(NY):
                    p1[cc, yy, xx, :, lo : lo + wide] = val[yy, cc, 1]
        copy = remote(p0.at[1 - c, xx], c0.at[xx], cs.at[i], cr.at[i], peer)
        copy.start()
        core0.append(copy)
    for i, d in enumerate(order):
        yy = next_of(y, d)
        copy = remote(p1.at[1 - c, yy], c1.at[yy], cs.at[4 + i], cr.at[4 + i], peer)
        copy.start()
        core1.append(copy)

    own0, own1 = p0.at[c], p1.at[c]
    lanes = (slice(0, SPLIT), slice(SPLIT, W))
    ring0 = Ring(own0, near0, far0, lanes, x, xp, xm, rs, rr, 0)
    ring1 = Ring(own1, near1, far1, lanes, y, yp, ym, rs, rr, 6)
    both = ((ring0, own0, c0, core0, x), (ring1, own1, c1, core1, y))

    def take_core(i):
        for ring, own, came, copies, pos in both:
            copies[i].wait_recv()
            k = next_of(pos, order[i])
            own[k] = own[k] + came[k]

    take_core(0)
    ring0.start_far()
    ring1.start_far()
    take_core(1)
    take_core(2)
    ring0.start_near()
    ring1.start_near()
    take_core(3)

    def wait_z(step, carry):
        zz, other, device = z_peer(step)
        remote(xd_ref, xd_all.at[zz], zs.at[step], zr.at[step], device).wait()
        return carry

    lax.fori_loop(1, 8, wait_z, 0)
    asked = jnp.dot(sel_ref[...], xd_all[...].reshape(128, -1), preferred_element_type=F32).astype(BF16)
    for w_ref, lo, wide in ((wqa_ref, 0, QL), (wkv_s, QL, W - QL)):
        val = jnp.dot(asked, w_ref[...], preferred_element_type=F32)
        dec[:, :, lo : lo + wide] = val.reshape(2, 8, wide)
    dec_core = remote(dec.at[1 - c], dec_in, ds.at[0], dr.at[0], peer)
    dec_core.start()

    ring0.pass_on()
    ring1.pass_on()

    dec_core.wait()
    mine = dec[c] + dec_in[...]
    chip = x * 4 + y
    for j in range(16):
        tiles[j, :, 0:128] = mine[:, 128 * j : 128 * j + 128]
        tiles[j, :, 128:256] = mine[:, QL + KL :]

    def send_tile(step, carry):
        other, device = chip_peer(x, y, c, step)
        remote(tiles.at[other], tiles_in.at[chip], es.at[step], er.at[step], device).start()
        return carry

    lax.fori_loop(1, 16, send_tile, 0)
    tiles_in[chip] = tiles[chip]

    for side in range(2):
        q0[:, :, lanes[side]] = ring0.result(side)
        q1[:, :, lanes[side]] = ring1.result(side)
    last0 = Ring(q0, qnear0, qfar0, lanes, y, yp, ym, rs, rr, 12)
    last1 = Ring(q1, qnear1, qfar1, lanes, x, xp, xm, rs, rr, 18)
    for ring in (last0, last1):
        ring.start_far()
        ring.start_near()

    def wait_tile(step, carry):
        other, device = chip_peer(x, y, c, step)
        remote(tiles.at[other], tiles_in.at[chip], es.at[step], er.at[step], device).wait()
        return carry

    lax.fori_loop(1, 16, wait_tile, 0)
    total = jnp.sum(tiles_in[...], axis=0)
    sums_in[chip] = total[:, :128]

    def send_sum(step, carry):
        other, device = chip_peer(x, y, c, step)
        remote(sums_in.at[chip], sums_in.at[chip], gs.at[step], gr.at[step], device).start()
        return carry

    lax.fori_loop(1, 16, send_sum, 0)

    last0.pass_on()
    last1.pass_on()

    parts = [[ring.result(side) for side in range(2)] for ring in (last0, last1)]
    rows = jnp.concatenate([jnp.concatenate(part, axis=1) for part in parts], axis=0)
    q, kv, turn = latent_rows(rows, qg_ref[...], kvg_ref[...], cos_ref[tp], sin_ref[tp])
    out_ref[x, y, c, :, 0:QL] = q.astype(BF16)
    out_ref[x, y, c, :, QL : QL + KL] = kv.astype(BF16)
    out_ref[x, y, c, :, QL + KL : W] = turn.astype(BF16)

    copies = []
    ka, kb = slice(0, SPLIT), slice(SPLIT, W)
    cuts = ((slice(0, 640), slice(640, SPLIT)), (slice(SPLIT, 1664), slice(1664, W)))
    count = [0]

    def push(block, device):
        n = count[0]
        count[0] += 1
        copy = remote(block, block, ks.at[n], kr.at[n], device)
        copy.start()
        copies.append(copy)
        return copy

    mate = lambda xs, ys, cols: push(out_ref.at[xs, ys, c, :, cols], peer)
    xl, xr, yl, yr = next_of(x, -1), next_of(x, 1), next_of(y, -1), next_of(y, 1)
    a_right = push(out_ref.at[x, y, c, :, ka], xp)
    a_left = push(out_ref.at[x, y, c, :, ka], xm)
    b_right = push(out_ref.at[x, y, c, :, kb], yp)
    b_left = push(out_ref.at[x, y, c, :, kb], ym)
    a_right.wait_recv()
    f1 = push(out_ref.at[xl, y, c, :, cuts[0][0]], xp)
    a_left.wait_recv()
    f2 = push(out_ref.at[xr, y, c, :, cuts[0][1]], xm)
    b_right.wait_recv()
    f3 = push(out_ref.at[x, yl, c, :, cuts[1][0]], yp)
    b_left.wait_recv()
    f4 = push(out_ref.at[x, yr, c, :, cuts[1][1]], ym)

    def wait_sum(step, carry):
        other, device = chip_peer(x, y, c, step)
        remote(sums_in.at[chip], sums_in.at[chip], gs.at[step], gr.at[step], device).wait()
        return carry

    lax.fori_loop(1, 16, wait_sum, 0)
    for j in range(16):
        rows_in[c, :, 128 * j : 128 * j + 128] = sums_in[j]
    rows_in[c, :, QL + KL : W] = total[:, 128:]
    dec_mate = remote(rows_in.at[c], rows_in.at[c], ms.at[0], mr.at[0], peer)
    dec_mate.start()

    f1.wait_recv()
    f2.wait_recv()
    f3.wait_recv()
    f4.wait_recv()
    every = slice(None)
    a2_right = push(out_ref.at[:, y, c, :, ka], yp)
    a2_left = push(out_ref.at[:, y, c, :, ka], ym)
    b2_right = push(out_ref.at[x, :, c, :, kb], xp)
    b2_left = push(out_ref.at[x, :, c, :, kb], xm)
    mates = [mate(every, y, ka), mate(x, every, kb)]
    dec_mate.wait()
    q, kv, turn = latent_rows(rows_in[...].reshape(16, W), qg_ref[...], kvg_ref[...], cosd_ref[...], sind_ref[...])
    outd_ref[:, 0:QL] = q.astype(BF16)
    outd_ref[:, QL : QL + KL] = kv.astype(BF16)
    outd_ref[:, QL + KL : W] = turn.astype(BF16)
    a2_right.wait_recv()
    g1 = push(out_ref.at[:, yl, c, :, cuts[0][0]], yp)
    a2_left.wait_recv()
    g2 = push(out_ref.at[:, yr, c, :, cuts[0][1]], ym)
    b2_right.wait_recv()
    g3 = push(out_ref.at[xl, :, c, :, cuts[1][0]], xp)
    b2_left.wait_recv()
    g4 = push(out_ref.at[xr, :, c, :, cuts[1][1]], xm)
    mates += [mate(every, yl, ka), mate(every, yr, ka), mate(xl, every, kb), mate(xr, every, kb)]
    g1.wait_recv()
    g2.wait_recv()
    mates.append(mate(every, next_of(y, 2), ka))
    g3.wait_recv()
    g4.wait_recv()
    mates.append(mate(next_of(x, 2), every, kb))
    for copy in mates:
        copy.wait_recv()
    for copy in copies:
        copy.wait_send()
    for copy in core0 + core1:
        copy.wait_send()
    for ring in (ring0, ring1, last0, last1):
        ring.close()


def down(xt, xd, wq_a, wkv_a, sel, q_gain, kv_gain, cosine, sine, cosd, sind):
    vm = pl.BlockSpec(memory_space=pltpu.VMEM)
    dma = pltpu.SemaphoreType.DMA
    return pl.pallas_call(
        down_kernel,
        out_shape=(
            jax.ShapeDtypeStruct((NX, NY, 2, 16, W), BF16),
            jax.ShapeDtypeStruct((16, W), BF16),
        ),
        in_specs=[vm] * 11,
        out_specs=(vm, vm),
        scratch_shapes=[
            pltpu.VMEM((wq_a.shape[0], W - QL), BF16),
            pltpu.VMEM((2, 4, 4, 8, W), F32),
            pltpu.VMEM((2, 4, 4, 8, W), F32),
            pltpu.VMEM((4, 4, 8, W), F32),
            pltpu.VMEM((4, 4, 8, W), F32),
            pltpu.VMEM((2, 4, 8, W), F32),
            pltpu.VMEM((2, 4, 8, W), F32),
            pltpu.VMEM((4, 8, W), F32),
            pltpu.VMEM((4, 8, W), F32),
            pltpu.VMEM((4, 8, W), F32),
            pltpu.VMEM((4, 8, W), F32),
            pltpu.VMEM((2, 8, W), F32),
            pltpu.VMEM((2, 8, W), F32),
            pltpu.VMEM((8, W), F32),
            pltpu.VMEM((8, W), F32),
            pltpu.VMEM((8,) + xd.shape, BF16),
            pltpu.VMEM((2, 8, W), F32),
            pltpu.VMEM((8, W), F32),
            pltpu.VMEM((16, 8, 256), F32),
            pltpu.VMEM((16, 8, 256), F32),
            pltpu.VMEM((16, 8, 128), F32),
            pltpu.VMEM((2, 8, W), F32),
        ]
        + [dma((n,)) for n in (8, 8, 8, 8, 24, 24, 1, 1, 16, 16, 16, 16, 24, 24, 1, 1)],
        compiler_params=pltpu.CompilerParams(
            collective_id=0, has_side_effects=True, vmem_limit_bytes=VMEM_LIMIT
        ),
        name="down",
    )(xt, xd, wq_a, wkv_a, sel, q_gain, kv_gain, cosine, sine, cosd, sind)


NT = (((1,), (1,)), ((), ()))


def split_query(query, cosine, sine):
    nope, rope = [], []
    lane = lax.broadcasted_iota(jnp.int32, (query.shape[0], 128), 1)
    for pair in range(query.shape[1] // 384):
        t0, t1, t2 = [query[:, 384 * pair + 128 * i : 384 * pair + 128 * i + 128] for i in range(3)]
        nope.append(t0.astype(BF16))
        nope.append(jnp.where(lane < 64, pltpu.roll(t1, 64, 1), pltpu.roll(t2, 64, 1)).astype(BF16))
        rope.append(rope_tile(jnp.where(lane < 64, t1, t2), cosine, sine).astype(BF16))
    return nope, rope


def attend_kernel(
    z_ref, zd_ref, wqb_ref, wkvb_ref, cos_ref, sin_ref, cosd_ref, sind_ref, segc_ref, segr_ref,
    o_ref, od_ref, kv_s,
):
    count = z_ref.shape[0]
    heads = wqb_ref.shape[1] // (NOPE + RD)
    scale = 1.0 / float(NOPE + RD) ** 0.5
    wide = NOPE + VD

    def project(i, carry):
        rows = pl.ds(pl.multiple_of(i * 128, 128), 128)
        kv = jnp.dot(z_ref[rows, QL : QL + KL], wkvb_ref[...], preferred_element_type=F32)
        kv_s[rows, :] = kv.astype(BF16)
        return carry

    lax.fori_loop(0, count // 128, project, 0)

    def block(i, carry):
        first = pl.multiple_of(i * 128, 128)
        begin = pl.multiple_of(jnp.maximum(i - 1, 0) * 128, 128)
        rows, keys = pl.ds(first, 128), pl.ds(begin, 256)
        query = jnp.dot(z_ref[rows, :QL], wqb_ref[...], preferred_element_type=F32)
        nope, rope = split_query(query, cos_ref[rows, :], sin_ref[rows, :])
        turn = z_ref[keys, QL + KL : W].astype(F32)
        turns = (turn.astype(BF16), pltpu.roll(turn, 64, 1).astype(BF16))
        own = first + lax.broadcasted_iota(jnp.int32, (128, 256), 0)
        other = begin + lax.broadcasted_iota(jnp.int32, (128, 256), 1)
        keep = (segc_ref[rows, 0:1] == segr_ref[0:1, keys]) & (other <= own)
        for h in range(heads):
            q = jnp.concatenate([nope[h], rope[h // 2]], axis=1)
            k = jnp.concatenate([kv_s[keys, wide * h : wide * h + NOPE], turns[h % 2]], axis=1)
            s = lax.dot_general(q, k, NT, preferred_element_type=F32) * scale
            s = jnp.where(keep, s, -1e30)
            e = jnp.exp(s - jnp.max(s, axis=-1, keepdims=True))
            p = (e / jnp.sum(e, axis=-1, keepdims=True)).astype(BF16)
            v = kv_s[keys, wide * h + NOPE : wide * h + wide]
            o = jnp.dot(p, v, preferred_element_type=F32)
            o_ref[rows, VD * h : VD * h + VD] = o.astype(BF16)
        return carry

    lax.fori_loop(0, count // 128, block, 0)

    query = jnp.dot(zd_ref[:, :QL], wqb_ref[...], preferred_element_type=F32)
    nope, rope = split_query(query, cosd_ref[...], sind_ref[...])
    latent, own_lat = z_ref[:, QL : QL + KL], zd_ref[:, QL : QL + KL]
    turn, own_turn = z_ref[:, QL + KL : W].astype(F32), zd_ref[:, QL + KL : W].astype(F32)
    turns = (turn.astype(BF16), pltpu.roll(turn, 64, 1).astype(BF16))
    own_turns = (own_turn.astype(BF16), pltpu.roll(own_turn, 64, 1).astype(BF16))
    doc = lax.broadcasted_iota(jnp.int32, (16, count), 0)
    keep = doc == segr_ref[0:1, :]
    diag = lax.broadcasted_iota(jnp.int32, (16, 16), 0) == lax.broadcasted_iota(jnp.int32, (16, 16), 1)
    for h in range(heads):
        up = wkvb_ref[:, wide * h : wide * h + NOPE]
        q_abs = lax.dot_general(nope[h], up, NT, preferred_element_type=F32).astype(BF16)
        s = lax.dot_general(q_abs, latent, NT, preferred_element_type=F32)
        s = (s + lax.dot_general(rope[h // 2], turns[h % 2], NT, preferred_element_type=F32)) * scale
        s = jnp.where(keep, s, -1e30)
        t = lax.dot_general(q_abs, own_lat, NT, preferred_element_type=F32)
        t = (t + lax.dot_general(rope[h // 2], own_turns[h % 2], NT, preferred_element_type=F32)) * scale
        t = jnp.where(diag, t, -1e30)
        top = jnp.maximum(jnp.max(s, axis=-1, keepdims=True), jnp.max(t, axis=-1, keepdims=True))
        e, f = jnp.exp(s - top), jnp.exp(t - top)
        total = jnp.sum(e, axis=-1, keepdims=True) + jnp.sum(f, axis=-1, keepdims=True)
        lat = jnp.dot((e / total).astype(BF16), latent, preferred_element_type=F32)
        lat = lat + jnp.dot((f / total).astype(BF16), own_lat, preferred_element_type=F32)
        down_v = wkvb_ref[:, wide * h + NOPE : wide * h + wide]
        o = jnp.dot(lat.astype(BF16), down_v, preferred_element_type=F32)
        od_ref[:, VD * h : VD * h + VD] = o.astype(BF16)


def attend(z, zd, wq_b, wkv_b, cosine, sine, cosd, sind, segc, segr):
    vm = pl.BlockSpec(memory_space=pltpu.VMEM)
    return pl.pallas_call(
        attend_kernel,
        out_shape=(
            jax.ShapeDtypeStruct((z.shape[0], 512), BF16),
            jax.ShapeDtypeStruct((16, 512), BF16),
        ),
        in_specs=[vm] * 10,
        out_specs=(vm, vm),
        scratch_shapes=[pltpu.VMEM((z.shape[0], wkv_b.shape[1]), BF16)],
        compiler_params=pltpu.CompilerParams(vmem_limit_bytes=VMEM_LIMIT),
        name="attend",
    )(z, zd, wq_b, wkv_b, cosine, sine, cosd, sind, segc, segr)


def up_kernel(
    o_ref, od_ref, wo_ref, sel_ref, out_ref, outd_ref,
    t0, t1, c0, c1, near0, near1, far0, far1, q0, q1, qnear0, qnear1, qfar0, qfar1,
    dd, dt, dc, dn, dz,
    cs, cr, rs, rr, ds, dr, es, er, zs, zr,
):
    tp, x, y, c = place()
    cols = 224
    peer = {"tp": tp_of(x, y, 1 - c)}
    xp, xm = {"tp": tp_of(next_of(x, 1), y, c)}, {"tp": tp_of(next_of(x, -1), y, c)}
    yp, ym = {"tp": tp_of(x, next_of(y, 1), c)}, {"tp": tp_of(x, next_of(y, -1), c)}
    greet(x, y, c)

    dims = (((0,), (1,)), ((), ()))
    dd[...] = jnp.zeros_like(dd)

    def part(k, carry):
        w = wo_ref[:, pl.ds(pl.multiple_of(k * 896, 128), 896)]
        xx, yy = k // 2, 2 * lax.rem(k, 2)
        dd[:, :896] = jnp.dot(od_ref[...], w, preferred_element_type=F32)
        for j in range(4):
            at = 224 * j // 128 * 128
            v = dd[:, at : at + 384]
            if 224 * j - at:
                v = pltpu.roll(v, 384 - (224 * j - at), 1)
            dt[j % 2, 2 * k + j // 2] = v[:, :256].astype(BF16)
        val = lax.dot_general(w, o_ref[...], dims, preferred_element_type=F32).astype(BF16)
        for j in range(4):
            blk = val[224 * j : 224 * j + 224]
            t0[j % 2, xx, yy + j // 2] = blk[:, :256]
            t1[j % 2, yy + j // 2, xx] = blk[:, 256:]
        return carry

    lax.fori_loop(0, 8, part, 0)

    dec_core = remote(dt.at[1 - c], dc, ds.at[0], dr.at[0], peer)
    dec_core.start()
    order = (2, 1, 3, 0)
    core0, core1 = [], []
    for i, d in enumerate(order):
        for n, (t, came, pos, copies) in enumerate(((t0, c0, x, core0), (t1, c1, y, core1))):
            k = next_of(pos, d)
            copy = remote(t.at[1 - c, k], came.at[k], cs.at[2 * i + n], cr.at[2 * i + n], peer)
            copy.start()
            copies.append(copy)
    own0, own1 = t0.at[c], t1.at[c]
    lanes = (slice(0, 128), slice(128, 256))
    ring0 = Ring(own0, near0, far0, lanes, x, xp, xm, rs, rr, 0)
    ring1 = Ring(own1, near1, far1, lanes, y, yp, ym, rs, rr, 6)
    both = ((ring0, own0, c0, core0, x), (ring1, own1, c1, core1, y))

    dec_core.wait()
    chip = x * 4 + y
    dt[c] = (dt[c].astype(F32) + dc[...].astype(F32)).astype(BF16)

    def send_tile(step, carry):
        other, device = chip_peer(x, y, c, step)
        remote(dt.at[c, other], dn.at[chip], es.at[step], er.at[step], device).start()
        return carry

    lax.fori_loop(1, 16, send_tile, 0)
    dn[chip] = dt[c, chip]

    def take_core(i):
        for ring, own, came, copies, pos in both:
            copies[i].wait_recv()
            k = next_of(pos, order[i])
            own[k] = (own[k].astype(F32) + came[k].astype(F32)).astype(BF16)

    take_core(0)
    ring0.start_far()
    ring1.start_far()
    take_core(1)
    take_core(2)
    ring0.start_near()
    ring1.start_near()
    take_core(3)

    def wait_tile(step, carry):
        other, device = chip_peer(x, y, c, step)
        remote(dt.at[c, other], dn.at[chip], es.at[step], er.at[step], device).wait()
        return carry

    lax.fori_loop(1, 16, wait_tile, 0)
    z, _, _ = z_peer(0)
    dz[z] = jnp.sum(dn[...].astype(F32), axis=0).astype(BF16)

    def send_z(step, carry):
        zz, _, device = z_peer(step)
        remote(dz.at[zz], dz.at[zz], zs.at[step], zr.at[step], device).start()
        return carry

    lax.fori_loop(1, 8, send_z, 0)

    ring0.pass_on()
    ring1.pass_on()
    for side in range(2):
        q0[:, :, lanes[side]] = ring0.result(side).astype(BF16)
        q1[:, :, lanes[side]] = ring1.result(side).astype(BF16)
    last0 = Ring(q0, qnear0, qfar0, lanes, y, yp, ym, rs, rr, 12)
    last1 = Ring(q1, qnear1, qfar1, lanes, x, xp, xm, rs, rr, 18)
    for ring in (last0, last1):
        ring.start_far()
        ring.start_near()

    def wait_z(step, carry):
        zz, _, device = z_peer(step)
        remote(dz.at[zz], dz.at[zz], zs.at[step], zr.at[step], device).wait()
        return carry

    lax.fori_loop(1, 8, wait_z, 0)
    asked = jnp.dot(sel_ref[...], dz[...].reshape(128, 256), preferred_element_type=F32)
    outd_ref[...] = asked[:, :cols].astype(BF16)

    last0.pass_on()
    last1.pass_on()
    for h, ring in enumerate((last0, last1)):
        for side in range(2):
            at = 256 * h + 128 * side
            out_ref[:, at : at + 128] = ring.result(side).astype(BF16)
    for copy in core0 + core1:
        copy.wait_send()
    for ring in (ring0, ring1, last0, last1):
        ring.close()


def up(o, od, wo, sel):
    vm = pl.BlockSpec(memory_space=pltpu.VMEM)
    dma = pltpu.SemaphoreType.DMA
    return pl.pallas_call(
        up_kernel,
        out_shape=(
            jax.ShapeDtypeStruct((224, 512), BF16),
            jax.ShapeDtypeStruct((16, 224), BF16),
        ),
        in_specs=[vm] * 4,
        out_specs=(vm, vm),
        scratch_shapes=[
            pltpu.VMEM((2, 4, 4, 224, 256), BF16),
            pltpu.VMEM((2, 4, 4, 224, 256), BF16),
            pltpu.VMEM((4, 4, 224, 256), BF16),
            pltpu.VMEM((4, 4, 224, 256), BF16),
            pltpu.VMEM((2, 4, 224, 256), BF16),
            pltpu.VMEM((2, 4, 224, 256), BF16),
            pltpu.VMEM((4, 224, 256), BF16),
            pltpu.VMEM((4, 224, 256), BF16),
            pltpu.VMEM((4, 224, 256), BF16),
            pltpu.VMEM((4, 224, 256), BF16),
            pltpu.VMEM((2, 224, 256), BF16),
            pltpu.VMEM((2, 224, 256), BF16),
            pltpu.VMEM((224, 256), BF16),
            pltpu.VMEM((224, 256), BF16),
            pltpu.VMEM((16, 1024), F32),
            pltpu.VMEM((2, 16, 16, 256), BF16),
            pltpu.VMEM((16, 16, 256), BF16),
            pltpu.VMEM((16, 16, 256), BF16),
            pltpu.VMEM((8, 16, 256), BF16),
        ]
        + [dma((n,)) for n in (8, 8, 24, 24, 1, 1, 16, 16, 8, 8)],
        compiler_params=pltpu.CompilerParams(
            collective_id=1, has_side_effects=True, vmem_limit_bytes=VMEM_LIMIT
        ),
        name="up",
    )(o, od, wo, sel)


def tables(positions):
    half = RD // 2
    freq = 10000.0 ** (-jnp.arange(half, dtype=F32) / half)
    turn = positions.astype(F32)[:, None] * freq[None, :]
    cosine, sine = jnp.cos(turn), jnp.sin(turn)
    return jnp.tile(cosine, (1, 4)), jnp.tile(jnp.concatenate([-sine, sine], axis=1), (1, 2))


def per_device(x_pre, x_dec, wq_a, wkv_a, q_gain, kv_gain, wq_b, wkv_b, wo, doc_len, request_docs):
    count = x_pre.shape[0]
    docs = doc_len.shape[1]
    group = lax.axis_index("role") * lax.axis_size("grp") + lax.axis_index("grp")
    lengths = lax.dynamic_slice_in_dim(doc_len, group, 1, 0)[0]
    ends = jnp.cumsum(lengths)
    starts = ends - lengths
    rows = jnp.arange(count, dtype=jnp.int32)
    past = rows[:, None] >= ends[None, :]
    seg = jnp.sum(past.astype(jnp.int32), axis=1)
    pos = rows - jnp.sum(jnp.where(past, lengths[None, :], 0), axis=1)
    cosine, sine = tables(jnp.concatenate([pos, lengths]))
    cosd, sind = cosine[count:], sine[count:]
    cosine, sine = cosine[:count], sine[:count]
    number = group * docs + jnp.arange(docs, dtype=jnp.int32)
    sel_in = (number[:, None] == request_docs[None, :]).astype(BF16)
    asked = lax.dynamic_slice_in_dim(request_docs, group * docs, docs, 0)
    sel_out = (asked[:, None] == jnp.arange(request_docs.shape[0], dtype=jnp.int32)[None, :]).astype(BF16)

    z, zd = down(
        x_pre.T, x_dec, wq_a, wkv_a, sel_in, q_gain.reshape(1, -1), kv_gain.reshape(1, -1),
        cosine.reshape(32, 16, 128), sine.reshape(32, 16, 128), cosd, sind,
    )
    o, od = attend(
        z.reshape(count, W), zd, wq_b, wkv_b, cosine, sine, cosd, sind,
        jnp.broadcast_to(seg[:, None], (count, 128)), jnp.broadcast_to(seg[None, :], (8, count)),
    )
    out_t, out_dec = up(o, od, wo, sel_out)
    return out_t.T, out_dec


def solution(mesh):
    placed = (
        P(("role", "grp"), "tp"),
        P(("role", "grp"), "tp"),
        P("tp", None),
        P("tp", None),
        P(),
        P(),
        P(None, "tp"),
        P(None, "tp"),
        P("tp", None),
        P(),
        P(),
    )
    return jax.shard_map(
        per_device,
        mesh=mesh,
        in_specs=placed,
        out_specs=(P(("role", "grp"), "tp"), P(("role", "grp"), "tp")),
        check_vma=False,
    )
```

```python
import jax
import jax.numpy as jnp
import numpy as np
from jax import lax
from jax.experimental import pallas as pl
from jax.experimental.pallas import tpu as pltpu
from jax.sharding import PartitionSpec as P

QL = 1536
KL = 512
RD = 64
NOPE = 128
VD = 128
NX = 4
NY = 4
W = QL + KL + 128
SPLIT = 1152
EPS = 1e-06
F32 = jnp.float32
BF16 = jnp.bfloat16
MESH = pl.DeviceIdType.MESH
VMEM_LIMIT = 58 * 2**20


def place():
    tp = lax.axis_index("tp")
    return tp, tp // 8, lax.rem(tp // 2, NY), lax.rem(tp, 2)


def tp_of(x, y, c):
    return x * 8 + y * 2 + c


def next_of(p, step):
    return lax.rem(p + step + 4, 4)


def z_peer(step):
    z = lax.axis_index("role") * 2 + lax.axis_index("grp")
    other = lax.rem(z + step, 8)
    return z, other, {"role": other // 2, "grp": lax.rem(other, 2)}


def remote(src, dst, send, recv, device):
    return pltpu.make_async_remote_copy(
        src_ref=src, dst_ref=dst, send_sem=send, recv_sem=recv, device_id=device, device_id_type=MESH
    )


def chip_peer(x, y, c, step):
    other = lax.rem(x * 4 + y + step, 16)
    return other, {"tp": tp_of(other // 4, lax.rem(other, 4), c)}


def greet_start(x, y, c):
    barrier = pltpu.get_barrier_semaphore()
    pl.semaphore_signal(barrier, inc=1, device_id={"tp": tp_of(x, y, 1 - c)}, device_id_type=MESH)

    def chips(step, carry):
        _, device = chip_peer(x, y, c, step)
        pl.semaphore_signal(barrier, inc=1, device_id=device, device_id_type=MESH)
        return carry

    lax.fori_loop(1, 16, chips, 0)

    def planes(step, carry):
        _, _, device = z_peer(step)
        pl.semaphore_signal(barrier, inc=1, device_id=device, device_id_type=MESH)
        return carry

    lax.fori_loop(1, 8, planes, 0)


def greet_wait():
    pl.semaphore_wait(pltpu.get_barrier_semaphore(), 1 + 15 + 7)


class Ring:
    def __init__(self, data, near, far, part, pos, plus, minus, send, recv, base):
        self.data, self.near, self.far, self.part = data, near, far, part
        self.pos, self.plus, self.minus = pos, plus, minus
        self.send, self.recv, self.base = send, recv, base
        self.copies = {}

    def cut(self, ref, side):
        return ref.at[(Ellipsis, self.part[side])]

    def go(self, key, number, src, dst, device):
        copy = remote(src, dst, self.send.at[self.base + number], self.recv.at[self.base + number], device)
        copy.start()
        self.copies[key] = copy

    def start_far(self):
        chunk = self.data.at[next_of(self.pos, 2)]
        self.go("far0", 0, self.cut(chunk, 0), self.cut(self.far, 0), self.plus)
        self.go("far1", 1, self.cut(chunk, 1), self.cut(self.far, 1), self.minus)

    def start_near(self):
        up, down = self.data.at[next_of(self.pos, 1)], self.data.at[next_of(self.pos, -1)]
        self.go("up1", 2, self.cut(up, 1), self.cut(self.near.at[0], 1), self.plus)
        self.go("down0", 3, self.cut(down, 0), self.cut(self.near.at[1], 0), self.minus)

    def add(self, chunk, side):
        ref, extra = self.cut(chunk, side), self.cut(self.far, side)
        ref[...] = (ref[...].astype(F32) + extra[...].astype(F32)).astype(ref.dtype)

    def pass_on(self):
        up, down = self.data.at[next_of(self.pos, 1)], self.data.at[next_of(self.pos, -1)]
        self.copies["far0"].wait_recv()
        self.add(up, 0)
        self.go("up0", 4, self.cut(up, 0), self.cut(self.near.at[0], 0), self.plus)
        self.copies["far1"].wait_recv()
        self.add(down, 1)
        self.go("down1", 5, self.cut(down, 1), self.cut(self.near.at[1], 1), self.minus)

    def result(self, side):
        for key in ("up%d" % side, "down%d" % side):
            self.copies[key].wait_recv()
        own = self.cut(self.data.at[self.pos], side)[...].astype(F32)
        left = self.cut(self.near.at[0], side)[...].astype(F32)
        right = self.cut(self.near.at[1], side)[...].astype(F32)
        return own + (left + right)

    def close(self):
        for copy in self.copies.values():
            copy.wait_send()


def latent_rows(rows, q_gain, kv_gain, cosine, sine):
    q = rows[:, :QL]
    kv = rows[:, QL : QL + KL]
    turn = rows[:, QL + KL :]
    q = q * lax.rsqrt(jnp.mean(q * q, axis=-1, keepdims=True) + EPS) * q_gain
    kv = kv * lax.rsqrt(jnp.mean(kv * kv, axis=-1, keepdims=True) + EPS) * kv_gain
    turn = rope_tile(turn, cosine, sine)
    lane = lax.broadcasted_iota(jnp.int32, turn.shape, 1)
    turn = jnp.where(lane < RD, turn, 0.0)
    return q, kv, turn


def rope_tile(tile, cosine, sine):
    lane = lax.broadcasted_iota(jnp.int32, tile.shape, 1)
    swapped = jnp.where(lane % RD < RD // 2, pltpu.roll(tile, 96, 1), pltpu.roll(tile, 32, 1))
    return tile * cosine + swapped * sine


def turn_tables(pos, freq):
    turn = pos * freq
    lane = lax.broadcasted_iota(jnp.int32, turn.shape, 1)
    sine = jnp.sin(turn)
    return jnp.cos(turn), jnp.where(lane % RD < RD // 2, -sine, sine)


NT = (((1,), (1,)), ((), ()))
TN = (((0,), (0,)), ((), ()))


def split_query(query, cosine, sine):
    nope, rope = [], []
    lane = lax.broadcasted_iota(jnp.int32, (query.shape[0], 128), 1)
    for pair in range(query.shape[1] // 384):
        t0, t1, t2 = [query[:, 384 * pair + 128 * i : 384 * pair + 128 * i + 128] for i in range(3)]
        nope.append(t0.astype(BF16))
        nope.append(jnp.where(lane < 64, pltpu.roll(t1, 64, 1), pltpu.roll(t2, 64, 1)).astype(BF16))
        rope.append(rope_tile(jnp.where(lane < 64, t1, t2), cosine, sine).astype(BF16))
    return nope, rope


def whole_kernel(
    xt_ref, xd_ref, wqa_ref, wkva_ref, qg_ref, kvg_ref, freq_ref, len_ref, docs_ref, wqb_hbm, wkvb_hbm, wo_hbm,
    out_ref, outd_ref,
    wqb, wkvb, wo, wot, wkv_s, p0, p1, c0, c1, near0, near1, far0, far1, q0, q1, in0, in1,
    xd_all, dec, dec_in, tiles, tiles_in, sums_in, rows_in,
    zb, zd, pos_s, cos_s, sin_s, kv_s, o_s, od_s,
    t0, t1, tc0, tc1, tnear0, tnear1, tfar0, tfar1, tq0, tq1, tqnear0, tqnear1, tqfar0, tqfar1,
    dd, dt, dc, dn, dz,
    ws, zs, zr, cs, cr, rs, rr, ds, dr, es, er, gs, gr, ks, kr, ms, mr,
    us, ur, vs, vr, fs, fr, hs, hr, ys, yr,
):
    tp, x, y, c = place()
    chip = x * 4 + y
    z, _, _ = z_peer(0)
    peer = {"tp": tp_of(x, y, 1 - c)}
    xp, xm = {"tp": tp_of(next_of(x, 1), y, c)}, {"tp": tp_of(next_of(x, -1), y, c)}
    yp, ym = {"tp": tp_of(x, next_of(y, 1), c)}, {"tp": tp_of(x, next_of(y, -1), c)}
    greet_start(x, y, c)
    loads = [
        pltpu.make_async_copy(src, dst, ws.at[i])
        for i, (src, dst) in enumerate(((wo_hbm, wo), (wkvb_hbm, wkvb), (wqb_hbm, wqb)))
    ]
    for load in loads:
        load.start()

    wkv_s[...] = jnp.zeros_like(wkv_s)
    wkv_s[:, : KL + RD] = wkva_ref[...]
    order = (2, 1, 3, 0)
    core0, core1 = [], []
    for i, d in enumerate(order):
        xx = next_of(x, d)
        rows = xt_ref[:, pl.ds(pl.multiple_of(xx * 128, 128), 128)]
        for w_ref, lo, wide in ((wqa_ref, 0, QL), (wkv_s, QL, W - QL)):
            val = lax.dot_general(rows, w_ref[...], TN, preferred_element_type=F32)
            val = val.reshape(NY, 2, 2, 8, wide)
            for cc in range(2):
                p0[cc, xx, :, :, lo : lo + wide] = val[:, cc, 0]
                for yy in range(NY):
                    p1[cc, yy, xx, :, lo : lo + wide] = val[yy, cc, 1]
        if i == 0:
            greet_wait()
            xd_all[z] = xd_ref[...]

            def send_z(step, carry):
                zz, _, device = z_peer(step)
                remote(xd_ref, xd_all.at[zz], zs.at[step], zr.at[step], device).start()
                return carry

            lax.fori_loop(1, 8, send_z, 0)
        copy = remote(p0.at[1 - c, xx], c0.at[xx], cs.at[i], cr.at[i], peer)
        copy.start()
        core0.append(copy)
    for i, d in enumerate(order):
        yy = next_of(y, d)
        copy = remote(p1.at[1 - c, yy], c1.at[yy], cs.at[4 + i], cr.at[4 + i], peer)
        copy.start()
        core1.append(copy)

    own0, own1 = p0.at[c], p1.at[c]
    lanes = (slice(0, SPLIT), slice(SPLIT, W))
    ring0 = Ring(own0, near0, far0, lanes, x, xp, xm, rs, rr, 0)
    ring1 = Ring(own1, near1, far1, lanes, y, yp, ym, rs, rr, 6)
    both = ((ring0, own0, c0, core0, x), (ring1, own1, c1, core1, y))

    def take_core(i):
        for ring, own, came, copies, pos in both:
            copies[i].wait_recv()
            k = next_of(pos, order[i])
            own[k] = own[k] + came[k]

    take_core(0)
    ring0.start_far()
    ring1.start_far()
    take_core(1)
    take_core(2)
    ring0.start_near()
    ring1.start_near()
    take_core(3)

    def wait_z(step, carry):
        zz, other, device = z_peer(step)
        remote(xd_ref, xd_all.at[zz], zs.at[step], zr.at[step], device).wait()
        return carry

    lax.fori_loop(1, 8, wait_z, 0)
    ii = lax.broadcasted_iota(jnp.int32, (16, 128), 0)
    jj = lax.broadcasted_iota(jnp.int32, (16, 128), 1)
    docs = docs_ref[...].reshape(1, 128)
    sel_in = jnp.where(docs == z * 16 + ii, 1.0, 0.0).astype(BF16)
    asked = jnp.dot(sel_in, xd_all[...].reshape(128, -1), preferred_element_type=F32).astype(BF16)
    for w_ref, lo, wide in ((wqa_ref, 0, QL), (wkv_s, QL, W - QL)):
        val = jnp.dot(asked, w_ref[...], preferred_element_type=F32)
        dec[:, :, lo : lo + wide] = val.reshape(2, 8, wide)
    dec_core = remote(dec.at[1 - c], dec_in, ds.at[0], dr.at[0], peer)
    dec_core.start()

    lens = len_ref[pl.ds(z, 1), :].astype(F32)
    i16 = lax.broadcasted_iota(jnp.int32, (16, 16), 0)
    j16 = lax.broadcasted_iota(jnp.int32, (16, 16), 1)
    spread = jnp.broadcast_to(lens, (16, 16))
    len_col = jnp.sum(jnp.where(i16 == j16, spread, 0.0), axis=1, keepdims=True)
    end_col = jnp.sum(jnp.where(j16 <= i16, spread, 0.0), axis=1, keepdims=True)
    end_row = jnp.sum(jnp.where(i16 <= j16, jnp.broadcast_to(len_col, (16, 16)), 0.0), axis=0, keepdims=True)
    token = lax.broadcasted_iota(jnp.int32, (512, 16), 0).astype(F32)
    begun = jnp.sum(jnp.where(token >= end_row, jnp.broadcast_to(lens, (512, 16)), 0.0), axis=1, keepdims=True)
    pos = lax.broadcasted_iota(jnp.int32, (512, 128), 0).astype(F32) - begun
    pos_s[...] = pos
    freq = freq_ref[...]
    for i in range(4):
        part = pl.ds(128 * i, 128)
        cos_s[part, :], sin_s[part, :] = turn_tables(pos_s[part, :], freq)
    cosd, sind = turn_tables(jnp.broadcast_to(len_col, (16, 128)), freq)

    ring0.pass_on()
    ring1.pass_on()

    dec_core.wait()
    mine = dec[c] + dec_in[...]
    for j in range(16):
        tiles[j, :, 0:128] = mine[:, 128 * j : 128 * j + 128]
        tiles[j, :, 128:256] = mine[:, QL + KL :]

    def send_tile(step, carry):
        other, device = chip_peer(x, y, c, step)
        remote(tiles.at[other], tiles_in.at[chip], es.at[step], er.at[step], device).start()
        return carry

    lax.fori_loop(1, 16, send_tile, 0)
    tiles_in[chip] = tiles[chip]

    loads[0].wait()

    def turn_wo(k, carry):
        cut = pl.multiple_of(k * 896, 128)
        wot[pl.ds(cut, 896), :] = wo[:, pl.ds(cut, 896)].T
        return carry

    lax.fori_loop(0, 3, turn_wo, 0)

    for side in range(2):
        q0[:, :, lanes[side]] = ring0.result(side)
        q1[:, :, lanes[side]] = ring1.result(side)
    finals = []
    for h, (q, box, pos_h, dev) in enumerate(
        ((q0, in0, y, lambda d: tp_of(x, next_of(y, d), c)), (q1, in1, x, lambda d: tp_of(next_of(x, d), y, c)))
    ):
        for d in (2, 1, 3):
            n = 12 + 3 * h + d - 1
            copy = remote(q.at[next_of(pos_h, d)], box.at[d - 1], rs.at[n], rr.at[n], {"tp": dev(d)})
            copy.start()
            finals.append(copy)

    def wait_tile(step, carry):
        other, device = chip_peer(x, y, c, step)
        remote(tiles.at[other], tiles_in.at[chip], es.at[step], er.at[step], device).wait()
        return carry

    lax.fori_loop(1, 16, wait_tile, 0)
    total = jnp.sum(tiles_in[...], axis=0)
    sums_in[chip] = total[:, :128]

    def send_sum(step, carry):
        other, device = chip_peer(x, y, c, step)
        remote(sums_in.at[chip], sums_in.at[chip], gs.at[step], gr.at[step], device).start()
        return carry

    lax.fori_loop(1, 16, send_sum, 0)

    for copy in finals:
        copy.wait_recv()
    rows = jnp.concatenate(
        [q0[y] + (in0[0] + in0[1]) + in0[2], q1[x] + (in1[0] + in1[1]) + in1[2]], axis=0
    )
    own_rows = pl.ds(pl.multiple_of(tp * 16, 16), 16)
    q_gain, kv_gain = qg_ref[...].reshape(1, QL), kvg_ref[...].reshape(1, KL)
    q, kv, turn = latent_rows(rows, q_gain, kv_gain, cos_s[own_rows, :], sin_s[own_rows, :])
    zb[x, y, c, :, 0:QL] = q.astype(BF16)
    zb[x, y, c, :, QL : QL + KL] = kv.astype(BF16)
    zb[x, y, c, :, QL + KL : W] = turn.astype(BF16)

    copies = []
    ka, kb = slice(0, SPLIT), slice(SPLIT, W)
    every = slice(None)

    def push(block, device):
        n = len(copies)
        copy = remote(block, block, ks.at[n], kr.at[n], device)
        copy.start()
        copies.append(copy)
        return copy

    def along_x(d):
        return {"tp": tp_of(next_of(x, d), y, c)}

    def along_y(d):
        return {"tp": tp_of(x, next_of(y, d), c)}

    from_x, from_y = {}, {}
    for d in (1, 3, 2):
        from_x[d] = push(zb.at[x, y, c], along_x(d))
        from_y[d] = push(zb.at[x, y, c], along_y(d))
    diag_a, diag_b = [], []
    for d in (1, 3, 2):
        xn, yn = next_of(x, -d), next_of(y, -d)
        from_x[d].wait_recv()
        diag_a += [(e, push(zb.at[xn, y, c, :, ka], along_y(e))) for e in (1, 3, 2)]
        from_y[d].wait_recv()
        diag_b += [(e, push(zb.at[x, yn, c, :, kb], along_x(e))) for e in (1, 3, 2)]
    mates = [push(zb.at[:, y, c, :, ka], peer), push(zb.at[x, :, c, :, kb], peer)]

    def wait_sum(step, carry):
        other, device = chip_peer(x, y, c, step)
        remote(sums_in.at[chip], sums_in.at[chip], gs.at[step], gr.at[step], device).wait()
        return carry

    lax.fori_loop(1, 16, wait_sum, 0)
    for j in range(16):
        rows_in[c, :, 128 * j : 128 * j + 128] = sums_in[j]
    rows_in[c, :, QL + KL : W] = total[:, 128:]
    dec_mate = remote(rows_in.at[c], rows_in.at[c], ms.at[0], mr.at[0], peer)
    dec_mate.start()
    lax.fori_loop(3, 6, turn_wo, 0)
    dec_mate.wait()
    q, kv, turn = latent_rows(rows_in[...].reshape(16, W), q_gain, kv_gain, cosd, sind)
    zd[:, 0:QL] = q.astype(BF16)
    zd[:, QL : QL + KL] = kv.astype(BF16)
    zd[:, QL + KL : W] = turn.astype(BF16)
    lax.fori_loop(6, 8, turn_wo, 0)
    for e in (1, 3, 2):
        for number, copy in diag_a:
            if number == e:
                copy.wait_recv()
        mates.append(push(zb.at[:, next_of(y, -e), c, :, ka], peer))
        for number, copy in diag_b:
            if number == e:
                copy.wait_recv()
        mates.append(push(zb.at[next_of(x, -e), :, c, :, kb], peer))
    for load in loads[1:]:
        load.wait()
    for copy in mates:
        copy.wait_recv()

    heads = 4
    scale = 1.0 / float(NOPE + RD) ** 0.5
    wide = NOPE + VD

    def project(i, carry):
        kv = jnp.dot(zb[i, :, :, :, QL : QL + KL].reshape(128, KL), wkvb[...], preferred_element_type=F32)
        kv_s[pl.ds(pl.multiple_of(i * 128, 128), 128), :] = kv.astype(BF16)
        return carry

    def block(i, carry):
        first = pl.multiple_of(i * 128, 128)
        before = jnp.maximum(i - 1, 0)
        begin = pl.multiple_of(before * 128, 128)
        rows, keys = pl.ds(first, 128), pl.ds(begin, 256)
        query = jnp.dot(zb[i, :, :, :, :QL].reshape(128, QL), wqb[...], preferred_element_type=F32)
        nope, rope = split_query(query, cos_s[rows, :], sin_s[rows, :])
        turn = zb[pl.ds(before, 2), :, :, :, QL + KL : W].reshape(256, 128).astype(F32)
        turns = (turn.astype(BF16), pltpu.roll(turn, 64, 1).astype(BF16))
        own = first + lax.broadcasted_iota(jnp.int32, (128, 256), 0)
        other = begin + lax.broadcasted_iota(jnp.int32, (128, 256), 1)
        back = (own - other).astype(F32)
        keep = (back >= 0) & (back <= jnp.concatenate([pos_s[rows, :]] * 2, axis=1))
        for h in range(heads):
            q = jnp.concatenate([nope[h], rope[h // 2]], axis=1)
            k = jnp.concatenate([kv_s[keys, wide * h : wide * h + NOPE], turns[h % 2]], axis=1)
            s = lax.dot_general(q, k, NT, preferred_element_type=F32) * scale
            s = jnp.where(keep, s, -1e30)
            e = jnp.exp(s - jnp.max(s, axis=-1, keepdims=True))
            p = (e * (1.0 / jnp.sum(e, axis=-1, keepdims=True))).astype(BF16)
            v = kv_s[keys, wide * h + NOPE : wide * h + wide]
            o = jnp.dot(p, v, preferred_element_type=F32)
            o_s[rows, VD * h : VD * h + VD] = o.astype(BF16)
        return carry

    def decode():
        query = jnp.dot(zd[:, :QL], wqb[...], preferred_element_type=F32)
        nope, rope = split_query(query, cosd, sind)
        latent, own_lat = zb[..., QL : QL + KL].reshape(512, KL), zd[:, QL : QL + KL]
        turn, own_turn = zb[..., QL + KL : W].reshape(512, 128).astype(F32), zd[:, QL + KL : W].astype(F32)
        turns = (turn.astype(BF16), pltpu.roll(turn, 64, 1).astype(BF16))
        own_turns = (own_turn.astype(BF16), pltpu.roll(own_turn, 64, 1).astype(BF16))
        at = lax.broadcasted_iota(jnp.int32, (16, 512), 1).astype(F32)
        keep = (at < end_col) & (at >= end_col - len_col)
        diag = i16 == j16
        for h in range(heads):
            up_k = wkvb[:, wide * h : wide * h + NOPE]
            q_abs = lax.dot_general(nope[h], up_k, NT, preferred_element_type=F32).astype(BF16)
            s = lax.dot_general(q_abs, latent, NT, preferred_element_type=F32)
            s = (s + lax.dot_general(rope[h // 2], turns[h % 2], NT, preferred_element_type=F32)) * scale
            s = jnp.where(keep, s, -1e30)
            t = lax.dot_general(q_abs, own_lat, NT, preferred_element_type=F32)
            t = (t + lax.dot_general(rope[h // 2], own_turns[h % 2], NT, preferred_element_type=F32)) * scale
            t = jnp.where(diag, t, -1e30)
            top = jnp.maximum(jnp.max(s, axis=-1, keepdims=True), jnp.max(t, axis=-1, keepdims=True))
            e, f = jnp.exp(s - top), jnp.exp(t - top)
            part = 1.0 / (jnp.sum(e, axis=-1, keepdims=True) + jnp.sum(f, axis=-1, keepdims=True))
            lat = jnp.dot((e * part).astype(BF16), latent, preferred_element_type=F32)
            lat = lat + jnp.dot((f * part).astype(BF16), own_lat, preferred_element_type=F32)
            up_v = wkvb[:, wide * h + NOPE : wide * h + wide]
            o = jnp.dot(lat.astype(BF16), up_v, preferred_element_type=F32)
            od_s[:, VD * h : VD * h + VD] = o.astype(BF16)

    def output(s):
        def part(k, carry):
            xx, yy = k // 2, 2 * lax.rem(k, 2)
            w = wot[pl.ds(pl.multiple_of(k * 896, 128), 896), :]
            val = lax.dot_general(w, o_s[256 * s : 256 * s + 256, :], NT, preferred_element_type=F32).astype(BF16)
            for j in range(4):
                t0[s, j % 2, xx, yy + j // 2] = val[224 * j : 224 * j + 112]
                t1[s, j % 2, yy + j // 2, xx] = val[224 * j + 112 : 224 * j + 224]
            return carry

        lax.fori_loop(0, 8, part, 0)

    half = (slice(0, 128), slice(128, 256))

    class Stage:
        def __init__(self, s):
            self.s = s
            self.core = ([], [])
            self.rings = (
                Ring(t0.at[s, c], tnear0.at[s], tfar0.at[s], half, x, xp, xm, us, ur, 24 * s),
                Ring(t1.at[s, c], tnear1.at[s], tfar1.at[s], half, y, yp, ym, us, ur, 24 * s + 6),
            )
            self.lasts = (
                Ring(tq0.at[s], tqnear0.at[s], tqfar0.at[s], half, y, yp, ym, us, ur, 24 * s + 12),
                Ring(tq1.at[s], tqnear1.at[s], tqfar1.at[s], half, x, xp, xm, us, ur, 24 * s + 18),
            )
            self.parts = ((t0, tc0, x, self.core[0]), (t1, tc1, y, self.core[1]))

        def swap(self):
            for i, d in enumerate(order):
                for n, (t, came, pos_t, list_t) in enumerate(self.parts):
                    k, m = next_of(pos_t, d), 8 * self.s + 2 * i + n
                    copy = remote(t.at[self.s, 1 - c, k], came.at[self.s, k], vs.at[m], vr.at[m], peer)
                    copy.start()
                    list_t.append(copy)

        def take(self, i):
            for t, came, pos_t, list_t in self.parts:
                list_t[i].wait_recv()
                k = next_of(pos_t, order[i])
                t[self.s, c, k] = (t[self.s, c, k].astype(F32) + came[self.s, k].astype(F32)).astype(BF16)

        def first(self):
            self.take(0)
            for ring in self.rings:
                ring.start_far()
            self.take(1)
            self.take(2)
            for ring in self.rings:
                ring.start_near()
            self.take(3)

        def pass_on(self):
            for ring in self.rings:
                ring.pass_on()

        def second(self):
            for side in range(2):
                tq0[self.s, :, :, half[side]] = self.rings[0].result(side).astype(BF16)
                tq1[self.s, :, :, half[side]] = self.rings[1].result(side).astype(BF16)
            for ring in self.lasts:
                ring.start_far()
                ring.start_near()

        def pass_last(self):
            for ring in self.lasts:
                ring.pass_on()

        def finish(self):
            for h, ring in enumerate(self.lasts):
                for side in range(2):
                    at = 256 * self.s + 128 * side
                    out_ref[112 * h : 112 * h + 112, at : at + 128] = ring.result(side).astype(BF16)

        def close(self):
            for copy in self.core[0] + self.core[1]:
                copy.wait_send()
            for ring in self.rings + self.lasts:
                ring.close()

    s0, s1 = Stage(0), Stage(1)
    lax.fori_loop(0, 2, project, 0)
    lax.fori_loop(0, 2, block, 0)
    output(0)
    s0.swap()
    s0.first()
    decode()
    s0.pass_on()
    lax.fori_loop(2, 4, project, 0)
    lax.fori_loop(2, 4, block, 0)
    s0.second()
    output(1)
    s1.swap()

    dd[...] = jnp.zeros_like(dd)

    def dec_part(k, carry):
        w = wo[:, pl.ds(pl.multiple_of(k * 896, 128), 896)]
        dd[:, :896] = jnp.dot(od_s[...], w, preferred_element_type=F32)
        for j in range(4):
            at = 224 * j // 128 * 128
            v = dd[:, at : at + 384]
            if 224 * j - at:
                v = pltpu.roll(v, 384 - (224 * j - at), 1)
            dt[j % 2, 2 * k + j // 2] = v[:, :256].astype(BF16)
        return carry

    s0.pass_last()
    s1.first()
    lax.fori_loop(0, 8, dec_part, 0)
    dec_swap = remote(dt.at[1 - c], dc, fs.at[0], fr.at[0], peer)
    dec_swap.start()
    s0.finish()
    dec_swap.wait()
    dt[c] = (dt[c].astype(F32) + dc[...].astype(F32)).astype(BF16)

    def send_out(step, carry):
        other, device = chip_peer(x, y, c, step)
        remote(dt.at[c, other], dn.at[chip], hs.at[step], hr.at[step], device).start()
        return carry

    lax.fori_loop(1, 16, send_out, 0)
    dn[chip] = dt[c, chip]
    s1.pass_on()

    def wait_out(step, carry):
        other, device = chip_peer(x, y, c, step)
        remote(dt.at[c, other], dn.at[chip], hs.at[step], hr.at[step], device).wait()
        return carry

    lax.fori_loop(1, 16, wait_out, 0)
    dz[z] = jnp.sum(dn[...].astype(F32), axis=0).astype(BF16)

    def send_back(step, carry):
        zz, _, device = z_peer(step)
        remote(dz.at[zz], dz.at[zz], ys.at[step], yr.at[step], device).start()
        return carry

    lax.fori_loop(1, 8, send_back, 0)
    s1.second()

    def wait_back(step, carry):
        zz, _, device = z_peer(step)
        remote(dz.at[zz], dz.at[zz], ys.at[step], yr.at[step], device).wait()
        return carry

    lax.fori_loop(1, 8, wait_back, 0)
    wanted = jnp.sum(jnp.where(jj == z * 16 + ii, docs, 0).astype(F32), axis=1, keepdims=True)
    sel_out = jnp.where(jj.astype(F32) == wanted, 1.0, 0.0).astype(BF16)
    picked = jnp.dot(sel_out, dz[...].reshape(128, 256), preferred_element_type=F32)
    outd_ref[...] = picked[:, :224].astype(BF16)

    s1.pass_last()
    s1.finish()
    for copy in copies + core0 + core1 + finals:
        copy.wait_send()
    for ring in (ring0, ring1):
        ring.close()
    s0.close()
    s1.close()


def whole(xt, xd, wq_a, wkv_a, q_gain, kv_gain, freq, doc_len, docs, wq_b, wkv_b, wo):
    vm = pl.BlockSpec(memory_space=pltpu.VMEM)
    hbm = pl.BlockSpec(memory_space=pl.ANY)
    dma = pltpu.SemaphoreType.DMA
    shapes = [
        (wq_b.shape, BF16), (wkv_b.shape, BF16), (wo.shape, BF16), (wo.shape[::-1], BF16),
        ((wq_a.shape[0], W - QL), BF16),
        ((2, 4, 4, 8, W), F32), ((2, 4, 4, 8, W), F32), ((4, 4, 8, W), F32), ((4, 4, 8, W), F32),
        ((2, 4, 8, W), F32), ((2, 4, 8, W), F32), ((4, 8, W), F32), ((4, 8, W), F32),
        ((4, 8, W), F32), ((4, 8, W), F32), ((3, 8, W), F32), ((3, 8, W), F32),
        ((8,) + xd.shape, BF16), ((2, 8, W), F32), ((8, W), F32),
        ((16, 8, 256), F32), ((16, 8, 256), F32), ((16, 8, 128), F32), ((2, 8, W), F32),
        ((NX, NY, 2, 16, W), BF16), ((16, W), BF16), ((512, 128), F32), ((512, 128), F32), ((512, 128), F32),
        ((512, wkv_b.shape[1]), BF16), ((512, 512), BF16), ((16, 512), BF16),
        ((2, 2, 4, 4, 112, 256), BF16), ((2, 2, 4, 4, 112, 256), BF16),
        ((2, 4, 4, 112, 256), BF16), ((2, 4, 4, 112, 256), BF16),
        ((2, 2, 4, 112, 256), BF16), ((2, 2, 4, 112, 256), BF16),
        ((2, 4, 112, 256), BF16), ((2, 4, 112, 256), BF16),
        ((2, 4, 112, 256), BF16), ((2, 4, 112, 256), BF16),
        ((2, 2, 112, 256), BF16), ((2, 2, 112, 256), BF16),
        ((2, 112, 256), BF16), ((2, 112, 256), BF16),
        ((16, 1024), F32), ((2, 16, 16, 256), BF16), ((16, 16, 256), BF16), ((16, 16, 256), BF16),
        ((8, 16, 256), BF16),
    ]
    counts = (3, 8, 8, 8, 8, 18, 18, 1, 1, 16, 16, 16, 16, 32, 32, 1, 1, 48, 48, 16, 16, 1, 1, 16, 16, 8, 8)
    return pl.pallas_call(
        whole_kernel,
        out_shape=(jax.ShapeDtypeStruct((224, 512), BF16), jax.ShapeDtypeStruct((16, 224), BF16)),
        in_specs=[vm] * 9 + [hbm] * 3,
        out_specs=(vm, vm),
        scratch_shapes=[pltpu.VMEM(shape, kind) for shape, kind in shapes] + [dma((n,)) for n in counts],
        compiler_params=pltpu.CompilerParams(
            collective_id=0, has_side_effects=True, vmem_limit_bytes=VMEM_LIMIT
        ),
        name="whole",
    )(xt, xd, wq_a, wkv_a, q_gain, kv_gain, freq, doc_len, docs, wq_b, wkv_b, wo)


def per_device(x_pre, x_dec, wq_a, wkv_a, q_gain, kv_gain, wq_b, wkv_b, wo, doc_len, request_docs):
    half = RD // 2
    freq = np.tile(10000.0 ** (-np.arange(half) / half), 4).astype(np.float32)[None, :]
    out_t, out_dec = whole(
        x_pre.T, x_dec, wq_a, wkv_a, q_gain, kv_gain, jnp.asarray(freq), doc_len, request_docs, wq_b, wkv_b, wo
    )
    return out_t.T, out_dec


def solution(mesh):
    placed = (
        P(("role", "grp"), "tp"),
        P(("role", "grp"), "tp"),
        P("tp", None),
        P("tp", None),
        P(),
        P(),
        P(None, "tp"),
        P(None, "tp"),
        P("tp", None),
        P(),
        P(),
    )
    return jax.shard_map(
        per_device,
        mesh=mesh,
        in_specs=placed,
        out_specs=(P(("role", "grp"), "tp"), P(("role", "grp"), "tp")),
        check_vma=False,
    )
```

```python
import jax
import jax.numpy as jnp
import numpy as np
from jax import lax
from jax.experimental import pallas as pl
from jax.experimental.pallas import tpu as pltpu
from jax.sharding import PartitionSpec as P

QL = 1536
KL = 512
RD = 64
NOPE = 128
VD = 128
NX = 4
NY = 4
W = QL + KL + 128
SPLIT = 1152
EPS = 1e-06
F32 = jnp.float32
BF16 = jnp.bfloat16
MESH = pl.DeviceIdType.MESH
VMEM_LIMIT = 58 * 2**20


def place():
    tp = lax.axis_index("tp")
    return tp, tp // 8, lax.rem(tp // 2, NY), lax.rem(tp, 2)


def tp_of(x, y, c):
    return x * 8 + y * 2 + c


def next_of(p, step):
    return lax.rem(p + step + 4, 4)


def z_peer(step):
    z = lax.axis_index("role") * 2 + lax.axis_index("grp")
    other = lax.rem(z + step, 8)
    return z, other, {"role": other // 2, "grp": lax.rem(other, 2)}


def remote(src, dst, send, recv, device):
    return pltpu.make_async_remote_copy(
        src_ref=src, dst_ref=dst, send_sem=send, recv_sem=recv, device_id=device, device_id_type=MESH
    )


def chip_peer(x, y, c, step):
    other = lax.rem(x * 4 + y + step, 16)
    return other, {"tp": tp_of(other // 4, lax.rem(other, 4), c)}


def greet_start(x, y, c):
    barrier = pltpu.get_barrier_semaphore()
    pl.semaphore_signal(barrier, inc=1, device_id={"tp": tp_of(x, y, 1 - c)}, device_id_type=MESH)

    def chips(step, carry):
        _, device = chip_peer(x, y, c, step)
        pl.semaphore_signal(barrier, inc=1, device_id=device, device_id_type=MESH)
        return carry

    lax.fori_loop(1, 16, chips, 0)

    def planes(step, carry):
        _, _, device = z_peer(step)
        pl.semaphore_signal(barrier, inc=1, device_id=device, device_id_type=MESH)
        return carry

    lax.fori_loop(1, 8, planes, 0)


def greet_wait():
    pl.semaphore_wait(pltpu.get_barrier_semaphore(), 1 + 15 + 7)


class Ring:
    def __init__(self, data, near, far, part, pos, plus, minus, send, recv, base):
        self.data, self.near, self.far, self.part = data, near, far, part
        self.pos, self.plus, self.minus = pos, plus, minus
        self.send, self.recv, self.base = send, recv, base
        self.copies = {}

    def cut(self, ref, side):
        return ref.at[(Ellipsis, self.part[side])]

    def go(self, key, number, src, dst, device):
        copy = remote(src, dst, self.send.at[self.base + number], self.recv.at[self.base + number], device)
        copy.start()
        self.copies[key] = copy

    def start_far(self):
        chunk = self.data.at[next_of(self.pos, 2)]
        self.go("far0", 0, self.cut(chunk, 0), self.cut(self.far, 0), self.plus)
        self.go("far1", 1, self.cut(chunk, 1), self.cut(self.far, 1), self.minus)

    def start_near(self):
        up, down = self.data.at[next_of(self.pos, 1)], self.data.at[next_of(self.pos, -1)]
        self.go("up1", 2, self.cut(up, 1), self.cut(self.near.at[0], 1), self.plus)
        self.go("down0", 3, self.cut(down, 0), self.cut(self.near.at[1], 0), self.minus)

    def add(self, chunk, side):
        ref, extra = self.cut(chunk, side), self.cut(self.far, side)
        ref[...] = (ref[...].astype(F32) + extra[...].astype(F32)).astype(ref.dtype)

    def pass_on(self):
        up, down = self.data.at[next_of(self.pos, 1)], self.data.at[next_of(self.pos, -1)]
        self.copies["far0"].wait_recv()
        self.add(up, 0)
        self.go("up0", 4, self.cut(up, 0), self.cut(self.near.at[0], 0), self.plus)
        self.copies["far1"].wait_recv()
        self.add(down, 1)
        self.go("down1", 5, self.cut(down, 1), self.cut(self.near.at[1], 1), self.minus)

    def result(self, side):
        for key in ("up%d" % side, "down%d" % side):
            self.copies[key].wait_recv()
        own = self.cut(self.data.at[self.pos], side)[...].astype(F32)
        left = self.cut(self.near.at[0], side)[...].astype(F32)
        right = self.cut(self.near.at[1], side)[...].astype(F32)
        return own + (left + right)

    def close(self):
        for copy in self.copies.values():
            copy.wait_send()


def latent_rows(rows, q_gain, kv_gain, cosine, sine):
    q = rows[:, :QL]
    kv = rows[:, QL : QL + KL]
    turn = rows[:, QL + KL :]
    q = q * lax.rsqrt(jnp.mean(q * q, axis=-1, keepdims=True) + EPS) * q_gain
    kv = kv * lax.rsqrt(jnp.mean(kv * kv, axis=-1, keepdims=True) + EPS) * kv_gain
    turn = rope_tile(turn, cosine, sine)
    lane = lax.broadcasted_iota(jnp.int32, turn.shape, 1)
    turn = jnp.where(lane < RD, turn, 0.0)
    return q, kv, turn


def rope_tile(tile, cosine, sine):
    lane = lax.broadcasted_iota(jnp.int32, tile.shape, 1)
    swapped = jnp.where(lane % RD < RD // 2, pltpu.roll(tile, 96, 1), pltpu.roll(tile, 32, 1))
    return tile * cosine + swapped * sine


def turn_tables(pos, freq):
    turn = pos * freq
    lane = lax.broadcasted_iota(jnp.int32, turn.shape, 1)
    sine = jnp.sin(turn)
    return jnp.cos(turn), jnp.where(lane % RD < RD // 2, -sine, sine)


NT = (((1,), (1,)), ((), ()))
TN = (((0,), (0,)), ((), ()))


def split_query(query, cosine, sine):
    nope, rope = [], []
    lane = lax.broadcasted_iota(jnp.int32, (query.shape[0], 128), 1)
    for pair in range(query.shape[1] // 384):
        t0, t1, t2 = [query[:, 384 * pair + 128 * i : 384 * pair + 128 * i + 128] for i in range(3)]
        nope.append(t0.astype(BF16))
        nope.append(jnp.where(lane < 64, pltpu.roll(t1, 64, 1), pltpu.roll(t2, 64, 1)).astype(BF16))
        rope.append(rope_tile(jnp.where(lane < 64, t1, t2), cosine, sine).astype(BF16))
    return nope, rope


def whole_kernel(
    xt_ref, xd_ref, wqa_ref, wkva_ref, qg_ref, kvg_ref, freq_ref, len_ref, docs_ref, wqb_hbm, wkvb_hbm, wo_hbm,
    out_ref, outd_ref,
    wqb, wkvb, wo, wot, wkv_s, p0, p1, c0, c1, near0, near1, far0, far1, q0, q1, in0, in1,
    xd_all, dec, dec_in, tiles, tiles_in, sums_in, rows_in,
    zb, zd, qabs_s, qrope_s, pos_s, cos_s, sin_s, kv_s, o_s, od_s,
    t0, t1, tc0, tc1, tnear0, tnear1, tfar0, tfar1, tq0, tq1, tqin0, tqin1,
    dd, dt, dc, dn, dz,
    ws, zs, zr, cs, cr, rs, rr, ds, dr, es, er, gs, gr, ks, kr, ms, mr,
    us, ur, vs, vr, fs, fr, hs, hr, ys, yr,
):
    tp, x, y, c = place()
    chip = x * 4 + y
    z, _, _ = z_peer(0)
    peer = {"tp": tp_of(x, y, 1 - c)}
    xp, xm = {"tp": tp_of(next_of(x, 1), y, c)}, {"tp": tp_of(next_of(x, -1), y, c)}
    yp, ym = {"tp": tp_of(x, next_of(y, 1), c)}, {"tp": tp_of(x, next_of(y, -1), c)}
    greet_start(x, y, c)
    loads = [
        pltpu.make_async_copy(src, dst, ws.at[i])
        for i, (src, dst) in enumerate(((wo_hbm, wo), (wkvb_hbm, wkvb), (wqb_hbm, wqb)))
    ]
    for load in loads:
        load.start()

    wkv_s[...] = jnp.zeros_like(wkv_s)
    wkv_s[:, : KL + RD] = wkva_ref[...]
    order = (2, 1, 3, 0)
    core0, core1 = [], []

    def swap_rows(i, p, came, pos_p, copies_p):
        k, n = next_of(pos_p, order[i]), i if p is p0 else 4 + i
        copy = remote(p.at[1 - c, k], came.at[k], cs.at[n], cr.at[n], peer)
        copy.start()
        copies_p.append(copy)

    for i, d in enumerate(order):
        xx = next_of(x, d)
        rows = xt_ref[:, pl.ds(pl.multiple_of(xx * 128, 128), 128)]
        for w_ref, lo, wide in ((wqa_ref, 0, QL), (wkv_s, QL, W - QL)):
            val = lax.dot_general(rows, w_ref[...], TN, preferred_element_type=F32)
            val = val.reshape(NY, 2, 2, 8, wide)
            for cc in range(2):
                p0[cc, xx, :, :, lo : lo + wide] = val[:, cc, 0]
                for yy in range(NY):
                    p1[cc, yy, xx, :, lo : lo + wide] = val[yy, cc, 1]
        if i == 0:
            greet_wait()
            xd_all[z] = xd_ref[...]

            def send_z(step, carry):
                zz, _, device = z_peer(step)
                remote(xd_ref, xd_all.at[zz], zs.at[step], zr.at[step], device).start()
                return carry

            lax.fori_loop(1, 8, send_z, 0)
            swap_rows(0, p0, c0, x, core0)
    for i in range(4):
        if i:
            swap_rows(i, p0, c0, x, core0)
        swap_rows(i, p1, c1, y, core1)

    own0, own1 = p0.at[c], p1.at[c]
    lanes = (slice(0, SPLIT), slice(SPLIT, W))
    ring0 = Ring(own0, near0, far0, lanes, x, xp, xm, rs, rr, 0)
    ring1 = Ring(own1, near1, far1, lanes, y, yp, ym, rs, rr, 6)
    both = ((ring0, own0, c0, core0, x), (ring1, own1, c1, core1, y))

    def take_core(i, only=None):
        for n, (ring, own, came, copies, pos) in enumerate(both):
            if only in (None, n):
                copies[i].wait_recv()
                k = next_of(pos, order[i])
                own[k] = own[k] + came[k]

    take_core(0, 0)
    ring0.start_far()
    take_core(0, 1)
    ring1.start_far()
    take_core(1)
    take_core(2)
    ring0.start_near()
    ring1.start_near()
    take_core(3)

    def wait_z(step, carry):
        zz, other, device = z_peer(step)
        remote(xd_ref, xd_all.at[zz], zs.at[step], zr.at[step], device).wait()
        return carry

    lax.fori_loop(1, 8, wait_z, 0)
    ii = lax.broadcasted_iota(jnp.int32, (16, 128), 0)
    jj = lax.broadcasted_iota(jnp.int32, (16, 128), 1)
    docs = docs_ref[...].reshape(1, 128)
    sel_in = jnp.where(docs == z * 16 + ii, 1.0, 0.0).astype(BF16)
    asked = jnp.dot(sel_in, xd_all[...].reshape(128, -1), preferred_element_type=F32).astype(BF16)
    for w_ref, lo, wide in ((wqa_ref, 0, QL), (wkv_s, QL, W - QL)):
        val = jnp.dot(asked, w_ref[...], preferred_element_type=F32)
        dec[:, :, lo : lo + wide] = val.reshape(2, 8, wide)
    dec_core = remote(dec.at[1 - c], dec_in, ds.at[0], dr.at[0], peer)
    dec_core.start()

    lens = len_ref[pl.ds(z, 1), :].astype(F32)
    i16 = lax.broadcasted_iota(jnp.int32, (16, 16), 0)
    j16 = lax.broadcasted_iota(jnp.int32, (16, 16), 1)
    spread = jnp.broadcast_to(lens, (16, 16))
    len_col = jnp.sum(jnp.where(i16 == j16, spread, 0.0), axis=1, keepdims=True)
    end_col = jnp.sum(jnp.where(j16 <= i16, spread, 0.0), axis=1, keepdims=True)
    end_row = jnp.sum(jnp.where(i16 <= j16, jnp.broadcast_to(len_col, (16, 16)), 0.0), axis=0, keepdims=True)
    token = lax.broadcasted_iota(jnp.int32, (512, 16), 0).astype(F32)
    begun = jnp.sum(jnp.where(token >= end_row, jnp.broadcast_to(lens, (512, 16)), 0.0), axis=1, keepdims=True)
    pos = lax.broadcasted_iota(jnp.int32, (512, 128), 0).astype(F32) - begun
    pos_s[...] = pos
    freq = freq_ref[...]
    for i in range(4):
        part = pl.ds(128 * i, 128)
        cos_s[part, :], sin_s[part, :] = turn_tables(pos_s[part, :], freq)
    cosd, sind = turn_tables(jnp.broadcast_to(len_col, (16, 128)), freq)

    ring0.pass_on()
    ring1.pass_on()

    dec_core.wait()
    mine = dec[c] + dec_in[...]
    for j in range(16):
        tiles[j, :, 0:128] = mine[:, 128 * j : 128 * j + 128]
        tiles[j, :, 128:256] = mine[:, QL + KL :]

    def send_tile(step, carry):
        other, device = chip_peer(x, y, c, step)
        remote(tiles.at[other], tiles_in.at[chip], es.at[step], er.at[step], device).start()
        return carry

    lax.fori_loop(1, 16, send_tile, 0)
    tiles_in[chip] = tiles[chip]

    loads[0].wait()

    def turn_wo(k, carry):
        cut = pl.multiple_of(k * 896, 128)
        wot[pl.ds(cut, 896), :] = wo[:, pl.ds(cut, 896)].T
        return carry

    lax.fori_loop(0, 3, turn_wo, 0)

    for side in range(2):
        q0[:, :, lanes[side]] = ring0.result(side)
        q1[:, :, lanes[side]] = ring1.result(side)
    finals = []
    for h, (q, box, pos_h, dev) in enumerate(
        ((q0, in0, y, lambda d: tp_of(x, next_of(y, d), c)), (q1, in1, x, lambda d: tp_of(next_of(x, d), y, c)))
    ):
        for d in (2, 1, 3):
            n = 12 + 3 * h + d - 1
            copy = remote(q.at[next_of(pos_h, d)], box.at[d - 1], rs.at[n], rr.at[n], {"tp": dev(d)})
            copy.start()
            finals.append(copy)

    def wait_tile(step, carry):
        other, device = chip_peer(x, y, c, step)
        remote(tiles.at[other], tiles_in.at[chip], es.at[step], er.at[step], device).wait()
        return carry

    lax.fori_loop(1, 16, wait_tile, 0)
    total = jnp.sum(tiles_in[...], axis=0)
    sums_in[chip] = total[:, :128]

    def send_sum(step, carry):
        other, device = chip_peer(x, y, c, step)
        remote(sums_in.at[chip], sums_in.at[chip], gs.at[step], gr.at[step], device).start()
        return carry

    lax.fori_loop(1, 16, send_sum, 0)

    for copy in finals:
        copy.wait_recv()
    rows = jnp.concatenate(
        [q0[y] + (in0[0] + in0[1]) + in0[2], q1[x] + (in1[0] + in1[1]) + in1[2]], axis=0
    )
    own_rows = pl.ds(pl.multiple_of(tp * 16, 16), 16)
    q_gain, kv_gain = qg_ref[...].reshape(1, QL), kvg_ref[...].reshape(1, KL)
    q, kv, turn = latent_rows(rows, q_gain, kv_gain, cos_s[own_rows, :], sin_s[own_rows, :])
    zb[x, y, c, :, 0:QL] = q.astype(BF16)
    zb[x, y, c, :, QL : QL + KL] = kv.astype(BF16)
    zb[x, y, c, :, QL + KL : W] = turn.astype(BF16)

    copies = []
    ka, kb = slice(0, SPLIT), slice(SPLIT, W)
    every = slice(None)

    def push(block, device):
        n = len(copies)
        copy = remote(block, block, ks.at[n], kr.at[n], device)
        copy.start()
        copies.append(copy)
        return copy

    def along_x(d):
        return {"tp": tp_of(next_of(x, d), y, c)}

    def along_y(d):
        return {"tp": tp_of(x, next_of(y, d), c)}

    from_x, from_y, rest_x, rest_y = {}, {}, {}, {}
    for d in (1, 3, 2):
        from_x[d] = push(zb.at[x, y, c, :, ka], along_x(d))
        from_y[d] = push(zb.at[x, y, c, :, kb], along_y(d))
    for d in (1, 3, 2):
        rest_x[d] = push(zb.at[x, y, c, :, kb], along_x(d))
        rest_y[d] = push(zb.at[x, y, c, :, ka], along_y(d))
    diag_a, diag_b = [], []
    for d in (1, 3, 2):
        xn, yn = next_of(x, -d), next_of(y, -d)
        from_x[d].wait_recv()
        diag_a += [(e, push(zb.at[xn, y, c, :, ka], along_y(e))) for e in (1, 3, 2)]
        from_y[d].wait_recv()
        diag_b += [(e, push(zb.at[x, yn, c, :, kb], along_x(e))) for e in (1, 3, 2)]
    mates = [push(zb.at[:, y, c, :, ka], peer), push(zb.at[x, :, c, :, kb], peer)]

    def wait_sum(step, carry):
        other, device = chip_peer(x, y, c, step)
        remote(sums_in.at[chip], sums_in.at[chip], gs.at[step], gr.at[step], device).wait()
        return carry

    lax.fori_loop(1, 16, wait_sum, 0)
    for j in range(16):
        rows_in[c, :, 128 * j : 128 * j + 128] = sums_in[j]
    rows_in[c, :, QL + KL : W] = total[:, 128:]
    dec_mate = remote(rows_in.at[c], rows_in.at[c], ms.at[0], mr.at[0], peer)
    dec_mate.start()
    lax.fori_loop(3, 6, turn_wo, 0)
    dec_mate.wait()
    q, kv, turn = latent_rows(rows_in[...].reshape(16, W), q_gain, kv_gain, cosd, sind)
    zd[:, 0:QL] = q.astype(BF16)
    zd[:, QL : QL + KL] = kv.astype(BF16)
    zd[:, QL + KL : W] = turn.astype(BF16)
    heads = 4
    scale = 1.0 / float(NOPE + RD) ** 0.5
    wide = NOPE + VD
    for load in loads[1:]:
        load.wait()
    query = jnp.dot(zd[:, :QL], wqb[...], preferred_element_type=F32)
    dec_nope, dec_rope = split_query(query, cosd, sind)
    for h in range(heads):
        up_k = wkvb[:, wide * h : wide * h + NOPE]
        qabs_s[h] = lax.dot_general(dec_nope[h], up_k, NT, preferred_element_type=F32).astype(BF16)
        qrope_s[h // 2] = dec_rope[h // 2]
    lax.fori_loop(6, 8, turn_wo, 0)
    for e in (1, 3, 2):
        for number, copy in diag_a:
            if number == e:
                copy.wait_recv()
        rest_y[e].wait_recv()
        mates.append(push(zb.at[:, next_of(y, -e), c, :, ka], peer))
        for number, copy in diag_b:
            if number == e:
                copy.wait_recv()
        rest_x[e].wait_recv()
        mates.append(push(zb.at[next_of(x, -e), :, c, :, kb], peer))
    for copy in mates:
        copy.wait_recv()

    def project(i, carry):
        kv = jnp.dot(zb[i, :, :, :, QL : QL + KL].reshape(128, KL), wkvb[...], preferred_element_type=F32)
        kv_s[pl.ds(pl.multiple_of(i * 128, 128), 128), :] = kv.astype(BF16)
        return carry

    def block(i, carry):
        first = pl.multiple_of(i * 128, 128)
        before = jnp.maximum(i - 1, 0)
        begin = pl.multiple_of(before * 128, 128)
        rows, keys = pl.ds(first, 128), pl.ds(begin, 256)
        query = jnp.dot(zb[i, :, :, :, :QL].reshape(128, QL), wqb[...], preferred_element_type=F32)
        nope, rope = split_query(query, cos_s[rows, :], sin_s[rows, :])
        turn = zb[pl.ds(before, 2), :, :, :, QL + KL : W].reshape(256, 128).astype(F32)
        turns = (turn.astype(BF16), pltpu.roll(turn, 64, 1).astype(BF16))
        own = first + lax.broadcasted_iota(jnp.int32, (128, 256), 0)
        other = begin + lax.broadcasted_iota(jnp.int32, (128, 256), 1)
        back = (own - other).astype(F32)
        keep = (back >= 0) & (back <= jnp.concatenate([pos_s[rows, :]] * 2, axis=1))
        for h in range(heads):
            q = jnp.concatenate([nope[h], rope[h // 2]], axis=1)
            k = jnp.concatenate([kv_s[keys, wide * h : wide * h + NOPE], turns[h % 2]], axis=1)
            s = lax.dot_general(q, k, NT, preferred_element_type=F32) * scale
            s = jnp.where(keep, s, -1e30)
            e = jnp.exp(s - jnp.max(s, axis=-1, keepdims=True))
            p = (e * (1.0 / jnp.sum(e, axis=-1, keepdims=True))).astype(BF16)
            v = kv_s[keys, wide * h + NOPE : wide * h + wide]
            o = jnp.dot(p, v, preferred_element_type=F32)
            o_s[rows, VD * h : VD * h + VD] = o.astype(BF16)
        return carry

    def decode():
        latent, own_lat = zb[..., QL : QL + KL].reshape(512, KL), zd[:, QL : QL + KL]
        turn, own_turn = zb[..., QL + KL : W].reshape(512, 128).astype(F32), zd[:, QL + KL : W].astype(F32)
        turns = (turn.astype(BF16), pltpu.roll(turn, 64, 1).astype(BF16))
        own_turns = (own_turn.astype(BF16), pltpu.roll(own_turn, 64, 1).astype(BF16))
        at = lax.broadcasted_iota(jnp.int32, (16, 512), 1).astype(F32)
        keep = (at < end_col) & (at >= end_col - len_col)
        diag = i16 == j16
        for h in range(heads):
            q_abs, q_rope = qabs_s[h], qrope_s[h // 2]
            s = lax.dot_general(q_abs, latent, NT, preferred_element_type=F32)
            s = (s + lax.dot_general(q_rope, turns[h % 2], NT, preferred_element_type=F32)) * scale
            s = jnp.where(keep, s, -1e30)
            t = lax.dot_general(q_abs, own_lat, NT, preferred_element_type=F32)
            t = (t + lax.dot_general(q_rope, own_turns[h % 2], NT, preferred_element_type=F32)) * scale
            t = jnp.where(diag, t, -1e30)
            top = jnp.maximum(jnp.max(s, axis=-1, keepdims=True), jnp.max(t, axis=-1, keepdims=True))
            e, f = jnp.exp(s - top), jnp.exp(t - top)
            part = 1.0 / (jnp.sum(e, axis=-1, keepdims=True) + jnp.sum(f, axis=-1, keepdims=True))
            lat = jnp.dot((e * part).astype(BF16), latent, preferred_element_type=F32)
            lat = lat + jnp.dot((f * part).astype(BF16), own_lat, preferred_element_type=F32)
            up_v = wkvb[:, wide * h + NOPE : wide * h + wide]
            o = jnp.dot(lat.astype(BF16), up_v, preferred_element_type=F32)
            od_s[:, VD * h : VD * h + VD] = o.astype(BF16)

    def output(s):
        far_x, far_y = next_of(x, 2), next_of(y, 2) // 2

        def part(n, carry):
            k = jnp.where(
                n < 2,
                2 * far_x + n,
                jnp.where(n < 5, 2 * next_of(far_x, n - 1) + far_y, 2 * next_of(far_x, n - 4) + 1 - far_y),
            )
            xx, yy = k // 2, 2 * lax.rem(k, 2)
            w = wot[pl.ds(pl.multiple_of(k * 896, 128), 896), :]
            val = lax.dot_general(w, o_s[256 * s : 256 * s + 256, :], NT, preferred_element_type=F32).astype(BF16)
            for j in range(4):
                t0[s, j % 2, xx, yy + j // 2] = val[224 * j : 224 * j + 112]
                t1[s, j % 2, yy + j // 2, xx] = val[224 * j + 112 : 224 * j + 224]
            return carry

        return part

    half = (slice(0, 128), slice(128, 256))

    class Stage:
        def __init__(self, s):
            self.s = s
            self.core = ([], [])
            self.rings = (
                Ring(t0.at[s, c], tnear0.at[s], tfar0.at[s], half, x, xp, xm, us, ur, 18 * s),
                Ring(t1.at[s, c], tnear1.at[s], tfar1.at[s], half, y, yp, ym, us, ur, 18 * s + 6),
            )
            self.lasts = [
                (tq0, tqin0, y, lambda d: tp_of(x, next_of(y, d), c)),
                (tq1, tqin1, x, lambda d: tp_of(next_of(x, d), y, c)),
            ]
            self.direct = ([], [])
            self.parts = ((t0, tc0, x, self.core[0]), (t1, tc1, y, self.core[1]))

        def swap(self, which):
            for i in which:
                d = order[i]
                for n, (t, came, pos_t, list_t) in enumerate(self.parts):
                    k, m = next_of(pos_t, d), 8 * self.s + 2 * i + n
                    copy = remote(t.at[self.s, 1 - c, k], came.at[self.s, k], vs.at[m], vr.at[m], peer)
                    copy.start()
                    list_t.append(copy)

        def take(self, i):
            for t, came, pos_t, list_t in self.parts:
                list_t[i].wait_recv()
                k = next_of(pos_t, order[i])
                t[self.s, c, k] = (t[self.s, c, k].astype(F32) + came[self.s, k].astype(F32)).astype(BF16)

        def first(self):
            self.take(0)
            for ring in self.rings:
                ring.start_far()
            self.take(1)
            self.take(2)
            for ring in self.rings:
                ring.start_near()
            self.take(3)

        def pass_on(self):
            for ring in self.rings:
                ring.pass_on()

        def second(self):
            for side in range(2):
                tq0[self.s, :, :, half[side]] = self.rings[0].result(side).astype(BF16)
                tq1[self.s, :, :, half[side]] = self.rings[1].result(side).astype(BF16)
            for d in (2, 1, 3):
                for h, (data, box, pos_q, dev) in enumerate(self.lasts):
                    n = 18 * self.s + 12 + 3 * h + d - 1
                    copy = remote(
                        data.at[self.s, next_of(pos_q, d)], box.at[self.s, d - 1], us.at[n], ur.at[n], {"tp": dev(d)}
                    )
                    copy.start()
                    self.direct[h].append(copy)

        def finish(self):
            for h, (data, box, pos_q, dev) in enumerate(self.lasts):
                for copy in self.direct[h]:
                    copy.wait_recv()
                came = [box[self.s, i].astype(F32) for i in range(3)]
                total = data[self.s, pos_q].astype(F32) + (came[0] + came[1]) + came[2]
                out_ref[112 * h : 112 * h + 112, 256 * self.s : 256 * self.s + 256] = total.astype(BF16)

        def close(self):
            for copy in self.core[0] + self.core[1]:
                copy.wait_send()
            for ring in self.rings:
                ring.close()
            for copy in self.direct[0] + self.direct[1]:
                copy.wait_send()

    s0, s1 = Stage(0), Stage(1)

    def produce(stage):
        part = output(stage.s)
        lax.fori_loop(0, 5, part, 0)
        stage.swap((0,))
        lax.fori_loop(5, 8, part, 0)
        stage.swap((1, 2, 3))

    lax.fori_loop(0, 2, project, 0)
    lax.fori_loop(0, 2, block, 0)
    produce(s0)
    s0.first()
    lax.fori_loop(2, 4, project, 0)
    lax.fori_loop(2, 4, block, 0)
    s0.pass_on()
    produce(s1)
    s1.first()
    s0.second()
    decode()

    dd[...] = jnp.zeros_like(dd)

    def dec_part(k, carry):
        w = wo[:, pl.ds(pl.multiple_of(k * 896, 128), 896)]
        dd[:, :896] = jnp.dot(od_s[...], w, preferred_element_type=F32)
        for j in range(4):
            at = 224 * j // 128 * 128
            v = dd[:, at : at + 384]
            if 224 * j - at:
                v = pltpu.roll(v, 384 - (224 * j - at), 1)
            dt[j % 2, 2 * k + j // 2] = v[:, :256].astype(BF16)
        return carry

    lax.fori_loop(0, 8, dec_part, 0)
    dec_swap = remote(dt.at[1 - c], dc, fs.at[0], fr.at[0], peer)
    dec_swap.start()
    s1.pass_on()
    s0.finish()
    dec_swap.wait()
    dt[c] = (dt[c].astype(F32) + dc[...].astype(F32)).astype(BF16)

    def send_out(step, carry):
        other, device = chip_peer(x, y, c, step)
        remote(dt.at[c, other], dn.at[chip], hs.at[step], hr.at[step], device).start()
        return carry

    lax.fori_loop(1, 16, send_out, 0)
    dn[chip] = dt[c, chip]

    def wait_out(step, carry):
        other, device = chip_peer(x, y, c, step)
        remote(dt.at[c, other], dn.at[chip], hs.at[step], hr.at[step], device).wait()
        return carry

    lax.fori_loop(1, 16, wait_out, 0)
    dz[z] = jnp.sum(dn[...].astype(F32), axis=0).astype(BF16)

    def send_back(step, carry):
        zz, _, device = z_peer(step)
        remote(dz.at[zz], dz.at[zz], ys.at[step], yr.at[step], device).start()
        return carry

    lax.fori_loop(1, 8, send_back, 0)
    s1.second()

    def wait_back(step, carry):
        zz, _, device = z_peer(step)
        remote(dz.at[zz], dz.at[zz], ys.at[step], yr.at[step], device).wait()
        return carry

    lax.fori_loop(1, 8, wait_back, 0)
    wanted = jnp.sum(jnp.where(jj == z * 16 + ii, docs, 0).astype(F32), axis=1, keepdims=True)
    sel_out = jnp.where(jj.astype(F32) == wanted, 1.0, 0.0).astype(BF16)
    picked = jnp.dot(sel_out, dz[...].reshape(128, 256), preferred_element_type=F32)
    outd_ref[...] = picked[:, :224].astype(BF16)

    s1.finish()
    for copy in copies + core0 + core1 + finals:
        copy.wait_send()
    for ring in (ring0, ring1):
        ring.close()
    s0.close()
    s1.close()


def whole(xt, xd, wq_a, wkv_a, q_gain, kv_gain, freq, doc_len, docs, wq_b, wkv_b, wo):
    vm = pl.BlockSpec(memory_space=pltpu.VMEM)
    hbm = pl.BlockSpec(memory_space=pl.ANY)
    dma = pltpu.SemaphoreType.DMA
    shapes = [
        (wq_b.shape, BF16), (wkv_b.shape, BF16), (wo.shape, BF16), (wo.shape[::-1], BF16),
        ((wq_a.shape[0], W - QL), BF16),
        ((2, 4, 4, 8, W), F32), ((2, 4, 4, 8, W), F32), ((4, 4, 8, W), F32), ((4, 4, 8, W), F32),
        ((2, 4, 8, W), F32), ((2, 4, 8, W), F32), ((4, 8, W), F32), ((4, 8, W), F32),
        ((4, 8, W), F32), ((4, 8, W), F32), ((3, 8, W), F32), ((3, 8, W), F32),
        ((8,) + xd.shape, BF16), ((2, 8, W), F32), ((8, W), F32),
        ((16, 8, 256), F32), ((16, 8, 256), F32), ((16, 8, 128), F32), ((2, 8, W), F32),
        ((NX, NY, 2, 16, W), BF16), ((16, W), BF16), ((4, 16, KL), BF16), ((2, 16, 128), BF16), ((512, 128), F32), ((512, 128), F32), ((512, 128), F32),
        ((512, wkv_b.shape[1]), BF16), ((512, 512), BF16), ((16, 512), BF16),
        ((2, 2, 4, 4, 112, 256), BF16), ((2, 2, 4, 4, 112, 256), BF16),
        ((2, 4, 4, 112, 256), BF16), ((2, 4, 4, 112, 256), BF16),
        ((2, 2, 4, 112, 256), BF16), ((2, 2, 4, 112, 256), BF16),
        ((2, 4, 112, 256), BF16), ((2, 4, 112, 256), BF16),
        ((2, 4, 112, 256), BF16), ((2, 4, 112, 256), BF16),
        ((2, 3, 112, 256), BF16), ((2, 3, 112, 256), BF16),
        ((16, 1024), F32), ((2, 16, 16, 256), BF16), ((16, 16, 256), BF16), ((16, 16, 256), BF16),
        ((8, 16, 256), BF16),
    ]
    counts = (3, 8, 8, 8, 8, 18, 18, 1, 1, 16, 16, 16, 16, 38, 38, 1, 1, 36, 36, 16, 16, 1, 1, 16, 16, 8, 8)
    return pl.pallas_call(
        whole_kernel,
        out_shape=(jax.ShapeDtypeStruct((224, 512), BF16), jax.ShapeDtypeStruct((16, 224), BF16)),
        in_specs=[vm] * 9 + [hbm] * 3,
        out_specs=(vm, vm),
        scratch_shapes=[pltpu.VMEM(shape, kind) for shape, kind in shapes] + [dma((n,)) for n in counts],
        compiler_params=pltpu.CompilerParams(
            collective_id=0, has_side_effects=True, vmem_limit_bytes=VMEM_LIMIT
        ),
        name="whole",
    )(xt, xd, wq_a, wkv_a, q_gain, kv_gain, freq, doc_len, docs, wq_b, wkv_b, wo)


def hand_over_kernel(a_ref, b_ref, out_ref, outd_ref):
    out_ref[...] = a_ref[...]
    outd_ref[...] = b_ref[...]


def hand_over(a, b):
    vm = pl.BlockSpec(memory_space=pltpu.VMEM)
    return pl.pallas_call(
        hand_over_kernel,
        out_shape=(jax.ShapeDtypeStruct(a.shape, a.dtype), jax.ShapeDtypeStruct(b.shape, b.dtype)),
        in_specs=[vm, vm],
        out_specs=(vm, vm),
        name="hand_over",
    )(a, b)


def per_device(x_pre, x_dec, wq_a, wkv_a, q_gain, kv_gain, wq_b, wkv_b, wo, doc_len, request_docs):
    half = RD // 2
    freq = np.tile(10000.0 ** (-np.arange(half) / half), 4).astype(np.float32)[None, :]
    out_t, out_dec = whole(
        x_pre.T, x_dec, wq_a, wkv_a, q_gain, kv_gain, jnp.asarray(freq), doc_len, request_docs, wq_b, wkv_b, wo
    )
    out_t, out_dec = hand_over(out_t, out_dec)
    return out_t.T, out_dec


def solution(mesh):
    placed = (
        P(("role", "grp"), "tp"),
        P(("role", "grp"), "tp"),
        P("tp", None),
        P("tp", None),
        P(),
        P(),
        P(None, "tp"),
        P(None, "tp"),
        P("tp", None),
        P(),
        P(),
    )
    return jax.shard_map(
        per_device,
        mesh=mesh,
        in_specs=placed,
        out_specs=(P(("role", "grp"), "tp"), P(("role", "grp"), "tp")),
        check_vma=False,
    )
```

```python
import jax
import jax.numpy as jnp
import numpy as np
from jax import lax
from jax.experimental import pallas as pl
from jax.experimental.pallas import tpu as pltpu
from jax.sharding import PartitionSpec as P

QL = 1536
KL = 512
RD = 64
NOPE = 128
VD = 128
NX = 4
NY = 4
W = QL + KL + 128
HALF = 1152
SPLIT = 640
EPS = 1e-06
F32 = jnp.float32
BF16 = jnp.bfloat16
MESH = pl.DeviceIdType.MESH
VMEM_LIMIT = 58 * 2**20


def place():
    tp = lax.axis_index("tp")
    return tp, tp // 8, lax.rem(tp // 2, NY), lax.rem(tp, 2)


def tp_of(x, y, c):
    return x * 8 + y * 2 + c


def next_of(p, step):
    return lax.rem(p + step + 4, 4)


def z_peer(step):
    z = lax.axis_index("role") * 2 + lax.axis_index("grp")
    other = lax.rem(z + step, 8)
    return z, other, {"role": other // 2, "grp": lax.rem(other, 2)}


def remote(src, dst, send, recv, device):
    return pltpu.make_async_remote_copy(
        src_ref=src, dst_ref=dst, send_sem=send, recv_sem=recv, device_id=device, device_id_type=MESH
    )


def chip_peer(x, y, c, step):
    other = lax.rem(x * 4 + y + step, 16)
    return other, {"tp": tp_of(other // 4, lax.rem(other, 4), c)}


def greet_start(x, y, c):
    barrier = pltpu.get_barrier_semaphore()
    pl.semaphore_signal(barrier, inc=1, device_id={"tp": tp_of(x, y, 1 - c)}, device_id_type=MESH)

    def chips(step, carry):
        _, device = chip_peer(x, y, c, step)
        pl.semaphore_signal(barrier, inc=1, device_id=device, device_id_type=MESH)
        return carry

    lax.fori_loop(1, 16, chips, 0)

    def planes(step, carry):
        _, _, device = z_peer(step)
        pl.semaphore_signal(barrier, inc=1, device_id=device, device_id_type=MESH)
        return carry

    lax.fori_loop(1, 8, planes, 0)


def greet_wait():
    pl.semaphore_wait(pltpu.get_barrier_semaphore(), 1 + 15 + 7)


class Ring:
    def __init__(self, data, near, far, part, pos, plus, minus, send, recv, base, sign=1):
        self.data, self.near, self.far, self.part = data, near, far, part
        self.pos, self.plus, self.minus = pos, plus, minus
        self.send, self.recv, self.base = send, recv, base
        self.sign = sign
        self.copies = {}

    def cut(self, ref, side):
        return ref.at[(Ellipsis, self.part[side])]

    def go(self, key, number, src, dst, device):
        copy = remote(src, dst, self.send.at[self.base + number], self.recv.at[self.base + number], device)
        copy.start()
        self.copies[key] = copy

    def start_far(self):
        chunk = self.data.at[next_of(self.pos, 2)]
        self.go("far0", 0, self.cut(chunk, 0), self.cut(self.far, 0), self.plus)
        self.go("far1", 1, self.cut(chunk, 1), self.cut(self.far, 1), self.minus)

    def start_near(self):
        up, down = self.data.at[next_of(self.pos, self.sign)], self.data.at[next_of(self.pos, -self.sign)]
        self.go("up1", 2, self.cut(up, 1), self.cut(self.near.at[0], 1), self.plus)
        self.go("down0", 3, self.cut(down, 0), self.cut(self.near.at[1], 0), self.minus)

    def add(self, chunk, side):
        ref, extra = self.cut(chunk, side), self.cut(self.far, side)
        ref[...] = (ref[...].astype(F32) + extra[...].astype(F32)).astype(ref.dtype)

    def pass_on(self):
        up, down = self.data.at[next_of(self.pos, self.sign)], self.data.at[next_of(self.pos, -self.sign)]
        self.copies["far0"].wait_recv()
        self.add(up, 0)
        self.go("up0", 4, self.cut(up, 0), self.cut(self.near.at[0], 0), self.plus)
        self.copies["far1"].wait_recv()
        self.add(down, 1)
        self.go("down1", 5, self.cut(down, 1), self.cut(self.near.at[1], 1), self.minus)

    def result(self, side):
        for key in ("up%d" % side, "down%d" % side):
            self.copies[key].wait_recv()
        own = self.cut(self.data.at[self.pos], side)[...].astype(F32)
        left = self.cut(self.near.at[0], side)[...].astype(F32)
        right = self.cut(self.near.at[1], side)[...].astype(F32)
        return own + (left + right)

    def close(self):
        for copy in self.copies.values():
            copy.wait_send()


def latent_rows(rows, q_gain, kv_gain, cosine, sine):
    q = rows[:, :QL]
    kv = rows[:, QL : QL + KL]
    turn = rows[:, QL + KL :]
    q = q * lax.rsqrt(jnp.mean(q * q, axis=-1, keepdims=True) + EPS) * q_gain
    kv = kv * lax.rsqrt(jnp.mean(kv * kv, axis=-1, keepdims=True) + EPS) * kv_gain
    turn = rope_tile(turn, cosine, sine)
    lane = lax.broadcasted_iota(jnp.int32, turn.shape, 1)
    turn = jnp.where(lane < RD, turn, 0.0)
    return q, kv, turn


def rope_tile(tile, cosine, sine):
    lane = lax.broadcasted_iota(jnp.int32, tile.shape, 1)
    swapped = jnp.where(lane % RD < RD // 2, pltpu.roll(tile, 96, 1), pltpu.roll(tile, 32, 1))
    return tile * cosine + swapped * sine


def turn_tables(pos, freq):
    turn = pos * freq
    lane = lax.broadcasted_iota(jnp.int32, turn.shape, 1)
    sine = jnp.sin(turn)
    return jnp.cos(turn), jnp.where(lane % RD < RD // 2, -sine, sine)


NT = (((1,), (1,)), ((), ()))
TN = (((0,), (0,)), ((), ()))


def split_query(query, cosine, sine):
    nope, rope = [], []
    lane = lax.broadcasted_iota(jnp.int32, (query.shape[0], 128), 1)
    for pair in range(query.shape[1] // 384):
        t0, t1, t2 = [query[:, 384 * pair + 128 * i : 384 * pair + 128 * i + 128] for i in range(3)]
        nope.append(t0.astype(BF16))
        nope.append(jnp.where(lane < 64, pltpu.roll(t1, 64, 1), pltpu.roll(t2, 64, 1)).astype(BF16))
        rope.append(rope_tile(jnp.where(lane < 64, t1, t2), cosine, sine).astype(BF16))
    return nope, rope


def whole_kernel(
    xt_ref, xd_ref, wqa_ref, wkva_ref, qg_ref, kvg_ref, freq_ref, len_ref, docs_ref, wqb_hbm, wkvb_hbm, wo_hbm,
    out_ref, outd_ref,
    wqb, wkvb, wo, wot, wkv_s, p0, p1, c0, c1, near0, near1, far0, far1, q0, q1, in0, in1,
    xd_all, dec, dec_in, tiles, tiles_in, sums_in, rows_in,
    rows_s, square_s, square_in, gain_s,
    zb, zd, qabs_s, qrope_s, pos_s, cos_s, sin_s, kv_s, turn_s, o_s, od_s,
    t0, t1, tc0, tc1, tnear0, tnear1, tfar0, tfar1, tq0, tq1, tqin0, tqin1,
    dd, dt, dc, dn, dz,
    ws, zs, zr, cs, cr, rs, rr, ds, dr, es, er, gs, gr, ks, kr, ms, mr,
    us, ur, vs, vr, fs, fr, hs, hr, ys, yr, qs, qr,
):
    tp, x, y, c = place()
    chip = x * 4 + y
    z, _, _ = z_peer(0)
    peer = {"tp": tp_of(x, y, 1 - c)}
    xp, xm = {"tp": tp_of(next_of(x, 1), y, c)}, {"tp": tp_of(next_of(x, -1), y, c)}
    yp, ym = {"tp": tp_of(x, next_of(y, 1), c)}, {"tp": tp_of(x, next_of(y, -1), c)}
    greet_start(x, y, c)
    loads = [
        pltpu.make_async_copy(src, dst, ws.at[i])
        for i, (src, dst) in enumerate(((wo_hbm, wo), (wkvb_hbm, wkvb), (wqb_hbm, wqb)))
    ]
    for load in loads:
        load.start()

    wkv_s[...] = jnp.zeros_like(wkv_s)
    wkv_s[:, : KL + RD] = wkva_ref[...]
    order = (2, 1, 3, 0)
    cut_q = 1024
    sign = 1 - 2 * c

    def product(s):
        rows = xt_ref[:, 256 * s : 256 * s + 256]
        for cc, w, lo in (
            (0, wqa_ref[:, :cut_q], 0),
            (1, wqa_ref[:, cut_q:], 0),
            (1, wkv_s[...], QL - cut_q),
        ):
            wide = w.shape[1]
            val = lax.dot_general(rows, w, TN, preferred_element_type=F32).reshape(NX, NY, 2, 8, wide)
            p0[s, cc, :, :, :, lo : lo + wide] = val[:, :, 0]
            for yy in range(NY):
                p1[s, cc, yy, :, :, lo : lo + wide] = val[:, yy, 1]
        p0[s, 0, :, :, :, cut_q:] = jnp.zeros((NX, NY, 8, HALF - cut_q), F32)
        p1[s, 0, :, :, :, cut_q:] = jnp.zeros((NX, NY, 8, HALF - cut_q), F32)

    lanes = (slice(0, SPLIT), slice(SPLIT, HALF))
    ka, kb = lanes
    copies = []

    def push(block, device):
        n = len(copies)
        copy = remote(block, block, ks.at[n], kr.at[n], device)
        copy.start()
        copies.append(copy)
        return copy

    def along_x(d):
        return {"tp": tp_of(next_of(x, d), y, c)}

    def along_y(d):
        return {"tp": tp_of(x, next_of(y, d), c)}

    class Front:
        def __init__(self, s):
            self.s = s
            self.core = ([], [])
            self.parts = ((p0, c0, x, self.core[0]), (p1, c1, y, self.core[1]))
            self.rings = (
                Ring(
                    p0.at[s, c], near0.at[s], far0.at[s], lanes, x, along_x(sign), along_x(-sign), rs, rr, 18 * s, sign
                ),
                Ring(
                    p1.at[s, c], near1.at[s], far1.at[s], lanes, y, along_y(sign), along_y(-sign), rs, rr, 18 * s + 6,
                    sign,
                ),
            )
            self.direct = []

        def swap(self):
            for i, d in enumerate(order):
                for h, (p, came, pos_p, list_p) in enumerate(self.parts):
                    k, n = next_of(pos_p, d), 8 * self.s + 2 * i + h
                    copy = remote(p.at[self.s, 1 - c, k], came.at[self.s, k], cs.at[n], cr.at[n], peer)
                    copy.start()
                    list_p.append(copy)

        def take(self, i, h):
            p, came, pos_p, list_p = self.parts[h]
            list_p[i].wait_recv()
            k = next_of(pos_p, order[i])
            p[self.s, c, k] = p[self.s, c, k] + came[self.s, k]

        def first(self):
            for h in range(2):
                self.take(0, h)
                self.rings[h].start_far()
            for h in range(2):
                self.take(1, h)
                self.take(2, h)
                self.rings[h].start_near()
            for h in range(2):
                self.take(3, h)

        def pass_on(self):
            for ring in self.rings:
                ring.pass_on()

        def second(self):
            for h, (q, box, pos_h, dev) in enumerate(((q0, in0, y, along_y), (q1, in1, x, along_x))):
                for side in range(2):
                    q[self.s, :, :, lanes[side]] = self.rings[h].result(side)
                for d in (2, 1, 3):
                    n = 18 * self.s + 12 + 3 * h + d - 1
                    copy = remote(
                        q.at[self.s, next_of(pos_h, d)], box.at[self.s, d - 1], rs.at[n], rr.at[n], dev(d)
                    )
                    copy.start()
                    self.direct.append(copy)

        def rows(self):
            for copy in self.direct:
                copy.wait_recv()
            s = self.s
            top = q0[s, y] + (in0[s, 0] + in0[s, 1]) + in0[s, 2]
            low = q1[s, x] + (in1[s, 0] + in1[s, 1]) + in1[s, 2]
            rows = jnp.concatenate([top, low], axis=0)
            rows_s[s] = rows
            left = jnp.sum(rows[:, :512] * rows[:, :512], axis=-1, keepdims=True)
            right = jnp.sum(rows[:, 512:cut_q] * rows[:, 512:cut_q], axis=-1, keepdims=True)
            square_s[s, 0] = jnp.broadcast_to(left + jnp.where(c == 0, right, 0.0), (16, 128))
            square_s[s, 1] = jnp.broadcast_to(right, (16, 128))
            self.square = remote(square_s.at[s, 0], square_in.at[s], qs.at[s], qr.at[s], peer)
            self.square.start()

        def norm(self):
            s = self.s
            self.square.wait_recv()
            rows = rows_s[s]
            mean_q = (square_s[s, 0] + square_in[s])[:, 0:1] * (1.0 / QL)
            mean_kv = square_s[s, 1][:, 0:1] * (1.0 / KL)
            scale_q, scale_kv = lax.rsqrt(mean_q + EPS), lax.rsqrt(mean_kv + EPS)
            gain = gain_s[pl.ds(c, 1), :]
            at = pl.ds(pl.multiple_of(256 * s + 16 * chip, 16), 16)
            turn = rope_tile(rows[:, cut_q:], cos_s[at, :], sin_s[at, :])
            lane = lax.broadcasted_iota(jnp.int32, turn.shape, 1)
            zb[s, c, x, y, :, 0:512] = (rows[:, :512] * scale_q * gain[:, :512]).astype(BF16)
            both = jnp.where(c == 0, scale_q, scale_kv)
            zb[s, c, x, y, :, 512:cut_q] = (rows[:, 512:cut_q] * both * gain[:, 512:cut_q]).astype(BF16)
            zb[s, c, x, y, :, cut_q:] = jnp.where(lane < RD, turn, 0.0).astype(BF16)

        def gather_one(self):
            s = self.s
            self.one = []
            for d in (1, 3, 2):
                self.one.append(push(zb.at[s, c, x, y, :, ka], along_x(d)))
                self.one.append(push(zb.at[s, c, x, y, :, kb], along_y(d)))

        def gather_two(self):
            s = self.s
            self.two_a, self.two_b = [], []
            for copy in self.one:
                copy.wait_recv()
            for d in (1, 3, 2):
                self.two_a.append(push(zb.at[s, c, :, y, :, ka], along_y(d)))
                self.two_b.append(push(zb.at[s, c, x, :, :, kb], along_x(d)))

        def gather_mate(self):
            for copy in self.two_a:
                copy.wait_recv()
            self.mates = [push(zb.at[self.s, c, :, :, :, ka], peer)]
            for copy in self.two_b:
                copy.wait_recv()
            self.mates.append(push(zb.at[self.s, c, :, :, :, kb], peer))

        def gather_end(self):
            for copy in self.mates:
                copy.wait_recv()

        def close(self):
            for copy in self.core[0] + self.core[1] + self.direct + [self.square]:
                copy.wait_send()
            for ring in self.rings:
                ring.close()

    f0, f1 = Front(0), Front(1)
    product(0)
    greet_wait()
    f0.swap()
    xd_all[z] = xd_ref[...]

    def send_z(step, carry):
        zz, _, device = z_peer(step)
        remote(xd_ref, xd_all.at[zz], zs.at[step], zr.at[step], device).start()
        return carry

    lax.fori_loop(1, 8, send_z, 0)
    product(1)
    f1.swap()
    f0.first()
    f1.first()

    def wait_z(step, carry):
        zz, other, device = z_peer(step)
        remote(xd_ref, xd_all.at[zz], zs.at[step], zr.at[step], device).wait()
        return carry

    lax.fori_loop(1, 8, wait_z, 0)
    ii = lax.broadcasted_iota(jnp.int32, (16, 128), 0)
    jj = lax.broadcasted_iota(jnp.int32, (16, 128), 1)
    docs = docs_ref[...].reshape(1, 128)
    sel_in = jnp.where(docs == z * 16 + ii, 1.0, 0.0).astype(BF16)
    asked = jnp.dot(sel_in, xd_all[...].reshape(128, -1), preferred_element_type=F32).astype(BF16)
    for w_ref, lo, wide in ((wqa_ref, 0, QL), (wkv_s, QL, W - QL)):
        val = jnp.dot(asked, w_ref[...], preferred_element_type=F32)
        dec[:, :, lo : lo + wide] = val.reshape(2, 8, wide)
    dec_core = remote(dec.at[1 - c], dec_in, ds.at[0], dr.at[0], peer)
    dec_core.start()
    f0.pass_on()

    q_gain, kv_gain = qg_ref[...].reshape(1, QL), kvg_ref[...].reshape(1, KL)
    gain_s[...] = jnp.zeros_like(gain_s)
    gain_s[0:1, :cut_q] = q_gain[:, :cut_q]
    gain_s[1:2, : QL - cut_q] = q_gain[:, cut_q:]
    gain_s[1:2, QL - cut_q : cut_q] = kv_gain
    lens = len_ref[pl.ds(z, 1), :].astype(F32)
    i16 = lax.broadcasted_iota(jnp.int32, (16, 16), 0)
    j16 = lax.broadcasted_iota(jnp.int32, (16, 16), 1)
    spread = jnp.broadcast_to(lens, (16, 16))
    len_col = jnp.sum(jnp.where(i16 == j16, spread, 0.0), axis=1, keepdims=True)
    end_col = jnp.sum(jnp.where(j16 <= i16, spread, 0.0), axis=1, keepdims=True)
    end_row = jnp.sum(jnp.where(i16 <= j16, jnp.broadcast_to(len_col, (16, 16)), 0.0), axis=0, keepdims=True)
    token = lax.broadcasted_iota(jnp.int32, (512, 16), 0).astype(F32)
    begun = jnp.sum(jnp.where(token >= end_row, jnp.broadcast_to(lens, (512, 16)), 0.0), axis=1, keepdims=True)
    pos = lax.broadcasted_iota(jnp.int32, (512, 128), 0).astype(F32) - begun
    pos_s[...] = pos
    freq = freq_ref[...]
    for i in range(4):
        part = pl.ds(128 * i, 128)
        cos_s[part, :], sin_s[part, :] = turn_tables(pos_s[part, :], freq)
    cosd, sind = turn_tables(jnp.broadcast_to(len_col, (16, 128)), freq)

    dec_core.wait()
    mine = dec[c] + dec_in[...]
    for j in range(16):
        tiles[j, :, 0:128] = mine[:, 128 * j : 128 * j + 128]
        tiles[j, :, 128:256] = mine[:, QL + KL :]

    def send_tile(step, carry):
        other, device = chip_peer(x, y, c, step)
        remote(tiles.at[other], tiles_in.at[chip], es.at[step], er.at[step], device).start()
        return carry

    lax.fori_loop(1, 16, send_tile, 0)
    tiles_in[chip] = tiles[chip]

    f0.second()
    f1.pass_on()
    loads[0].wait()

    def turn_wo(k, carry):
        cut = pl.multiple_of(k * 896, 128)
        wot[pl.ds(cut, 896), :] = wo[:, pl.ds(cut, 896)].T
        return carry

    def wait_tile(step, carry):
        other, device = chip_peer(x, y, c, step)
        remote(tiles.at[other], tiles_in.at[chip], es.at[step], er.at[step], device).wait()
        return carry

    lax.fori_loop(1, 16, wait_tile, 0)
    total = jnp.sum(tiles_in[...], axis=0)
    sums_in[chip] = total[:, :128]

    def send_sum(step, carry):
        other, device = chip_peer(x, y, c, step)
        remote(sums_in.at[chip], sums_in.at[chip], gs.at[step], gr.at[step], device).start()
        return carry

    lax.fori_loop(1, 16, send_sum, 0)
    f0.rows()
    f1.second()
    f0.norm()
    f0.gather_one()

    def wait_sum(step, carry):
        other, device = chip_peer(x, y, c, step)
        remote(sums_in.at[chip], sums_in.at[chip], gs.at[step], gr.at[step], device).wait()
        return carry

    lax.fori_loop(1, 16, wait_sum, 0)
    for j in range(16):
        rows_in[c, :, 128 * j : 128 * j + 128] = sums_in[j]
    rows_in[c, :, QL + KL : W] = total[:, 128:]
    dec_mate = remote(rows_in.at[c], rows_in.at[c], ms.at[0], mr.at[0], peer)
    dec_mate.start()
    f1.rows()
    f0.gather_two()
    f1.norm()
    f1.gather_one()
    dec_mate.wait()
    q, kv, turn = latent_rows(rows_in[...].reshape(16, W), q_gain, kv_gain, cosd, sind)
    zd[:, 0:QL] = q.astype(BF16)
    zd[:, QL : QL + KL] = kv.astype(BF16)
    zd[:, QL + KL : W] = turn.astype(BF16)
    heads = 4
    scale = 1.0 / float(NOPE + RD) ** 0.5
    wide = NOPE + VD
    for load in loads[1:]:
        load.wait()
    query = jnp.dot(zd[:, :QL], wqb[...], preferred_element_type=F32)
    dec_nope, dec_rope = split_query(query, cosd, sind)
    for h in range(heads):
        up_k = wkvb[:, wide * h : wide * h + NOPE]
        qabs_s[h] = lax.dot_general(dec_nope[h], up_k, NT, preferred_element_type=F32).astype(BF16)
        qrope_s[h // 2] = dec_rope[h // 2]
    f1.gather_two()
    lax.fori_loop(0, 4, turn_wo, 0)
    f0.gather_mate()
    lax.fori_loop(4, 8, turn_wo, 0)
    f0.gather_end()

    def project(s):
        rows = slice(256 * s, 256 * s + 256)
        latent = zb[s, 1, :, :, :, QL - cut_q : cut_q].reshape(256, KL)
        kv_s[rows, :] = jnp.dot(latent, wkvb[...], preferred_element_type=F32).astype(BF16)
        turn = zb[s, 1, :, :, :, cut_q:].reshape(256, 128)
        turn_s[0, rows, :] = turn
        turn_s[1, rows, :] = pltpu.roll(turn.astype(F32), 64, 1).astype(BF16)

    def block(s):
        def attend(j, carry):
            i = 2 * s + j
            first = pl.multiple_of(i * 128, 128)
            begin = pl.multiple_of(jnp.maximum(i - 1, 0) * 128, 128)
            rows, keys = pl.ds(first, 128), pl.ds(begin, 256)
            chips = pl.ds(2 * j, 2)
            query = jnp.dot(
                zb[s, 0, chips, :, :, :cut_q].reshape(128, cut_q), wqb[:cut_q, :], preferred_element_type=F32
            )
            query = query + jnp.dot(
                zb[s, 1, chips, :, :, : QL - cut_q].reshape(128, QL - cut_q), wqb[cut_q:, :], preferred_element_type=F32
            )
            nope, rope = split_query(query, cos_s[rows, :], sin_s[rows, :])
            own = first + lax.broadcasted_iota(jnp.int32, (128, 256), 0)
            other = begin + lax.broadcasted_iota(jnp.int32, (128, 256), 1)
            back = (own - other).astype(F32)
            keep = (back >= 0) & (back <= jnp.concatenate([pos_s[rows, :]] * 2, axis=1))
            for h in range(heads):
                q = jnp.concatenate([nope[h], rope[h // 2]], axis=1)
                k = jnp.concatenate([kv_s[keys, wide * h : wide * h + NOPE], turn_s[h % 2, keys, :]], axis=1)
                s_h = lax.dot_general(q, k, NT, preferred_element_type=F32) * scale
                s_h = jnp.where(keep, s_h, -1e30)
                e = jnp.exp(s_h - jnp.max(s_h, axis=-1, keepdims=True))
                p = (e * (1.0 / jnp.sum(e, axis=-1, keepdims=True))).astype(BF16)
                v = kv_s[keys, wide * h + NOPE : wide * h + wide]
                o = jnp.dot(p, v, preferred_element_type=F32)
                o_s[rows, VD * h : VD * h + VD] = o.astype(BF16)
            return carry

        lax.fori_loop(0, 2, attend, 0)

    def decode():
        latent, own_lat = zb[:, 1, :, :, :, QL - cut_q : cut_q].reshape(512, KL), zd[:, QL : QL + KL]
        turns, own_turn = (turn_s[0], turn_s[1]), zd[:, QL + KL : W].astype(F32)
        own_turns = (own_turn.astype(BF16), pltpu.roll(own_turn, 64, 1).astype(BF16))
        at = lax.broadcasted_iota(jnp.int32, (16, 512), 1).astype(F32)
        keep = (at < end_col) & (at >= end_col - len_col)
        diag = i16 == j16
        for h in range(heads):
            q_abs, q_rope = qabs_s[h], qrope_s[h // 2]
            s = lax.dot_general(q_abs, latent, NT, preferred_element_type=F32)
            s = (s + lax.dot_general(q_rope, turns[h % 2], NT, preferred_element_type=F32)) * scale
            s = jnp.where(keep, s, -1e30)
            t = lax.dot_general(q_abs, own_lat, NT, preferred_element_type=F32)
            t = (t + lax.dot_general(q_rope, own_turns[h % 2], NT, preferred_element_type=F32)) * scale
            t = jnp.where(diag, t, -1e30)
            top = jnp.maximum(jnp.max(s, axis=-1, keepdims=True), jnp.max(t, axis=-1, keepdims=True))
            e, f = jnp.exp(s - top), jnp.exp(t - top)
            part = 1.0 / (jnp.sum(e, axis=-1, keepdims=True) + jnp.sum(f, axis=-1, keepdims=True))
            lat = jnp.dot((e * part).astype(BF16), latent, preferred_element_type=F32)
            lat = lat + jnp.dot((f * part).astype(BF16), own_lat, preferred_element_type=F32)
            up_v = wkvb[:, wide * h + NOPE : wide * h + wide]
            o = jnp.dot(lat.astype(BF16), up_v, preferred_element_type=F32)
            od_s[:, VD * h : VD * h + VD] = o.astype(BF16)

    def output(s):
        far_x, far_y = next_of(x, 2), next_of(y, 2) // 2

        def part(n, carry):
            k = jnp.where(
                n < 2,
                2 * far_x + n,
                jnp.where(n < 5, 2 * next_of(far_x, n - 1) + far_y, 2 * next_of(far_x, n - 4) + 1 - far_y),
            )
            xx, yy = k // 2, 2 * lax.rem(k, 2)
            w = wot[pl.ds(pl.multiple_of(k * 896, 128), 896), :]
            val = lax.dot_general(w, o_s[256 * s : 256 * s + 256, :], NT, preferred_element_type=F32).astype(BF16)
            for j in range(4):
                t0[s, j % 2, xx, yy + j // 2] = val[224 * j : 224 * j + 112]
                t1[s, j % 2, yy + j // 2, xx] = val[224 * j + 112 : 224 * j + 224]
            return carry

        return part

    half = (slice(0, 128), slice(128, 256))

    class Stage:
        def __init__(self, s):
            self.s = s
            self.core = ([], [])
            self.rings = (
                Ring(t0.at[s, c], tnear0.at[s], tfar0.at[s], half, x, xp, xm, us, ur, 18 * s),
                Ring(t1.at[s, c], tnear1.at[s], tfar1.at[s], half, y, yp, ym, us, ur, 18 * s + 6),
            )
            self.lasts = [
                (tq0, tqin0, y, lambda d: tp_of(x, next_of(y, d), c)),
                (tq1, tqin1, x, lambda d: tp_of(next_of(x, d), y, c)),
            ]
            self.direct = ([], [])
            self.parts = ((t0, tc0, x, self.core[0]), (t1, tc1, y, self.core[1]))

        def swap(self, which):
            for i in which:
                d = order[i]
                for n, (t, came, pos_t, list_t) in enumerate(self.parts):
                    k, m = next_of(pos_t, d), 8 * self.s + 2 * i + n
                    copy = remote(t.at[self.s, 1 - c, k], came.at[self.s, k], vs.at[m], vr.at[m], peer)
                    copy.start()
                    list_t.append(copy)

        def take(self, i):
            for t, came, pos_t, list_t in self.parts:
                list_t[i].wait_recv()
                k = next_of(pos_t, order[i])
                t[self.s, c, k] = (t[self.s, c, k].astype(F32) + came[self.s, k].astype(F32)).astype(BF16)

        def first(self):
            self.take(0)
            for ring in self.rings:
                ring.start_far()
            self.take(1)
            self.take(2)
            for ring in self.rings:
                ring.start_near()
            self.take(3)

        def pass_on(self):
            for ring in self.rings:
                ring.pass_on()

        def second(self):
            for side in range(2):
                tq0[self.s, :, :, half[side]] = self.rings[0].result(side).astype(BF16)
                tq1[self.s, :, :, half[side]] = self.rings[1].result(side).astype(BF16)
            for d in (2, 1, 3):
                for h, (data, box, pos_q, dev) in enumerate(self.lasts):
                    n = 18 * self.s + 12 + 3 * h + d - 1
                    copy = remote(
                        data.at[self.s, next_of(pos_q, d)], box.at[self.s, d - 1], us.at[n], ur.at[n], {"tp": dev(d)}
                    )
                    copy.start()
                    self.direct[h].append(copy)

        def finish(self):
            for h, (data, box, pos_q, dev) in enumerate(self.lasts):
                for copy in self.direct[h]:
                    copy.wait_recv()
                came = [box[self.s, i].astype(F32) for i in range(3)]
                total = data[self.s, pos_q].astype(F32) + (came[0] + came[1]) + came[2]
                out_ref[112 * h : 112 * h + 112, 256 * self.s : 256 * self.s + 256] = total.astype(BF16)

        def close(self):
            for copy in self.core[0] + self.core[1]:
                copy.wait_send()
            for ring in self.rings:
                ring.close()
            for copy in self.direct[0] + self.direct[1]:
                copy.wait_send()

    s0, s1 = Stage(0), Stage(1)

    def produce(stage):
        part = output(stage.s)
        lax.fori_loop(0, 5, part, 0)
        stage.swap((0,))
        lax.fori_loop(5, 8, part, 0)
        stage.swap((1, 2, 3))

    project(0)
    block(0)
    f1.gather_mate()
    produce(s0)
    s0.first()
    f1.gather_end()
    project(1)
    block(1)
    s0.pass_on()
    produce(s1)
    s1.first()
    s0.second()
    decode()

    dd[...] = jnp.zeros_like(dd)

    def dec_part(k, carry):
        w = wo[:, pl.ds(pl.multiple_of(k * 896, 128), 896)]
        dd[:, :896] = jnp.dot(od_s[...], w, preferred_element_type=F32)
        for j in range(4):
            at = 224 * j // 128 * 128
            v = dd[:, at : at + 384]
            if 224 * j - at:
                v = pltpu.roll(v, 384 - (224 * j - at), 1)
            dt[j % 2, 2 * k + j // 2] = v[:, :256].astype(BF16)
        return carry

    lax.fori_loop(0, 8, dec_part, 0)
    dec_swap = remote(dt.at[1 - c], dc, fs.at[0], fr.at[0], peer)
    dec_swap.start()
    s1.pass_on()
    s0.finish()
    dec_swap.wait()
    dt[c] = (dt[c].astype(F32) + dc[...].astype(F32)).astype(BF16)

    def send_out(step, carry):
        other, device = chip_peer(x, y, c, step)
        remote(dt.at[c, other], dn.at[chip], hs.at[step], hr.at[step], device).start()
        return carry

    lax.fori_loop(1, 16, send_out, 0)
    dn[chip] = dt[c, chip]

    def wait_out(step, carry):
        other, device = chip_peer(x, y, c, step)
        remote(dt.at[c, other], dn.at[chip], hs.at[step], hr.at[step], device).wait()
        return carry

    lax.fori_loop(1, 16, wait_out, 0)
    dz[z] = jnp.sum(dn[...].astype(F32), axis=0).astype(BF16)

    def send_back(step, carry):
        zz, _, device = z_peer(step)
        remote(dz.at[zz], dz.at[zz], ys.at[step], yr.at[step], device).start()
        return carry

    lax.fori_loop(1, 8, send_back, 0)
    s1.second()

    def wait_back(step, carry):
        zz, _, device = z_peer(step)
        remote(dz.at[zz], dz.at[zz], ys.at[step], yr.at[step], device).wait()
        return carry

    lax.fori_loop(1, 8, wait_back, 0)
    wanted = jnp.sum(jnp.where(jj == z * 16 + ii, docs, 0).astype(F32), axis=1, keepdims=True)
    sel_out = jnp.where(jj.astype(F32) == wanted, 1.0, 0.0).astype(BF16)
    picked = jnp.dot(sel_out, dz[...].reshape(128, 256), preferred_element_type=F32)
    outd_ref[...] = picked[:, :224].astype(BF16)

    s1.finish()
    for copy in copies:
        copy.wait_send()
    f0.close()
    f1.close()
    s0.close()
    s1.close()


def whole(xt, xd, wq_a, wkv_a, q_gain, kv_gain, freq, doc_len, docs, wq_b, wkv_b, wo):
    vm = pl.BlockSpec(memory_space=pltpu.VMEM)
    hbm = pl.BlockSpec(memory_space=pl.ANY)
    dma = pltpu.SemaphoreType.DMA
    shapes = [
        (wq_b.shape, BF16), (wkv_b.shape, BF16), (wo.shape, BF16), (wo.shape[::-1], BF16),
        ((wq_a.shape[0], W - QL), BF16),
        ((2, 2, 4, 4, 8, HALF), F32), ((2, 2, 4, 4, 8, HALF), F32),
        ((2, 4, 4, 8, HALF), F32), ((2, 4, 4, 8, HALF), F32),
        ((2, 2, 4, 8, HALF), F32), ((2, 2, 4, 8, HALF), F32),
        ((2, 4, 8, HALF), F32), ((2, 4, 8, HALF), F32),
        ((2, 4, 8, HALF), F32), ((2, 4, 8, HALF), F32),
        ((2, 3, 8, HALF), F32), ((2, 3, 8, HALF), F32),
        ((8,) + xd.shape, BF16), ((2, 8, W), F32), ((8, W), F32),
        ((16, 8, 256), F32), ((16, 8, 256), F32), ((16, 8, 128), F32), ((2, 8, W), F32),
        ((2, 16, HALF), F32), ((2, 2, 16, 128), F32), ((2, 16, 128), F32), ((8, HALF), F32),
        ((2, 2, NX, NY, 16, HALF), BF16), ((16, W), BF16), ((4, 16, KL), BF16), ((2, 16, 128), BF16), ((512, 128), F32), ((512, 128), F32), ((512, 128), F32),
        ((512, wkv_b.shape[1]), BF16), ((2, 512, 128), BF16), ((512, 512), BF16), ((16, 512), BF16),
        ((2, 2, 4, 4, 112, 256), BF16), ((2, 2, 4, 4, 112, 256), BF16),
        ((2, 4, 4, 112, 256), BF16), ((2, 4, 4, 112, 256), BF16),
        ((2, 2, 4, 112, 256), BF16), ((2, 2, 4, 112, 256), BF16),
        ((2, 4, 112, 256), BF16), ((2, 4, 112, 256), BF16),
        ((2, 4, 112, 256), BF16), ((2, 4, 112, 256), BF16),
        ((2, 3, 112, 256), BF16), ((2, 3, 112, 256), BF16),
        ((16, 1024), F32), ((2, 16, 16, 256), BF16), ((16, 16, 256), BF16), ((16, 16, 256), BF16),
        ((8, 16, 256), BF16),
    ]
    counts = (3, 8, 8, 16, 16, 36, 36, 1, 1, 16, 16, 16, 16, 28, 28, 1, 1, 36, 36, 16, 16, 1, 1, 16, 16, 8, 8, 2, 2)
    return pl.pallas_call(
        whole_kernel,
        out_shape=(jax.ShapeDtypeStruct((224, 512), BF16), jax.ShapeDtypeStruct((16, 224), BF16)),
        in_specs=[vm] * 9 + [hbm] * 3,
        out_specs=(vm, vm),
        scratch_shapes=[pltpu.VMEM(shape, kind) for shape, kind in shapes] + [dma((n,)) for n in counts],
        compiler_params=pltpu.CompilerParams(
            collective_id=0, has_side_effects=True, vmem_limit_bytes=VMEM_LIMIT
        ),
        name="whole",
    )(xt, xd, wq_a, wkv_a, q_gain, kv_gain, freq, doc_len, docs, wq_b, wkv_b, wo)


def hand_over_kernel(a_ref, b_ref, out_ref, outd_ref):
    out_ref[...] = a_ref[...]
    outd_ref[...] = b_ref[...]


def hand_over(a, b):
    vm = pl.BlockSpec(memory_space=pltpu.VMEM)
    return pl.pallas_call(
        hand_over_kernel,
        out_shape=(jax.ShapeDtypeStruct(a.shape, a.dtype), jax.ShapeDtypeStruct(b.shape, b.dtype)),
        in_specs=[vm, vm],
        out_specs=(vm, vm),
        name="hand_over",
    )(a, b)


def per_device(x_pre, x_dec, wq_a, wkv_a, q_gain, kv_gain, wq_b, wkv_b, wo, doc_len, request_docs):
    half = RD // 2
    freq = np.tile(10000.0 ** (-np.arange(half) / half), 4).astype(np.float32)[None, :]
    out_t, out_dec = whole(
        x_pre.T, x_dec, wq_a, wkv_a, q_gain, kv_gain, jnp.asarray(freq), doc_len, request_docs, wq_b, wkv_b, wo
    )
    out_t, out_dec = hand_over(out_t, out_dec)
    return out_t.T, out_dec


def solution(mesh):
    placed = (
        P(("role", "grp"), "tp"),
        P(("role", "grp"), "tp"),
        P("tp", None),
        P("tp", None),
        P(),
        P(),
        P(None, "tp"),
        P(None, "tp"),
        P("tp", None),
        P(),
        P(),
    )
    return jax.shard_map(
        per_device,
        mesh=mesh,
        in_specs=placed,
        out_specs=(P(("role", "grp"), "tp"), P(("role", "grp"), "tp")),
        check_vma=False,
    )
```

```python
import jax
import jax.numpy as jnp
import numpy as np
from jax import lax
from jax.experimental import pallas as pl
from jax.experimental.pallas import tpu as pltpu
from jax.sharding import PartitionSpec as P

QL = 1536
KL = 512
RD = 64
NOPE = 128
VD = 128
NX = 4
NY = 4
W = QL + KL + 128
HALF = 1152
SPLIT = 640
EPS = 1e-06
F32 = jnp.float32
BF16 = jnp.bfloat16
MESH = pl.DeviceIdType.MESH
VMEM_LIMIT = 58 * 2**20


def place():
    tp = lax.axis_index("tp")
    return tp, tp // 8, lax.rem(tp // 2, NY), lax.rem(tp, 2)


def tp_of(x, y, c):
    return x * 8 + y * 2 + c


def next_of(p, step):
    return lax.rem(p + step + 4, 4)


def z_peer(step):
    z = lax.axis_index("role") * 2 + lax.axis_index("grp")
    other = lax.rem(z + step, 8)
    return z, other, {"role": other // 2, "grp": lax.rem(other, 2)}


def remote(src, dst, send, recv, device):
    return pltpu.make_async_remote_copy(
        src_ref=src, dst_ref=dst, send_sem=send, recv_sem=recv, device_id=device, device_id_type=MESH
    )


def chip_peer(x, y, c, step):
    other = lax.rem(x * 4 + y + step, 16)
    return other, {"tp": tp_of(other // 4, lax.rem(other, 4), c)}


def greet_start(x, y, c):
    barrier = pltpu.get_barrier_semaphore()
    pl.semaphore_signal(barrier, inc=1, device_id={"tp": tp_of(x, y, 1 - c)}, device_id_type=MESH)

    def chips(step, carry):
        _, device = chip_peer(x, y, c, step)
        pl.semaphore_signal(barrier, inc=1, device_id=device, device_id_type=MESH)
        return carry

    lax.fori_loop(1, 16, chips, 0)

    def planes(step, carry):
        _, _, device = z_peer(step)
        pl.semaphore_signal(barrier, inc=1, device_id=device, device_id_type=MESH)
        return carry

    lax.fori_loop(1, 8, planes, 0)


def greet_wait():
    pl.semaphore_wait(pltpu.get_barrier_semaphore(), 1 + 15 + 7)


class Ring:
    def __init__(self, data, near, far, part, pos, plus, minus, send, recv, base, sign=1):
        self.data, self.near, self.far, self.part = data, near, far, part
        self.pos, self.plus, self.minus = pos, plus, minus
        self.send, self.recv, self.base = send, recv, base
        self.sign = sign
        self.copies = {}

    def cut(self, ref, side):
        return ref.at[(Ellipsis, self.part[side])]

    def go(self, key, number, src, dst, device):
        copy = remote(src, dst, self.send.at[self.base + number], self.recv.at[self.base + number], device)
        copy.start()
        self.copies[key] = copy

    def start_far(self):
        chunk = self.data.at[next_of(self.pos, 2)]
        self.go("far0", 0, self.cut(chunk, 0), self.cut(self.far, 0), self.plus)
        self.go("far1", 1, self.cut(chunk, 1), self.cut(self.far, 1), self.minus)

    def start_near(self):
        up, down = self.data.at[next_of(self.pos, self.sign)], self.data.at[next_of(self.pos, -self.sign)]
        self.go("up1", 2, self.cut(up, 1), self.cut(self.near.at[0], 1), self.plus)
        self.go("down0", 3, self.cut(down, 0), self.cut(self.near.at[1], 0), self.minus)

    def add(self, chunk, side):
        ref, extra = self.cut(chunk, side), self.cut(self.far, side)
        ref[...] = (ref[...].astype(F32) + extra[...].astype(F32)).astype(ref.dtype)

    def pass_on(self):
        up, down = self.data.at[next_of(self.pos, self.sign)], self.data.at[next_of(self.pos, -self.sign)]
        self.copies["far0"].wait_recv()
        self.add(up, 0)
        self.go("up0", 4, self.cut(up, 0), self.cut(self.near.at[0], 0), self.plus)
        self.copies["far1"].wait_recv()
        self.add(down, 1)
        self.go("down1", 5, self.cut(down, 1), self.cut(self.near.at[1], 1), self.minus)

    def result(self, side):
        for key in ("up%d" % side, "down%d" % side):
            self.copies[key].wait_recv()
        own = self.cut(self.data.at[self.pos], side)[...].astype(F32)
        left = self.cut(self.near.at[0], side)[...].astype(F32)
        right = self.cut(self.near.at[1], side)[...].astype(F32)
        return own + (left + right)

    def close(self):
        for copy in self.copies.values():
            copy.wait_send()


def latent_rows(rows, q_gain, kv_gain, cosine, sine):
    q = rows[:, :QL]
    kv = rows[:, QL : QL + KL]
    turn = rows[:, QL + KL :]
    q = q * lax.rsqrt(jnp.mean(q * q, axis=-1, keepdims=True) + EPS) * q_gain
    kv = kv * lax.rsqrt(jnp.mean(kv * kv, axis=-1, keepdims=True) + EPS) * kv_gain
    turn = rope_tile(turn, cosine, sine)
    lane = lax.broadcasted_iota(jnp.int32, turn.shape, 1)
    turn = jnp.where(lane < RD, turn, 0.0)
    return q, kv, turn


def rope_tile(tile, cosine, sine):
    lane = lax.broadcasted_iota(jnp.int32, tile.shape, 1)
    swapped = jnp.where(lane % RD < RD // 2, pltpu.roll(tile, 96, 1), pltpu.roll(tile, 32, 1))
    return tile * cosine + swapped * sine


def turn_tables(pos, freq):
    turn = pos * freq
    lane = lax.broadcasted_iota(jnp.int32, turn.shape, 1)
    sine = jnp.sin(turn)
    return jnp.cos(turn), jnp.where(lane % RD < RD // 2, -sine, sine)


NT = (((1,), (1,)), ((), ()))
TN = (((0,), (0,)), ((), ()))


def split_query(query, cosine, sine):
    nope, rope = [], []
    lane = lax.broadcasted_iota(jnp.int32, (query.shape[0], 128), 1)
    for pair in range(query.shape[1] // 384):
        t0, t1, t2 = [query[:, 384 * pair + 128 * i : 384 * pair + 128 * i + 128] for i in range(3)]
        nope.append(t0.astype(BF16))
        nope.append(jnp.where(lane < 64, pltpu.roll(t1, 64, 1), pltpu.roll(t2, 64, 1)).astype(BF16))
        rope.append(rope_tile(jnp.where(lane < 64, t1, t2), cosine, sine).astype(BF16))
    return nope, rope


def whole_kernel(
    xt_ref, xd_ref, wqa_ref, wkva_ref, qg_ref, kvg_ref, freq_ref, len_ref, docs_ref, wqb_hbm, wkvb_hbm, wo_hbm,
    out_ref, outd_ref,
    wqb, wkvb, wo, wot, wkv_s, p0, p1, c0, c1, near0, near1, far0, far1, q0, q1, in0, in1,
    xd_all, dec, dec_in, tiles, tiles_in, sums_in, rows_in,
    rows_s, square_s, square_in, gain_s,
    zb, zd, qabs_s, qrope_s, pos_s, cos_s, sin_s, kv_s, turn_s, o_s, od_s,
    t0, t1, tc0, tc1, tnear0, tnear1, tfar0, tfar1, tq0, tq1, tqin0, tqin1,
    dt, dc, dn, dz,
    ws, zs, zr, cs, cr, rs, rr, ds, dr, es, er, gs, gr, ks, kr, ms, mr,
    us, ur, vs, vr, fs, fr, hs, hr, ys, yr, qs, qr,
):
    tp, x, y, c = place()
    chip = x * 4 + y
    z, _, _ = z_peer(0)
    peer = {"tp": tp_of(x, y, 1 - c)}
    xp, xm = {"tp": tp_of(next_of(x, 1), y, c)}, {"tp": tp_of(next_of(x, -1), y, c)}
    yp, ym = {"tp": tp_of(x, next_of(y, 1), c)}, {"tp": tp_of(x, next_of(y, -1), c)}
    greet_start(x, y, c)
    loads = [
        pltpu.make_async_copy(src, dst, ws.at[i])
        for i, (src, dst) in enumerate(((wo_hbm, wo), (wkvb_hbm, wkvb), (wqb_hbm, wqb)))
    ]
    for load in loads:
        load.start()

    wkv_s[...] = jnp.zeros_like(wkv_s)
    wkv_s[:, : KL + RD] = wkva_ref[...]
    order = (2, 1, 3, 0)
    cut_q = 1024
    sign = 1 - 2 * c

    def product(s):
        rows = xt_ref[:, 256 * s : 256 * s + 256]
        for cc, w, lo in (
            (0, wqa_ref[:, :cut_q], 0),
            (1, wqa_ref[:, cut_q:], 0),
            (1, wkv_s[...], QL - cut_q),
        ):
            wide = w.shape[1]
            val = lax.dot_general(rows, w, TN, preferred_element_type=F32).reshape(NX, NY, 2, 8, wide)
            p0[s, cc, :, :, :, lo : lo + wide] = val[:, :, 0]
            for yy in range(NY):
                p1[s, cc, yy, :, :, lo : lo + wide] = val[:, yy, 1]
        p0[s, 0, :, :, :, cut_q:] = jnp.zeros((NX, NY, 8, HALF - cut_q), F32)
        p1[s, 0, :, :, :, cut_q:] = jnp.zeros((NX, NY, 8, HALF - cut_q), F32)

    lanes = (slice(0, SPLIT), slice(SPLIT, HALF))
    ka, kb = lanes
    copies = []

    def push(block, device):
        n = len(copies)
        copy = remote(block, block, ks.at[n], kr.at[n], device)
        copy.start()
        copies.append(copy)
        return copy

    def along_x(d):
        return {"tp": tp_of(next_of(x, d), y, c)}

    def along_y(d):
        return {"tp": tp_of(x, next_of(y, d), c)}

    class Front:
        def __init__(self, s):
            self.s = s
            self.core = ([], [])
            self.parts = ((p0, c0, x, self.core[0]), (p1, c1, y, self.core[1]))
            self.rings = (
                Ring(
                    p0.at[s, c], near0.at[s], far0.at[s], lanes, x, along_x(sign), along_x(-sign), rs, rr, 18 * s, sign
                ),
                Ring(
                    p1.at[s, c], near1.at[s], far1.at[s], lanes, y, along_y(sign), along_y(-sign), rs, rr, 18 * s + 6,
                    sign,
                ),
            )
            self.direct = []

        def swap(self):
            for i, d in enumerate(order):
                for h, (p, came, pos_p, list_p) in enumerate(self.parts):
                    k, n = next_of(pos_p, d), 8 * self.s + 2 * i + h
                    copy = remote(p.at[self.s, 1 - c, k], came.at[self.s, k], cs.at[n], cr.at[n], peer)
                    copy.start()
                    list_p.append(copy)

        def take(self, i, h):
            p, came, pos_p, list_p = self.parts[h]
            list_p[i].wait_recv()
            k = next_of(pos_p, order[i])
            p[self.s, c, k] = p[self.s, c, k] + came[self.s, k]

        def far(self):
            for h in range(2):
                self.take(0, h)
                self.rings[h].start_far()

        def near(self):
            for h in range(2):
                self.take(1, h)
                self.take(2, h)
                self.rings[h].start_near()
            for h in range(2):
                self.take(3, h)

        def pass_on(self):
            for ring in self.rings:
                ring.pass_on()

        def second(self):
            for h, (q, box, pos_h, dev) in enumerate(((q0, in0, y, along_y), (q1, in1, x, along_x))):
                for side in range(2):
                    q[self.s, :, :, lanes[side]] = self.rings[h].result(side)
                for d in (2, 1, 3):
                    n = 18 * self.s + 12 + 3 * h + d - 1
                    copy = remote(
                        q.at[self.s, next_of(pos_h, d)], box.at[self.s, d - 1], rs.at[n], rr.at[n], dev(d)
                    )
                    copy.start()
                    self.direct.append(copy)

        def rows(self):
            for copy in self.direct:
                copy.wait_recv()
            s = self.s
            top = q0[s, y] + (in0[s, 0] + in0[s, 1]) + in0[s, 2]
            low = q1[s, x] + (in1[s, 0] + in1[s, 1]) + in1[s, 2]
            rows = jnp.concatenate([top, low], axis=0)
            rows_s[s] = rows
            left = jnp.sum(rows[:, :512] * rows[:, :512], axis=-1, keepdims=True)
            right = jnp.sum(rows[:, 512:cut_q] * rows[:, 512:cut_q], axis=-1, keepdims=True)
            square_s[s, 0] = jnp.broadcast_to(left + jnp.where(c == 0, right, 0.0), (16, 128))
            square_s[s, 1] = jnp.broadcast_to(right, (16, 128))
            self.square = remote(square_s.at[s, 0], square_in.at[s], qs.at[s], qr.at[s], peer)
            self.square.start()

        def norm(self):
            s = self.s
            self.square.wait_recv()
            rows = rows_s[s]
            mean_q = (square_s[s, 0] + square_in[s])[:, 0:1] * (1.0 / QL)
            mean_kv = square_s[s, 1][:, 0:1] * (1.0 / KL)
            scale_q, scale_kv = lax.rsqrt(mean_q + EPS), lax.rsqrt(mean_kv + EPS)
            gain = gain_s[pl.ds(c, 1), :]
            at = pl.ds(pl.multiple_of(256 * s + 16 * chip, 16), 16)
            turn = rope_tile(rows[:, cut_q:], cos_s[at, :], sin_s[at, :])
            lane = lax.broadcasted_iota(jnp.int32, turn.shape, 1)
            zb[s, c, x, y, :, 0:512] = (rows[:, :512] * scale_q * gain[:, :512]).astype(BF16)
            both = jnp.where(c == 0, scale_q, scale_kv)
            zb[s, c, x, y, :, 512:cut_q] = (rows[:, 512:cut_q] * both * gain[:, 512:cut_q]).astype(BF16)
            zb[s, c, x, y, :, cut_q:] = jnp.where(lane < RD, turn, 0.0).astype(BF16)

        def gather_one(self):
            s = self.s
            self.one = []
            for d in (1, 3, 2):
                self.one.append(push(zb.at[s, c, x, y, :, ka], along_x(d)))
                self.one.append(push(zb.at[s, c, x, y, :, kb], along_y(d)))

        def gather_two(self):
            s = self.s
            self.two_a, self.two_b = [], []
            for copy in self.one:
                copy.wait_recv()
            for d in (1, 3, 2):
                self.two_a.append(push(zb.at[s, c, :, y, :, ka], along_y(d)))
                self.two_b.append(push(zb.at[s, c, x, :, :, kb], along_x(d)))

        def gather_mate(self):
            for copy in self.two_a:
                copy.wait_recv()
            self.mates = [push(zb.at[self.s, c, :, :, :, ka], peer)]
            for copy in self.two_b:
                copy.wait_recv()
            self.mates.append(push(zb.at[self.s, c, :, :, :, kb], peer))

        def gather_end(self):
            for copy in self.mates:
                copy.wait_recv()

        def close(self):
            for copy in self.core[0] + self.core[1] + self.direct + [self.square]:
                copy.wait_send()
            for ring in self.rings:
                ring.close()

    f0, f1 = Front(0), Front(1)
    product(0)
    greet_wait()
    f0.swap()
    xd_all[z] = xd_ref[...]

    def send_z(step, carry):
        zz, _, device = z_peer(step)
        remote(xd_ref, xd_all.at[zz], zs.at[step], zr.at[step], device).start()
        return carry

    lax.fori_loop(1, 8, send_z, 0)
    product(1)
    f0.far()
    f0.near()
    f1.swap()

    def wait_z(step, carry):
        zz, other, device = z_peer(step)
        remote(xd_ref, xd_all.at[zz], zs.at[step], zr.at[step], device).wait()
        return carry

    lax.fori_loop(1, 8, wait_z, 0)
    ii = lax.broadcasted_iota(jnp.int32, (16, 128), 0)
    jj = lax.broadcasted_iota(jnp.int32, (16, 128), 1)
    docs = docs_ref[...].reshape(1, 128)
    sel_in = jnp.where(docs == z * 16 + ii, 1.0, 0.0).astype(BF16)
    asked = jnp.dot(sel_in, xd_all[...].reshape(128, -1), preferred_element_type=F32).astype(BF16)
    for w_ref, lo, wide in ((wqa_ref, 0, QL), (wkv_s, QL, W - QL)):
        val = jnp.dot(asked, w_ref[...], preferred_element_type=F32)
        dec[:, :, lo : lo + wide] = val.reshape(2, 8, wide)
    dec_core = remote(dec.at[1 - c], dec_in, ds.at[0], dr.at[0], peer)
    dec_core.start()
    f1.far()
    f0.pass_on()
    f1.near()

    q_gain, kv_gain = qg_ref[...].reshape(1, QL), kvg_ref[...].reshape(1, KL)
    gain_s[...] = jnp.zeros_like(gain_s)
    gain_s[0:1, :cut_q] = q_gain[:, :cut_q]
    gain_s[1:2, : QL - cut_q] = q_gain[:, cut_q:]
    gain_s[1:2, QL - cut_q : cut_q] = kv_gain
    lens = len_ref[pl.ds(z, 1), :].astype(F32)
    i16 = lax.broadcasted_iota(jnp.int32, (16, 16), 0)
    j16 = lax.broadcasted_iota(jnp.int32, (16, 16), 1)
    spread = jnp.broadcast_to(lens, (16, 16))
    len_col = jnp.sum(jnp.where(i16 == j16, spread, 0.0), axis=1, keepdims=True)
    end_col = jnp.sum(jnp.where(j16 <= i16, spread, 0.0), axis=1, keepdims=True)
    end_row = jnp.sum(jnp.where(i16 <= j16, jnp.broadcast_to(len_col, (16, 16)), 0.0), axis=0, keepdims=True)
    token = lax.broadcasted_iota(jnp.int32, (512, 16), 0).astype(F32)
    begun = jnp.sum(jnp.where(token >= end_row, jnp.broadcast_to(lens, (512, 16)), 0.0), axis=1, keepdims=True)
    pos = lax.broadcasted_iota(jnp.int32, (512, 128), 0).astype(F32) - begun
    pos_s[...] = pos
    freq = freq_ref[...]
    for i in range(4):
        part = pl.ds(128 * i, 128)
        cos_s[part, :], sin_s[part, :] = turn_tables(pos_s[part, :], freq)
    cosd, sind = turn_tables(jnp.broadcast_to(len_col, (16, 128)), freq)

    dec_core.wait()
    mine = dec[c] + dec_in[...]
    for j in range(16):
        tiles[j, :, 0:128] = mine[:, 128 * j : 128 * j + 128]
        tiles[j, :, 128:256] = mine[:, QL + KL :]

    def send_tile(step, carry):
        other, device = chip_peer(x, y, c, step)
        remote(tiles.at[other], tiles_in.at[chip], es.at[step], er.at[step], device).start()
        return carry

    lax.fori_loop(1, 16, send_tile, 0)
    tiles_in[chip] = tiles[chip]

    f0.second()
    f1.pass_on()

    def turn_wo(k, carry):
        cut = pl.multiple_of(k * 896, 128)
        wot[pl.ds(cut, 896), :] = wo[:, pl.ds(cut, 896)].T
        return carry

    def wait_tile(step, carry):
        other, device = chip_peer(x, y, c, step)
        remote(tiles.at[other], tiles_in.at[chip], es.at[step], er.at[step], device).wait()
        return carry

    lax.fori_loop(1, 16, wait_tile, 0)
    total = jnp.sum(tiles_in[...], axis=0)
    sums_in[chip] = total[:, :128]

    def send_sum(step, carry):
        other, device = chip_peer(x, y, c, step)
        remote(sums_in.at[chip], sums_in.at[chip], gs.at[step], gr.at[step], device).start()
        return carry

    lax.fori_loop(1, 16, send_sum, 0)
    f0.rows()
    f1.second()
    f0.norm()
    f0.gather_one()

    loads[0].wait()
    lax.fori_loop(0, 3, turn_wo, 0)
    f0.gather_two()
    f1.rows()

    def wait_sum(step, carry):
        other, device = chip_peer(x, y, c, step)
        remote(sums_in.at[chip], sums_in.at[chip], gs.at[step], gr.at[step], device).wait()
        return carry

    lax.fori_loop(1, 16, wait_sum, 0)
    for j in range(16):
        rows_in[c, :, 128 * j : 128 * j + 128] = sums_in[j]
    rows_in[c, :, QL + KL : W] = total[:, 128:]
    dec_mate = remote(rows_in.at[c], rows_in.at[c], ms.at[0], mr.at[0], peer)
    dec_mate.start()
    f1.norm()
    f1.gather_one()
    dec_mate.wait()
    q, kv, turn = latent_rows(rows_in[...].reshape(16, W), q_gain, kv_gain, cosd, sind)
    zd[:, 0:QL] = q.astype(BF16)
    zd[:, QL : QL + KL] = kv.astype(BF16)
    zd[:, QL + KL : W] = turn.astype(BF16)
    heads = 4
    scale = 1.0 / float(NOPE + RD) ** 0.5
    wide = NOPE + VD
    for load in loads[1:]:
        load.wait()
    query = jnp.dot(zd[:, :QL], wqb[...], preferred_element_type=F32)
    dec_nope, dec_rope = split_query(query, cosd, sind)
    for h in range(heads):
        up_k = wkvb[:, wide * h : wide * h + NOPE]
        qabs_s[h] = lax.dot_general(dec_nope[h], up_k, NT, preferred_element_type=F32).astype(BF16)
        if h % 2:
            qrope_s[h] = pltpu.roll(dec_rope[h // 2].astype(F32), 64, 1).astype(BF16)
        else:
            qrope_s[h] = dec_rope[h // 2]
    lax.fori_loop(3, 8, turn_wo, 0)
    f0.gather_mate()
    f1.gather_two()
    f0.gather_end()

    def project(s):
        rows = slice(256 * s, 256 * s + 256)
        latent = zb[s, 1, :, :, :, QL - cut_q : cut_q].reshape(256, KL)
        kv_s[rows, :] = jnp.dot(latent, wkvb[...], preferred_element_type=F32).astype(BF16)
        turn = zb[s, 1, :, :, :, cut_q:].reshape(256, 128)
        turn_s[0, rows, :] = turn
        turn_s[1, rows, :] = pltpu.roll(turn.astype(F32), 64, 1).astype(BF16)

    def block(s):
        for j in range(2):
            first = 256 * s + 128 * j
            begin = max(first - 128, 0)
            rows, keys = slice(first, first + 128), slice(begin, begin + 256)
            chips = slice(2 * j, 2 * j + 2)
            query = jnp.dot(
                zb[s, 0, chips, :, :, :cut_q].reshape(128, cut_q), wqb[:cut_q, :], preferred_element_type=F32
            )
            query = query + jnp.dot(
                zb[s, 1, chips, :, :, : QL - cut_q].reshape(128, QL - cut_q), wqb[cut_q:, :], preferred_element_type=F32
            )
            nope, rope = split_query(query, cos_s[rows, :], sin_s[rows, :])
            own = first + lax.broadcasted_iota(jnp.int32, (128, 256), 0)
            other = begin + lax.broadcasted_iota(jnp.int32, (128, 256), 1)
            back = (own - other).astype(F32)
            keep = (back >= 0) & (back <= jnp.concatenate([pos_s[rows, :]] * 2, axis=1))
            scores = []
            for h in range(heads):
                q = jnp.concatenate([nope[h], rope[h // 2]], axis=1)
                k = jnp.concatenate([kv_s[keys, wide * h : wide * h + NOPE], turn_s[h % 2, keys, :]], axis=1)
                scores.append(lax.dot_general(q, k, NT, preferred_element_type=F32))
            scores = jnp.concatenate(scores, axis=0) * scale
            scores = jnp.where(jnp.concatenate([keep] * heads, axis=0), scores, -1e30)
            e = jnp.exp(scores - jnp.max(scores, axis=-1, keepdims=True))
            p = (e * (1.0 / jnp.sum(e, axis=-1, keepdims=True))).astype(BF16)
            for h in range(heads):
                v = kv_s[keys, wide * h + NOPE : wide * h + wide]
                o = jnp.dot(p[128 * h : 128 * h + 128], v, preferred_element_type=F32)
                o_s[rows, VD * h : VD * h + VD] = o.astype(BF16)

    def decode():
        latent, own_lat = zb[:, 1, :, :, :, QL - cut_q : cut_q].reshape(512, KL), zd[:, QL : QL + KL]
        own_turn = zd[:, QL + KL : W]
        at = lax.broadcasted_iota(jnp.int32, (16, 512), 1).astype(F32)
        keep = (at < end_col) & (at >= end_col - len_col)
        keep = jnp.concatenate([keep] * heads, axis=0)
        diag = jnp.concatenate([i16 == j16] * heads, axis=0)
        q_abs, q_rope = qabs_s[...].reshape(16 * heads, KL), qrope_s[...].reshape(16 * heads, 128)
        s = lax.dot_general(q_abs, latent, NT, preferred_element_type=F32)
        s = (s + lax.dot_general(q_rope, turn_s[0], NT, preferred_element_type=F32)) * scale
        s = jnp.where(keep, s, -1e30)
        t = lax.dot_general(q_abs, own_lat, NT, preferred_element_type=F32)
        t = (t + lax.dot_general(q_rope, own_turn, NT, preferred_element_type=F32)) * scale
        t = jnp.where(diag, t, -1e30)
        top = jnp.maximum(jnp.max(s, axis=-1, keepdims=True), jnp.max(t, axis=-1, keepdims=True))
        e, f = jnp.exp(s - top), jnp.exp(t - top)
        part = 1.0 / (jnp.sum(e, axis=-1, keepdims=True) + jnp.sum(f, axis=-1, keepdims=True))
        lat = jnp.dot((e * part).astype(BF16), latent, preferred_element_type=F32)
        lat = (lat + jnp.dot((f * part).astype(BF16), own_lat, preferred_element_type=F32)).astype(BF16)
        for h in range(heads):
            up_v = wkvb[:, wide * h + NOPE : wide * h + wide]
            o = jnp.dot(lat[16 * h : 16 * h + 16], up_v, preferred_element_type=F32)
            od_s[:, VD * h : VD * h + VD] = o.astype(BF16)

    def decode_out():
        for k in range(8):
            val = jnp.dot(od_s[...], wo[:, 896 * k : 896 * k + 896], preferred_element_type=F32)
            for j in range(4):
                at = 224 * j // 128 * 128
                if at + 384 <= 896:
                    v = val[:, at : at + 384]
                else:
                    v = jnp.concatenate([val[:, at:896], val[:, : at + 384 - 896]], axis=1)
                if 224 * j - at:
                    v = pltpu.roll(v, 384 - (224 * j - at), 1)
                dt[j % 2, 2 * k + j // 2] = v[:, :256].astype(BF16)

    def output(s):
        far_x, far_y = next_of(x, 2), next_of(y, 2) // 2

        def part(n):
            if n < 2:
                k = 2 * far_x + n
            elif n < 5:
                k = 2 * next_of(far_x, n - 1) + far_y
            else:
                k = 2 * next_of(far_x, n - 4) + 1 - far_y
            xx, yy = k // 2, 2 * lax.rem(k, 2)
            w = wot[pl.ds(pl.multiple_of(k * 896, 128), 896), :]
            val = lax.dot_general(w, o_s[256 * s : 256 * s + 256, :], NT, preferred_element_type=F32).astype(BF16)
            for j in range(4):
                t0[s, j % 2, xx, yy + j // 2] = val[224 * j : 224 * j + 112]
                t1[s, j % 2, yy + j // 2, xx] = val[224 * j + 112 : 224 * j + 224]

        return part

    half = (slice(0, 128), slice(128, 256))

    class Stage:
        def __init__(self, s):
            self.s = s
            self.core = ([], [])
            self.rings = (
                Ring(t0.at[s, c], tnear0.at[s], tfar0.at[s], half, x, xp, xm, us, ur, 18 * s),
                Ring(t1.at[s, c], tnear1.at[s], tfar1.at[s], half, y, yp, ym, us, ur, 18 * s + 6),
            )
            self.lasts = [
                (tq0, tqin0, y, lambda d: tp_of(x, next_of(y, d), c)),
                (tq1, tqin1, x, lambda d: tp_of(next_of(x, d), y, c)),
            ]
            self.direct = ([], [])
            self.parts = ((t0, tc0, x, self.core[0]), (t1, tc1, y, self.core[1]))

        def swap(self, which):
            for i in which:
                d = order[i]
                for n, (t, came, pos_t, list_t) in enumerate(self.parts):
                    k, m = next_of(pos_t, d), 8 * self.s + 2 * i + n
                    copy = remote(t.at[self.s, 1 - c, k], came.at[self.s, k], vs.at[m], vr.at[m], peer)
                    copy.start()
                    list_t.append(copy)

        def take(self, i):
            for t, came, pos_t, list_t in self.parts:
                list_t[i].wait_recv()
                k = next_of(pos_t, order[i])
                t[self.s, c, k] = (t[self.s, c, k].astype(F32) + came[self.s, k].astype(F32)).astype(BF16)

        def first(self):
            self.take(0)
            for ring in self.rings:
                ring.start_far()
            self.take(1)
            self.take(2)
            for ring in self.rings:
                ring.start_near()
            self.take(3)

        def pass_on(self):
            for ring in self.rings:
                ring.pass_on()

        def second(self):
            for side in range(2):
                tq0[self.s, :, :, half[side]] = self.rings[0].result(side).astype(BF16)
                tq1[self.s, :, :, half[side]] = self.rings[1].result(side).astype(BF16)
            for d in (2, 1, 3):
                for h, (data, box, pos_q, dev) in enumerate(self.lasts):
                    n = 18 * self.s + 12 + 3 * h + d - 1
                    copy = remote(
                        data.at[self.s, next_of(pos_q, d)], box.at[self.s, d - 1], us.at[n], ur.at[n], {"tp": dev(d)}
                    )
                    copy.start()
                    self.direct[h].append(copy)

        def finish(self):
            for h, (data, box, pos_q, dev) in enumerate(self.lasts):
                for copy in self.direct[h]:
                    copy.wait_recv()
                came = [box[self.s, i].astype(F32) for i in range(3)]
                total = data[self.s, pos_q].astype(F32) + (came[0] + came[1]) + came[2]
                out_ref[112 * h : 112 * h + 112, 256 * self.s : 256 * self.s + 256] = total.astype(BF16)

        def close(self):
            for copy in self.core[0] + self.core[1]:
                copy.wait_send()
            for ring in self.rings:
                ring.close()
            for copy in self.direct[0] + self.direct[1]:
                copy.wait_send()

    s0, s1 = Stage(0), Stage(1)

    def produce(stage):
        part = output(stage.s)
        for n in range(5):
            part(n)
        stage.swap((0,))
        for n in range(5, 8):
            part(n)
        stage.swap((1, 2, 3))

    project(0)
    block(0)
    f1.gather_mate()
    produce(s0)
    s0.first()
    f1.gather_end()
    project(1)
    block(1)
    decode()
    decode_out()
    dec_swap = remote(dt.at[1 - c], dc, fs.at[0], fr.at[0], peer)
    dec_swap.start()
    s0.pass_on()
    produce(s1)
    s1.first()
    dec_swap.wait()
    dt[c] = (dt[c].astype(F32) + dc[...].astype(F32)).astype(BF16)

    def send_out(step, carry):
        other, device = chip_peer(x, y, c, step)
        remote(dt.at[c, other], dn.at[chip], hs.at[step], hr.at[step], device).start()
        return carry

    lax.fori_loop(1, 16, send_out, 0)
    dn[chip] = dt[c, chip]
    s0.second()

    def wait_out(step, carry):
        other, device = chip_peer(x, y, c, step)
        remote(dt.at[c, other], dn.at[chip], hs.at[step], hr.at[step], device).wait()
        return carry

    lax.fori_loop(1, 16, wait_out, 0)
    dz[z] = jnp.sum(dn[...].astype(F32), axis=0).astype(BF16)

    def send_back(step, carry):
        zz, _, device = z_peer(step)
        remote(dz.at[zz], dz.at[zz], ys.at[step], yr.at[step], device).start()
        return carry

    lax.fori_loop(1, 8, send_back, 0)
    s1.pass_on()
    s0.finish()

    def wait_back(step, carry):
        zz, _, device = z_peer(step)
        remote(dz.at[zz], dz.at[zz], ys.at[step], yr.at[step], device).wait()
        return carry

    lax.fori_loop(1, 8, wait_back, 0)
    wanted = jnp.sum(jnp.where(jj == z * 16 + ii, docs, 0).astype(F32), axis=1, keepdims=True)
    sel_out = jnp.where(jj.astype(F32) == wanted, 1.0, 0.0).astype(BF16)
    picked = jnp.dot(sel_out, dz[...].reshape(128, 256), preferred_element_type=F32)
    outd_ref[...] = picked[:, :224].astype(BF16)
    s1.second()
    s1.finish()
    for copy in copies:
        copy.wait_send()
    f0.close()
    f1.close()
    s0.close()
    s1.close()


def whole(xt, xd, wq_a, wkv_a, q_gain, kv_gain, freq, doc_len, docs, wq_b, wkv_b, wo):
    vm = pl.BlockSpec(memory_space=pltpu.VMEM)
    hbm = pl.BlockSpec(memory_space=pl.ANY)
    dma = pltpu.SemaphoreType.DMA
    shapes = [
        (wq_b.shape, BF16), (wkv_b.shape, BF16), (wo.shape, BF16), (wo.shape[::-1], BF16),
        ((wq_a.shape[0], W - QL), BF16),
        ((2, 2, 4, 4, 8, HALF), F32), ((2, 2, 4, 4, 8, HALF), F32),
        ((2, 4, 4, 8, HALF), F32), ((2, 4, 4, 8, HALF), F32),
        ((2, 2, 4, 8, HALF), F32), ((2, 2, 4, 8, HALF), F32),
        ((2, 4, 8, HALF), F32), ((2, 4, 8, HALF), F32),
        ((2, 4, 8, HALF), F32), ((2, 4, 8, HALF), F32),
        ((2, 3, 8, HALF), F32), ((2, 3, 8, HALF), F32),
        ((8,) + xd.shape, BF16), ((2, 8, W), F32), ((8, W), F32),
        ((16, 8, 256), F32), ((16, 8, 256), F32), ((16, 8, 128), F32), ((2, 8, W), F32),
        ((2, 16, HALF), F32), ((2, 2, 16, 128), F32), ((2, 16, 128), F32), ((8, HALF), F32),
        ((2, 2, NX, NY, 16, HALF), BF16), ((16, W), BF16), ((4, 16, KL), BF16), ((4, 16, 128), BF16), ((512, 128), F32), ((512, 128), F32), ((512, 128), F32),
        ((512, wkv_b.shape[1]), BF16), ((2, 512, 128), BF16), ((512, 512), BF16), ((16, 512), BF16),
        ((2, 2, 4, 4, 112, 256), BF16), ((2, 2, 4, 4, 112, 256), BF16),
        ((2, 4, 4, 112, 256), BF16), ((2, 4, 4, 112, 256), BF16),
        ((2, 2, 4, 112, 256), BF16), ((2, 2, 4, 112, 256), BF16),
        ((2, 4, 112, 256), BF16), ((2, 4, 112, 256), BF16),
        ((2, 4, 112, 256), BF16), ((2, 4, 112, 256), BF16),
        ((2, 3, 112, 256), BF16), ((2, 3, 112, 256), BF16),
        ((2, 16, 16, 256), BF16), ((16, 16, 256), BF16), ((16, 16, 256), BF16),
        ((8, 16, 256), BF16),
    ]
    counts = (3, 8, 8, 16, 16, 36, 36, 1, 1, 16, 16, 16, 16, 28, 28, 1, 1, 36, 36, 16, 16, 1, 1, 16, 16, 8, 8, 2, 2)
    return pl.pallas_call(
        whole_kernel,
        out_shape=(jax.ShapeDtypeStruct((224, 512), BF16), jax.ShapeDtypeStruct((16, 224), BF16)),
        in_specs=[vm] * 9 + [hbm] * 3,
        out_specs=(vm, vm),
        scratch_shapes=[pltpu.VMEM(shape, kind) for shape, kind in shapes] + [dma((n,)) for n in counts],
        compiler_params=pltpu.CompilerParams(
            collective_id=0, has_side_effects=True, vmem_limit_bytes=VMEM_LIMIT
        ),
        name="whole",
    )(xt, xd, wq_a, wkv_a, q_gain, kv_gain, freq, doc_len, docs, wq_b, wkv_b, wo)


def hand_over_kernel(a_ref, b_ref, out_ref, outd_ref):
    out_ref[...] = a_ref[...]
    outd_ref[...] = b_ref[...]


def hand_over(a, b):
    vm = pl.BlockSpec(memory_space=pltpu.VMEM)
    return pl.pallas_call(
        hand_over_kernel,
        out_shape=(jax.ShapeDtypeStruct(a.shape, a.dtype), jax.ShapeDtypeStruct(b.shape, b.dtype)),
        in_specs=[vm, vm],
        out_specs=(vm, vm),
        name="hand_over",
    )(a, b)


def per_device(x_pre, x_dec, wq_a, wkv_a, q_gain, kv_gain, wq_b, wkv_b, wo, doc_len, request_docs):
    half = RD // 2
    freq = np.tile(10000.0 ** (-np.arange(half) / half), 4).astype(np.float32)[None, :]
    out_t, out_dec = whole(
        x_pre.T, x_dec, wq_a, wkv_a, q_gain, kv_gain, jnp.asarray(freq), doc_len, request_docs, wq_b, wkv_b, wo
    )
    out_t, out_dec = hand_over(out_t, out_dec)
    return out_t.T, out_dec


def solution(mesh):
    placed = (
        P(("role", "grp"), "tp"),
        P(("role", "grp"), "tp"),
        P("tp", None),
        P("tp", None),
        P(),
        P(),
        P(None, "tp"),
        P(None, "tp"),
        P("tp", None),
        P(),
        P(),
    )
    return jax.shard_map(
        per_device,
        mesh=mesh,
        in_specs=placed,
        out_specs=(P(("role", "grp"), "tp"), P(("role", "grp"), "tp")),
        check_vma=False,
    )
```

```python
import jax
import jax.numpy as jnp
import numpy as np
from jax import lax
from jax.experimental import pallas as pl
from jax.experimental.pallas import tpu as pltpu
from jax.sharding import PartitionSpec as P

QL = 1536
KL = 512
RD = 64
NOPE = 128
VD = 128
NX = 4
NY = 4
W = QL + KL + 128
HALF = 1152
SPLIT = 640
EPS = 1e-06
F32 = jnp.float32
BF16 = jnp.bfloat16
MESH = pl.DeviceIdType.MESH
VMEM_LIMIT = 58 * 2**20


def place():
    tp = lax.axis_index("tp")
    return tp, tp // 8, lax.rem(tp // 2, NY), lax.rem(tp, 2)


def tp_of(x, y, c):
    return x * 8 + y * 2 + c


def next_of(p, step):
    return lax.rem(p + step + 4, 4)


def z_peer(step):
    z = lax.axis_index("role") * 2 + lax.axis_index("grp")
    other = lax.rem(z + step, 8)
    return z, other, {"role": other // 2, "grp": lax.rem(other, 2)}


def remote(src, dst, send, recv, device):
    return pltpu.make_async_remote_copy(
        src_ref=src, dst_ref=dst, send_sem=send, recv_sem=recv, device_id=device, device_id_type=MESH
    )


def chip_peer(x, y, c, step):
    other = lax.rem(x * 4 + y + step, 16)
    return other, {"tp": tp_of(other // 4, lax.rem(other, 4), c)}


def greet_start(x, y, c):
    barrier = pltpu.get_barrier_semaphore()
    pl.semaphore_signal(barrier, inc=1, device_id={"tp": tp_of(x, y, 1 - c)}, device_id_type=MESH)

    def chips(step, carry):
        _, device = chip_peer(x, y, c, step)
        pl.semaphore_signal(barrier, inc=1, device_id=device, device_id_type=MESH)
        return carry

    lax.fori_loop(1, 16, chips, 0)

    def planes(step, carry):
        _, _, device = z_peer(step)
        pl.semaphore_signal(barrier, inc=1, device_id=device, device_id_type=MESH)
        return carry

    lax.fori_loop(1, 8, planes, 0)


def greet_wait():
    pl.semaphore_wait(pltpu.get_barrier_semaphore(), 1 + 15 + 7)


class Ring:
    def __init__(self, data, near, far, part, pos, plus, minus, send, recv, base, sign=1):
        self.data, self.near, self.far, self.part = data, near, far, part
        self.pos, self.plus, self.minus = pos, plus, minus
        self.send, self.recv, self.base = send, recv, base
        self.sign = sign
        self.copies = {}

    def cut(self, ref, side):
        return ref.at[(Ellipsis, self.part[side])]

    def go(self, key, number, src, dst, device):
        copy = remote(src, dst, self.send.at[self.base + number], self.recv.at[self.base + number], device)
        copy.start()
        self.copies[key] = copy

    def start_far(self):
        chunk = self.data.at[next_of(self.pos, 2)]
        self.go("far0", 0, self.cut(chunk, 0), self.cut(self.far, 0), self.plus)
        self.go("far1", 1, self.cut(chunk, 1), self.cut(self.far, 1), self.minus)

    def start_near(self):
        up, down = self.data.at[next_of(self.pos, self.sign)], self.data.at[next_of(self.pos, -self.sign)]
        self.go("up1", 2, self.cut(up, 1), self.cut(self.near.at[0], 1), self.plus)
        self.go("down0", 3, self.cut(down, 0), self.cut(self.near.at[1], 0), self.minus)

    def add(self, chunk, side):
        ref, extra = self.cut(chunk, side), self.cut(self.far, side)
        ref[...] = (ref[...].astype(F32) + extra[...].astype(F32)).astype(ref.dtype)

    def pass_on(self):
        up, down = self.data.at[next_of(self.pos, self.sign)], self.data.at[next_of(self.pos, -self.sign)]
        self.copies["far0"].wait_recv()
        self.add(up, 0)
        self.go("up0", 4, self.cut(up, 0), self.cut(self.near.at[0], 0), self.plus)
        self.copies["far1"].wait_recv()
        self.add(down, 1)
        self.go("down1", 5, self.cut(down, 1), self.cut(self.near.at[1], 1), self.minus)

    def result(self, side):
        for key in ("up%d" % side, "down%d" % side):
            self.copies[key].wait_recv()
        own = self.cut(self.data.at[self.pos], side)[...].astype(F32)
        left = self.cut(self.near.at[0], side)[...].astype(F32)
        right = self.cut(self.near.at[1], side)[...].astype(F32)
        return own + (left + right)

    def close(self):
        for copy in self.copies.values():
            copy.wait_send()


def latent_rows(rows, q_gain, kv_gain, cosine, sine):
    q = rows[:, :QL]
    kv = rows[:, QL : QL + KL]
    turn = rows[:, QL + KL :]
    q = q * lax.rsqrt(jnp.mean(q * q, axis=-1, keepdims=True) + EPS) * q_gain
    kv = kv * lax.rsqrt(jnp.mean(kv * kv, axis=-1, keepdims=True) + EPS) * kv_gain
    turn = rope_tile(turn, cosine, sine)
    lane = lax.broadcasted_iota(jnp.int32, turn.shape, 1)
    turn = jnp.where(lane < RD, turn, 0.0)
    return q, kv, turn


def rope_tile(tile, cosine, sine):
    lane = lax.broadcasted_iota(jnp.int32, tile.shape, 1)
    swapped = jnp.where(lane % RD < RD // 2, pltpu.roll(tile, 96, 1), pltpu.roll(tile, 32, 1))
    return tile * cosine + swapped * sine


def turn_tables(pos, freq):
    turn = pos * freq
    lane = lax.broadcasted_iota(jnp.int32, turn.shape, 1)
    sine = jnp.sin(turn)
    return jnp.cos(turn), jnp.where(lane % RD < RD // 2, -sine, sine)


NT = (((1,), (1,)), ((), ()))
TN = (((0,), (0,)), ((), ()))


def split_query(query, cosine, sine):
    nope, rope = [], []
    lane = lax.broadcasted_iota(jnp.int32, (query.shape[0], 128), 1)
    for pair in range(query.shape[1] // 384):
        t0, t1, t2 = [query[:, 384 * pair + 128 * i : 384 * pair + 128 * i + 128] for i in range(3)]
        nope.append(t0.astype(BF16))
        nope.append(jnp.where(lane < 64, pltpu.roll(t1, 64, 1), pltpu.roll(t2, 64, 1)).astype(BF16))
        rope.append(rope_tile(jnp.where(lane < 64, t1, t2), cosine, sine).astype(BF16))
    return nope, rope


def whole_kernel(
    xt_hbm, xd_ref, wqa_hbm, wkva_hbm, qg_ref, kvg_ref, freq_ref, len_ref, docs_ref, wqb_hbm, wkvb_hbm, wo_hbm,
    out_ref, outd_ref, xt_ref, wqa_ref, wkva_ref,
    wqb, wkvb, wo, wot, wkv_s, p0, p1, c0, c1, near0, near1, far0, far1, q0, q1, in0, in1,
    xd_all, dec, dec_in, tiles, tiles_in, sums_in, rows_in,
    rows_s, square_s, square_in, gain_s,
    zb, zd, qabs_s, qrope_s, pos_s, cos_s, sin_s, kv_s, turn_s, o_s, od_s,
    t0, t1, tc0, tc1, tnear0, tnear1, tfar0, tfar1, tq0, tq1, tqin0, tqin1,
    dt, dc, dn, dz,
    ws, zs, zr, cs, cr, rs, rr, ds, dr, es, er, gs, gr, ks, kr, ms, mr,
    us, ur, vs, vr, fs, fr, hs, hr, ys, yr, qs, qr,
):
    tp, x, y, c = place()
    chip = x * 4 + y
    z, _, _ = z_peer(0)
    peer = {"tp": tp_of(x, y, 1 - c)}
    xp, xm = {"tp": tp_of(next_of(x, 1), y, c)}, {"tp": tp_of(next_of(x, -1), y, c)}
    yp, ym = {"tp": tp_of(x, next_of(y, 1), c)}, {"tp": tp_of(x, next_of(y, -1), c)}
    greet_start(x, y, c)
    loads = [
        pltpu.make_async_copy(src, dst, ws.at[i])
        for i, (src, dst) in enumerate(
            (
                (wo_hbm, wo), (wkvb_hbm, wkvb), (wqb_hbm, wqb),
                (xt_hbm, xt_ref), (wqa_hbm, wqa_ref), (wkva_hbm, wkva_ref),
            )
        )
    ]
    for load in loads[3:]:
        load.start()
    for load in loads[3:]:
        load.wait()

    wkv_s[...] = jnp.zeros_like(wkv_s)
    wkv_s[:, : KL + RD] = wkva_ref[...]
    order = (2, 1, 3, 0)
    cut_q = 1024
    sign = 1 - 2 * c

    def product(s):
        rows = xt_ref[:, 256 * s : 256 * s + 256]
        for cc, w, lo in (
            (0, wqa_ref[:, :cut_q], 0),
            (1, wqa_ref[:, cut_q:], 0),
            (1, wkv_s[...], QL - cut_q),
        ):
            wide = w.shape[1]
            val = lax.dot_general(rows, w, TN, preferred_element_type=F32).reshape(NX, NY, 2, 8, wide)
            p0[s, cc, :, :, :, lo : lo + wide] = val[:, :, 0]
            for yy in range(NY):
                p1[s, cc, yy, :, :, lo : lo + wide] = val[:, yy, 1]
        p0[s, 0, :, :, :, cut_q:] = jnp.zeros((NX, NY, 8, HALF - cut_q), F32)
        p1[s, 0, :, :, :, cut_q:] = jnp.zeros((NX, NY, 8, HALF - cut_q), F32)

    lanes = (slice(0, SPLIT), slice(SPLIT, HALF))
    ka, kb = lanes
    copies = []

    def push(block, device):
        n = len(copies)
        copy = remote(block, block, ks.at[n], kr.at[n], device)
        copy.start()
        copies.append(copy)
        return copy

    def along_x(d):
        return {"tp": tp_of(next_of(x, d), y, c)}

    def along_y(d):
        return {"tp": tp_of(x, next_of(y, d), c)}

    class Front:
        def __init__(self, s):
            self.s = s
            self.core = ([], [])
            self.parts = ((p0, c0, x, self.core[0]), (p1, c1, y, self.core[1]))
            self.rings = (
                Ring(
                    p0.at[s, c], near0.at[s], far0.at[s], lanes, x, along_x(sign), along_x(-sign), rs, rr, 18 * s, sign
                ),
                Ring(
                    p1.at[s, c], near1.at[s], far1.at[s], lanes, y, along_y(sign), along_y(-sign), rs, rr, 18 * s + 6,
                    sign,
                ),
            )
            self.direct = []

        def swap(self):
            for i, d in enumerate(order):
                for h, (p, came, pos_p, list_p) in enumerate(self.parts):
                    k, n = next_of(pos_p, d), 8 * self.s + 2 * i + h
                    copy = remote(p.at[self.s, 1 - c, k], came.at[self.s, k], cs.at[n], cr.at[n], peer)
                    copy.start()
                    list_p.append(copy)

        def take(self, i, h):
            p, came, pos_p, list_p = self.parts[h]
            list_p[i].wait_recv()
            k = next_of(pos_p, order[i])
            p[self.s, c, k] = p[self.s, c, k] + came[self.s, k]

        def far(self):
            for h in range(2):
                self.take(0, h)
                self.rings[h].start_far()

        def near(self):
            for h in range(2):
                self.take(1, h)
                self.take(2, h)
                self.rings[h].start_near()
            for h in range(2):
                self.take(3, h)

        def pass_on(self):
            for ring in self.rings:
                ring.pass_on()

        def second(self):
            for h, (q, box, pos_h, dev) in enumerate(((q0, in0, y, along_y), (q1, in1, x, along_x))):
                for side in range(2):
                    q[self.s, :, :, lanes[side]] = self.rings[h].result(side)
                for d in (2, 1, 3):
                    n = 18 * self.s + 12 + 3 * h + d - 1
                    copy = remote(
                        q.at[self.s, next_of(pos_h, d)], box.at[self.s, d - 1], rs.at[n], rr.at[n], dev(d)
                    )
                    copy.start()
                    self.direct.append(copy)

        def rows(self):
            for copy in self.direct:
                copy.wait_recv()
            s = self.s
            top = q0[s, y] + (in0[s, 0] + in0[s, 1]) + in0[s, 2]
            low = q1[s, x] + (in1[s, 0] + in1[s, 1]) + in1[s, 2]
            rows = jnp.concatenate([top, low], axis=0)
            rows_s[s] = rows
            left = jnp.sum(rows[:, :512] * rows[:, :512], axis=-1, keepdims=True)
            right = jnp.sum(rows[:, 512:cut_q] * rows[:, 512:cut_q], axis=-1, keepdims=True)
            square_s[s, 0] = jnp.broadcast_to(left + jnp.where(c == 0, right, 0.0), (16, 128))
            square_s[s, 1] = jnp.broadcast_to(right, (16, 128))
            self.square = remote(square_s.at[s, 0], square_in.at[s], qs.at[s], qr.at[s], peer)
            self.square.start()

        def norm(self):
            s = self.s
            self.square.wait_recv()
            rows = rows_s[s]
            mean_q = (square_s[s, 0] + square_in[s])[:, 0:1] * (1.0 / QL)
            mean_kv = square_s[s, 1][:, 0:1] * (1.0 / KL)
            scale_q, scale_kv = lax.rsqrt(mean_q + EPS), lax.rsqrt(mean_kv + EPS)
            gain = gain_s[pl.ds(c, 1), :]
            at = pl.ds(pl.multiple_of(256 * s + 16 * chip, 16), 16)
            turn = rope_tile(rows[:, cut_q:], cos_s[at, :], sin_s[at, :])
            lane = lax.broadcasted_iota(jnp.int32, turn.shape, 1)
            zb[s, c, x, y, :, 0:512] = (rows[:, :512] * scale_q * gain[:, :512]).astype(BF16)
            both = jnp.where(c == 0, scale_q, scale_kv)
            zb[s, c, x, y, :, 512:cut_q] = (rows[:, 512:cut_q] * both * gain[:, 512:cut_q]).astype(BF16)
            zb[s, c, x, y, :, cut_q:] = jnp.where(lane < RD, turn, 0.0).astype(BF16)

        def gather_one(self):
            s = self.s
            self.one = []
            for d in (1, 3, 2):
                self.one.append(push(zb.at[s, c, x, y, :, ka], along_x(d)))
                self.one.append(push(zb.at[s, c, x, y, :, kb], along_y(d)))

        def gather_two(self):
            s = self.s
            self.two_a, self.two_b = [], []
            for copy in self.one:
                copy.wait_recv()
            for d in (1, 3, 2):
                self.two_a.append(push(zb.at[s, c, :, y, :, ka], along_y(d)))
                self.two_b.append(push(zb.at[s, c, x, :, :, kb], along_x(d)))

        def gather_mate(self):
            for copy in self.two_a:
                copy.wait_recv()
            self.mates = [push(zb.at[self.s, c, :, :, :, ka], peer)]
            for copy in self.two_b:
                copy.wait_recv()
            self.mates.append(push(zb.at[self.s, c, :, :, :, kb], peer))

        def gather_end(self):
            for copy in self.mates:
                copy.wait_recv()

        def close(self):
            for copy in self.core[0] + self.core[1] + self.direct + [self.square]:
                copy.wait_send()
            for ring in self.rings:
                ring.close()

    f0, f1 = Front(0), Front(1)
    product(0)
    greet_wait()
    f0.swap()
    xd_all[z] = xd_ref[...]

    def send_z(step, carry):
        zz, _, device = z_peer(step)
        remote(xd_ref, xd_all.at[zz], zs.at[step], zr.at[step], device).start()
        return carry

    lax.fori_loop(1, 8, send_z, 0)
    product(1)
    f0.far()
    f0.near()
    f1.swap()
    for load in loads[1:3]:
        load.start()

    def wait_z(step, carry):
        zz, other, device = z_peer(step)
        remote(xd_ref, xd_all.at[zz], zs.at[step], zr.at[step], device).wait()
        return carry

    f1.far()
    lax.fori_loop(1, 8, wait_z, 0)
    ii = lax.broadcasted_iota(jnp.int32, (16, 128), 0)
    jj = lax.broadcasted_iota(jnp.int32, (16, 128), 1)
    docs = docs_ref[...].reshape(1, 128)
    sel_in = jnp.where(docs == z * 16 + ii, 1.0, 0.0).astype(BF16)
    asked = jnp.dot(sel_in, xd_all[...].reshape(128, -1), preferred_element_type=F32).astype(BF16)
    for w_ref, lo, wide in ((wqa_ref, 0, QL), (wkv_s, QL, W - QL)):
        val = jnp.dot(asked, w_ref[...], preferred_element_type=F32)
        dec[:, :, lo : lo + wide] = val.reshape(2, 8, wide)
    dec_core = remote(dec.at[1 - c], dec_in, ds.at[0], dr.at[0], peer)
    dec_core.start()
    f0.pass_on()
    f1.near()
    loads[0].start()

    q_gain, kv_gain = qg_ref[...].reshape(1, QL), kvg_ref[...].reshape(1, KL)
    gain_s[...] = jnp.zeros_like(gain_s)
    gain_s[0:1, :cut_q] = q_gain[:, :cut_q]
    gain_s[1:2, : QL - cut_q] = q_gain[:, cut_q:]
    gain_s[1:2, QL - cut_q : cut_q] = kv_gain
    lens = len_ref[pl.ds(z, 1), :].astype(F32)
    i16 = lax.broadcasted_iota(jnp.int32, (16, 16), 0)
    j16 = lax.broadcasted_iota(jnp.int32, (16, 16), 1)
    spread = jnp.broadcast_to(lens, (16, 16))
    len_col = jnp.sum(jnp.where(i16 == j16, spread, 0.0), axis=1, keepdims=True)
    end_col = jnp.sum(jnp.where(j16 <= i16, spread, 0.0), axis=1, keepdims=True)
    end_row = jnp.sum(jnp.where(i16 <= j16, jnp.broadcast_to(len_col, (16, 16)), 0.0), axis=0, keepdims=True)
    token = lax.broadcasted_iota(jnp.int32, (512, 16), 0).astype(F32)
    begun = jnp.sum(jnp.where(token >= end_row, jnp.broadcast_to(lens, (512, 16)), 0.0), axis=1, keepdims=True)
    pos = lax.broadcasted_iota(jnp.int32, (512, 128), 0).astype(F32) - begun
    pos_s[...] = pos
    freq = freq_ref[...]
    for i in range(4):
        part = pl.ds(128 * i, 128)
        cos_s[part, :], sin_s[part, :] = turn_tables(pos_s[part, :], freq)
    cosd, sind = turn_tables(jnp.broadcast_to(len_col, (16, 128)), freq)

    f0.second()
    dec_core.wait()
    mine = dec[c] + dec_in[...]
    for j in range(16):
        tiles[j, :, 0:128] = mine[:, 128 * j : 128 * j + 128]
        tiles[j, :, 128:256] = mine[:, QL + KL :]

    def send_tile(step, carry):
        other, device = chip_peer(x, y, c, step)
        remote(tiles.at[other], tiles_in.at[chip], es.at[step], er.at[step], device).start()
        return carry

    lax.fori_loop(1, 16, send_tile, 0)
    tiles_in[chip] = tiles[chip]

    f1.pass_on()

    def turn_wo(k, carry):
        cut = pl.multiple_of(k * 896, 128)
        wot[pl.ds(cut, 896), :] = wo[:, pl.ds(cut, 896)].T
        return carry

    f0.rows()
    f0.norm()
    f0.gather_one()
    f1.second()

    loads[0].wait()
    lax.fori_loop(0, 3, turn_wo, 0)
    f0.gather_two()
    f1.rows()

    f1.norm()
    f1.gather_one()
    def wait_tile(step, carry):
        other, device = chip_peer(x, y, c, step)
        remote(tiles.at[other], tiles_in.at[chip], es.at[step], er.at[step], device).wait()
        return carry

    lax.fori_loop(1, 16, wait_tile, 0)
    total = jnp.sum(tiles_in[...], axis=0)
    sums_in[chip] = total[:, :128]

    def send_sum(step, carry):
        other, device = chip_peer(x, y, c, step)
        remote(sums_in.at[chip], sums_in.at[chip], gs.at[step], gr.at[step], device).start()
        return carry

    lax.fori_loop(1, 16, send_sum, 0)
    lax.fori_loop(3, 5, turn_wo, 0)
    f1.gather_two()
    f0.gather_mate()
    def wait_sum(step, carry):
        other, device = chip_peer(x, y, c, step)
        remote(sums_in.at[chip], sums_in.at[chip], gs.at[step], gr.at[step], device).wait()
        return carry

    lax.fori_loop(1, 16, wait_sum, 0)
    for j in range(16):
        rows_in[c, :, 128 * j : 128 * j + 128] = sums_in[j]
    rows_in[c, :, QL + KL : W] = total[:, 128:]
    dec_mate = remote(rows_in.at[c], rows_in.at[c], ms.at[0], mr.at[0], peer)
    dec_mate.start()
    heads = 4
    scale = 1.0 / float(NOPE + RD) ** 0.5
    wide = NOPE + VD
    for load in loads[1:3]:
        load.wait()
    lax.fori_loop(5, 8, turn_wo, 0)
    f0.gather_end()

    def project(s):
        rows = slice(256 * s, 256 * s + 256)
        latent = zb[s, 1, :, :, :, QL - cut_q : cut_q].reshape(256, KL)
        kv_s[rows, :] = jnp.dot(latent, wkvb[...], preferred_element_type=F32).astype(BF16)
        turn = zb[s, 1, :, :, :, cut_q:].reshape(256, 128)
        turn_s[0, rows, :] = turn
        turn_s[1, rows, :] = pltpu.roll(turn.astype(F32), 64, 1).astype(BF16)

    def block(s):
        for j in range(2):
            first = 256 * s + 128 * j
            begin = max(first - 128, 0)
            rows, keys = slice(first, first + 128), slice(begin, begin + 256)
            chips = slice(2 * j, 2 * j + 2)
            query = jnp.dot(
                zb[s, 0, chips, :, :, :cut_q].reshape(128, cut_q), wqb[:cut_q, :], preferred_element_type=F32
            )
            query = query + jnp.dot(
                zb[s, 1, chips, :, :, : QL - cut_q].reshape(128, QL - cut_q), wqb[cut_q:, :], preferred_element_type=F32
            )
            nope, rope = split_query(query, cos_s[rows, :], sin_s[rows, :])
            own = first + lax.broadcasted_iota(jnp.int32, (128, 256), 0)
            other = begin + lax.broadcasted_iota(jnp.int32, (128, 256), 1)
            back = (own - other).astype(F32)
            keep = (back >= 0) & (back <= jnp.concatenate([pos_s[rows, :]] * 2, axis=1))
            scores = []
            for h in range(heads):
                q = jnp.concatenate([nope[h], rope[h // 2]], axis=1)
                k = jnp.concatenate([kv_s[keys, wide * h : wide * h + NOPE], turn_s[h % 2, keys, :]], axis=1)
                scores.append(lax.dot_general(q, k, NT, preferred_element_type=F32))
            scores = jnp.concatenate(scores, axis=0) * scale
            scores = jnp.where(jnp.concatenate([keep] * heads, axis=0), scores, -1e30)
            e = jnp.exp(scores - jnp.max(scores, axis=-1, keepdims=True))
            p = (e * (1.0 / jnp.sum(e, axis=-1, keepdims=True))).astype(BF16)
            for h in range(heads):
                v = kv_s[keys, wide * h + NOPE : wide * h + wide]
                o = jnp.dot(p[128 * h : 128 * h + 128], v, preferred_element_type=F32)
                o_s[rows, VD * h : VD * h + VD] = o.astype(BF16)

    def decode():
        latent, own_lat = zb[:, 1, :, :, :, QL - cut_q : cut_q].reshape(512, KL), zd[:, QL : QL + KL]
        own_turn = zd[:, QL + KL : W]
        at = lax.broadcasted_iota(jnp.int32, (16, 512), 1).astype(F32)
        keep = (at < end_col) & (at >= end_col - len_col)
        keep = jnp.concatenate([keep] * heads, axis=0)
        diag = jnp.concatenate([i16 == j16] * heads, axis=0)
        q_abs, q_rope = qabs_s[...].reshape(16 * heads, KL), qrope_s[...].reshape(16 * heads, 128)
        s = lax.dot_general(q_abs, latent, NT, preferred_element_type=F32)
        s = (s + lax.dot_general(q_rope, turn_s[0], NT, preferred_element_type=F32)) * scale
        s = jnp.where(keep, s, -1e30)
        t = lax.dot_general(q_abs, own_lat, NT, preferred_element_type=F32)
        t = (t + lax.dot_general(q_rope, own_turn, NT, preferred_element_type=F32)) * scale
        t = jnp.where(diag, t, -1e30)
        top = jnp.maximum(jnp.max(s, axis=-1, keepdims=True), jnp.max(t, axis=-1, keepdims=True))
        e, f = jnp.exp(s - top), jnp.exp(t - top)
        part = 1.0 / (jnp.sum(e, axis=-1, keepdims=True) + jnp.sum(f, axis=-1, keepdims=True))
        lat = jnp.dot((e * part).astype(BF16), latent, preferred_element_type=F32)
        lat = (lat + jnp.dot((f * part).astype(BF16), own_lat, preferred_element_type=F32)).astype(BF16)
        for h in range(heads):
            up_v = wkvb[:, wide * h + NOPE : wide * h + wide]
            o = jnp.dot(lat[16 * h : 16 * h + 16], up_v, preferred_element_type=F32)
            od_s[:, VD * h : VD * h + VD] = o.astype(BF16)

    def decode_out():
        for k in range(8):
            val = jnp.dot(od_s[...], wo[:, 896 * k : 896 * k + 896], preferred_element_type=F32)
            for j in range(4):
                at = 224 * j // 128 * 128
                if at + 384 <= 896:
                    v = val[:, at : at + 384]
                else:
                    v = jnp.concatenate([val[:, at:896], val[:, : at + 384 - 896]], axis=1)
                if 224 * j - at:
                    v = pltpu.roll(v, 384 - (224 * j - at), 1)
                dt[j % 2, 2 * k + j // 2] = v[:, :256].astype(BF16)

    def output(s):
        far_x, far_y = next_of(x, 2), next_of(y, 2) // 2

        def part(n):
            if n < 2:
                k = 2 * far_x + n
            elif n < 5:
                k = 2 * next_of(far_x, n - 1) + far_y
            else:
                k = 2 * next_of(far_x, n - 4) + 1 - far_y
            xx, yy = k // 2, 2 * lax.rem(k, 2)
            w = wot[pl.ds(pl.multiple_of(k * 896, 128), 896), :]
            val = lax.dot_general(w, o_s[256 * s : 256 * s + 256, :], NT, preferred_element_type=F32).astype(BF16)
            for j in range(4):
                t0[s, j % 2, xx, yy + j // 2] = val[224 * j : 224 * j + 112]
                t1[s, j % 2, yy + j // 2, xx] = val[224 * j + 112 : 224 * j + 224]

        return part

    half = (slice(0, 128), slice(128, 256))

    class Stage:
        def __init__(self, s):
            self.s = s
            self.core = ([], [])
            self.rings = (
                Ring(t0.at[s, c], tnear0.at[s], tfar0.at[s], half, x, xp, xm, us, ur, 18 * s),
                Ring(t1.at[s, c], tnear1.at[s], tfar1.at[s], half, y, yp, ym, us, ur, 18 * s + 6),
            )
            self.lasts = [
                (tq0, tqin0, y, lambda d: tp_of(x, next_of(y, d), c)),
                (tq1, tqin1, x, lambda d: tp_of(next_of(x, d), y, c)),
            ]
            self.direct = ([], [])
            self.parts = ((t0, tc0, x, self.core[0]), (t1, tc1, y, self.core[1]))

        def swap(self, which):
            for i in which:
                d = order[i]
                for n, (t, came, pos_t, list_t) in enumerate(self.parts):
                    k, m = next_of(pos_t, d), 8 * self.s + 2 * i + n
                    copy = remote(t.at[self.s, 1 - c, k], came.at[self.s, k], vs.at[m], vr.at[m], peer)
                    copy.start()
                    list_t.append(copy)

        def take(self, i):
            for t, came, pos_t, list_t in self.parts:
                list_t[i].wait_recv()
                k = next_of(pos_t, order[i])
                t[self.s, c, k] = (t[self.s, c, k].astype(F32) + came[self.s, k].astype(F32)).astype(BF16)

        def first(self):
            self.take(0)
            for ring in self.rings:
                ring.start_far()
            self.take(1)
            self.take(2)
            for ring in self.rings:
                ring.start_near()
            self.take(3)

        def pass_on(self):
            for ring in self.rings:
                ring.pass_on()

        def second(self):
            for side in range(2):
                tq0[self.s, :, :, half[side]] = self.rings[0].result(side).astype(BF16)
                tq1[self.s, :, :, half[side]] = self.rings[1].result(side).astype(BF16)
            for d in (2, 1, 3):
                for h, (data, box, pos_q, dev) in enumerate(self.lasts):
                    n = 18 * self.s + 12 + 3 * h + d - 1
                    copy = remote(
                        data.at[self.s, next_of(pos_q, d)], box.at[self.s, d - 1], us.at[n], ur.at[n], {"tp": dev(d)}
                    )
                    copy.start()
                    self.direct[h].append(copy)

        def finish(self):
            for h, (data, box, pos_q, dev) in enumerate(self.lasts):
                for copy in self.direct[h]:
                    copy.wait_recv()
                came = [box[self.s, i].astype(F32) for i in range(3)]
                total = data[self.s, pos_q].astype(F32) + (came[0] + came[1]) + came[2]
                out_ref[112 * h : 112 * h + 112, 256 * self.s : 256 * self.s + 256] = total.astype(BF16)

        def close(self):
            for copy in self.core[0] + self.core[1]:
                copy.wait_send()
            for ring in self.rings:
                ring.close()
            for copy in self.direct[0] + self.direct[1]:
                copy.wait_send()

    s0, s1 = Stage(0), Stage(1)

    def produce(stage):
        part = output(stage.s)
        for n in range(5):
            part(n)
        stage.swap((0,))
        for n in range(5, 8):
            part(n)
        stage.swap((1, 2, 3))

    project(0)
    block(0)
    produce(s0)
    f1.gather_mate()
    s0.first()
    f1.gather_end()
    project(1)
    block(1)
    produce(s1)
    s0.pass_on()
    s1.first()
    dec_mate.wait()
    q, kv, turn = latent_rows(rows_in[...].reshape(16, W), q_gain, kv_gain, cosd, sind)
    zd[:, 0:QL] = q.astype(BF16)
    zd[:, QL : QL + KL] = kv.astype(BF16)
    zd[:, QL + KL : W] = turn.astype(BF16)
    query = jnp.dot(zd[:, :QL], wqb[...], preferred_element_type=F32)
    dec_nope, dec_rope = split_query(query, cosd, sind)
    for h in range(heads):
        up_k = wkvb[:, wide * h : wide * h + NOPE]
        qabs_s[h] = lax.dot_general(dec_nope[h], up_k, NT, preferred_element_type=F32).astype(BF16)
        if h % 2:
            qrope_s[h] = pltpu.roll(dec_rope[h // 2].astype(F32), 64, 1).astype(BF16)
        else:
            qrope_s[h] = dec_rope[h // 2]
    decode()
    decode_out()
    dec_swap = remote(dt.at[1 - c], dc, fs.at[0], fr.at[0], peer)
    dec_swap.start()
    s0.second()
    dec_swap.wait()
    dt[c] = (dt[c].astype(F32) + dc[...].astype(F32)).astype(BF16)

    def send_out(step, carry):
        other, device = chip_peer(x, y, c, step)
        remote(dt.at[c, other], dn.at[chip], hs.at[step], hr.at[step], device).start()
        return carry

    lax.fori_loop(1, 16, send_out, 0)
    dn[chip] = dt[c, chip]
    s1.pass_on()
    s0.finish()

    def wait_out(step, carry):
        other, device = chip_peer(x, y, c, step)
        remote(dt.at[c, other], dn.at[chip], hs.at[step], hr.at[step], device).wait()
        return carry

    lax.fori_loop(1, 16, wait_out, 0)
    dz[z] = jnp.sum(dn[...].astype(F32), axis=0).astype(BF16)

    def send_back(step, carry):
        zz, _, device = z_peer(step)
        remote(dz.at[zz], dz.at[zz], ys.at[step], yr.at[step], device).start()
        return carry

    lax.fori_loop(1, 8, send_back, 0)
    s1.second()

    def wait_back(step, carry):
        zz, _, device = z_peer(step)
        remote(dz.at[zz], dz.at[zz], ys.at[step], yr.at[step], device).wait()
        return carry

    lax.fori_loop(1, 8, wait_back, 0)
    wanted = jnp.sum(jnp.where(jj == z * 16 + ii, docs, 0).astype(F32), axis=1, keepdims=True)
    sel_out = jnp.where(jj.astype(F32) == wanted, 1.0, 0.0).astype(BF16)
    picked = jnp.dot(sel_out, dz[...].reshape(128, 256), preferred_element_type=F32)
    outd_ref[...] = picked[:, :224].astype(BF16)
    s1.finish()
    for copy in copies:
        copy.wait_send()
    f0.close()
    f1.close()
    s0.close()
    s1.close()


def whole(xt, xd, wq_a, wkv_a, q_gain, kv_gain, freq, doc_len, docs, wq_b, wkv_b, wo):
    vm = pl.BlockSpec(memory_space=pltpu.VMEM)
    hbm = pl.BlockSpec(memory_space=pl.ANY)
    dma = pltpu.SemaphoreType.DMA
    shapes = [
        (xt.shape, BF16), (wq_a.shape, BF16), (wkv_a.shape, BF16),
        (wq_b.shape, BF16), (wkv_b.shape, BF16), (wo.shape, BF16), (wo.shape[::-1], BF16),
        ((wq_a.shape[0], W - QL), BF16),
        ((2, 2, 4, 4, 8, HALF), F32), ((2, 2, 4, 4, 8, HALF), F32),
        ((2, 4, 4, 8, HALF), F32), ((2, 4, 4, 8, HALF), F32),
        ((2, 2, 4, 8, HALF), F32), ((2, 2, 4, 8, HALF), F32),
        ((2, 4, 8, HALF), F32), ((2, 4, 8, HALF), F32),
        ((2, 4, 8, HALF), F32), ((2, 4, 8, HALF), F32),
        ((2, 3, 8, HALF), F32), ((2, 3, 8, HALF), F32),
        ((8,) + xd.shape, BF16), ((2, 8, W), F32), ((8, W), F32),
        ((16, 8, 256), F32), ((16, 8, 256), F32), ((16, 8, 128), F32), ((2, 8, W), F32),
        ((2, 16, HALF), F32), ((2, 2, 16, 128), F32), ((2, 16, 128), F32), ((8, HALF), F32),
        ((2, 2, NX, NY, 16, HALF), BF16), ((16, W), BF16), ((4, 16, KL), BF16), ((4, 16, 128), BF16), ((512, 128), F32), ((512, 128), F32), ((512, 128), F32),
        ((512, wkv_b.shape[1]), BF16), ((2, 512, 128), BF16), ((512, 512), BF16), ((16, 512), BF16),
        ((2, 2, 4, 4, 112, 256), BF16), ((2, 2, 4, 4, 112, 256), BF16),
        ((2, 4, 4, 112, 256), BF16), ((2, 4, 4, 112, 256), BF16),
        ((2, 2, 4, 112, 256), BF16), ((2, 2, 4, 112, 256), BF16),
        ((2, 4, 112, 256), BF16), ((2, 4, 112, 256), BF16),
        ((2, 4, 112, 256), BF16), ((2, 4, 112, 256), BF16),
        ((2, 3, 112, 256), BF16), ((2, 3, 112, 256), BF16),
        ((2, 16, 16, 256), BF16), ((16, 16, 256), BF16), ((16, 16, 256), BF16),
        ((8, 16, 256), BF16),
    ]
    counts = (6, 8, 8, 16, 16, 36, 36, 1, 1, 16, 16, 16, 16, 28, 28, 1, 1, 36, 36, 16, 16, 1, 1, 16, 16, 8, 8, 2, 2)
    return pl.pallas_call(
        whole_kernel,
        out_shape=(jax.ShapeDtypeStruct((224, 512), BF16), jax.ShapeDtypeStruct((16, 224), BF16)),
        in_specs=[hbm, vm, hbm, hbm] + [vm] * 5 + [hbm] * 3,
        out_specs=(vm, vm),
        scratch_shapes=[pltpu.VMEM(shape, kind) for shape, kind in shapes] + [dma((n,)) for n in counts],
        compiler_params=pltpu.CompilerParams(
            collective_id=0, has_side_effects=True, vmem_limit_bytes=VMEM_LIMIT
        ),
        name="whole",
    )(xt, xd, wq_a, wkv_a, q_gain, kv_gain, freq, doc_len, docs, wq_b, wkv_b, wo)


def hand_over_kernel(a_ref, b_ref, out_ref, outd_ref):
    out_ref[...] = a_ref[...]
    outd_ref[...] = b_ref[...]


def hand_over(a, b):
    vm = pl.BlockSpec(memory_space=pltpu.VMEM)
    return pl.pallas_call(
        hand_over_kernel,
        out_shape=(jax.ShapeDtypeStruct(a.shape, a.dtype), jax.ShapeDtypeStruct(b.shape, b.dtype)),
        in_specs=[vm, vm],
        out_specs=(vm, vm),
        name="hand_over",
    )(a, b)


def per_device(x_pre, x_dec, wq_a, wkv_a, q_gain, kv_gain, wq_b, wkv_b, wo, doc_len, request_docs):
    half = RD // 2
    freq = np.tile(10000.0 ** (-np.arange(half) / half), 4).astype(np.float32)[None, :]
    out_t, out_dec = whole(
        x_pre.T, x_dec, wq_a, wkv_a, q_gain, kv_gain, jnp.asarray(freq), doc_len, request_docs, wq_b, wkv_b, wo
    )
    out_t, out_dec = hand_over(out_t, out_dec)
    return out_t.T, out_dec


def solution(mesh):
    placed = (
        P(("role", "grp"), "tp"),
        P(("role", "grp"), "tp"),
        P("tp", None),
        P("tp", None),
        P(),
        P(),
        P(None, "tp"),
        P(None, "tp"),
        P("tp", None),
        P(),
        P(),
    )
    return jax.shard_map(
        per_device,
        mesh=mesh,
        in_specs=placed,
        out_specs=(P(("role", "grp"), "tp"), P(("role", "grp"), "tp")),
        check_vma=False,
    )
```

```python
import jax
import jax.numpy as jnp
import numpy as np
from jax import lax
from jax.experimental import pallas as pl
from jax.experimental.pallas import tpu as pltpu
from jax.sharding import PartitionSpec as P

QL = 1536
KL = 512
RD = 64
NOPE = 128
VD = 128
NX = 4
NY = 4
W = QL + KL + 128
HALF = 1152
SPLIT = 640
EPS = 1e-06
F32 = jnp.float32
BF16 = jnp.bfloat16
MESH = pl.DeviceIdType.MESH
VMEM_LIMIT = 58 * 2**20


def place():
    tp = lax.axis_index("tp")
    return tp, tp // 8, lax.rem(tp // 2, NY), lax.rem(tp, 2)


def tp_of(x, y, c):
    return x * 8 + y * 2 + c


def next_of(p, step):
    return lax.rem(p + step + 4, 4)


def z_peer(step):
    z = lax.axis_index("role") * 2 + lax.axis_index("grp")
    other = lax.rem(z + step, 8)
    return z, other, {"role": other // 2, "grp": lax.rem(other, 2)}


def remote(src, dst, send, recv, device):
    return pltpu.make_async_remote_copy(
        src_ref=src, dst_ref=dst, send_sem=send, recv_sem=recv, device_id=device, device_id_type=MESH
    )


def chip_peer(x, y, c, step):
    other = lax.rem(x * 4 + y + step, 16)
    return other, {"tp": tp_of(other // 4, lax.rem(other, 4), c)}


def greet_start(x, y, c):
    barrier = pltpu.get_barrier_semaphore()
    pl.semaphore_signal(barrier, inc=1, device_id={"tp": tp_of(x, y, 1 - c)}, device_id_type=MESH)

    def chips(step, carry):
        _, device = chip_peer(x, y, c, step)
        pl.semaphore_signal(barrier, inc=1, device_id=device, device_id_type=MESH)
        return carry

    lax.fori_loop(1, 16, chips, 0)

    def planes(step, carry):
        _, _, device = z_peer(step)
        pl.semaphore_signal(barrier, inc=1, device_id=device, device_id_type=MESH)
        return carry

    lax.fori_loop(1, 8, planes, 0)


def greet_wait():
    pl.semaphore_wait(pltpu.get_barrier_semaphore(), 1 + 15 + 7)


class Ring:
    def __init__(self, data, near, far, part, pos, plus, minus, send, recv, base, sign=1):
        self.data, self.near, self.far, self.part = data, near, far, part
        self.pos, self.plus, self.minus = pos, plus, minus
        self.send, self.recv, self.base = send, recv, base
        self.sign = sign
        self.copies = {}

    def cut(self, ref, side):
        return ref.at[(Ellipsis, self.part[side])]

    def go(self, key, number, src, dst, device):
        copy = remote(src, dst, self.send.at[self.base + number], self.recv.at[self.base + number], device)
        copy.start()
        self.copies[key] = copy

    def start_far(self):
        chunk = self.data.at[next_of(self.pos, 2)]
        self.go("far0", 0, self.cut(chunk, 0), self.cut(self.far, 0), self.plus)
        self.go("far1", 1, self.cut(chunk, 1), self.cut(self.far, 1), self.minus)

    def start_near(self):
        up, down = self.data.at[next_of(self.pos, self.sign)], self.data.at[next_of(self.pos, -self.sign)]
        self.go("up1", 2, self.cut(up, 1), self.cut(self.near.at[0], 1), self.plus)
        self.go("down0", 3, self.cut(down, 0), self.cut(self.near.at[1], 0), self.minus)

    def add(self, chunk, side):
        ref, extra = self.cut(chunk, side), self.cut(self.far, side)
        ref[...] = (ref[...].astype(F32) + extra[...].astype(F32)).astype(ref.dtype)

    def pass_on(self):
        up, down = self.data.at[next_of(self.pos, self.sign)], self.data.at[next_of(self.pos, -self.sign)]
        self.copies["far0"].wait_recv()
        self.add(up, 0)
        self.go("up0", 4, self.cut(up, 0), self.cut(self.near.at[0], 0), self.plus)
        self.copies["far1"].wait_recv()
        self.add(down, 1)
        self.go("down1", 5, self.cut(down, 1), self.cut(self.near.at[1], 1), self.minus)

    def result(self, side):
        for key in ("up%d" % side, "down%d" % side):
            self.copies[key].wait_recv()
        own = self.cut(self.data.at[self.pos], side)[...].astype(F32)
        left = self.cut(self.near.at[0], side)[...].astype(F32)
        right = self.cut(self.near.at[1], side)[...].astype(F32)
        return own + (left + right)

    def close(self):
        for copy in self.copies.values():
            copy.wait_send()


def latent_rows(rows, q_gain, kv_gain, cosine, sine):
    q = rows[:, :QL]
    kv = rows[:, QL : QL + KL]
    turn = rows[:, QL + KL :]
    q = q * lax.rsqrt(jnp.mean(q * q, axis=-1, keepdims=True) + EPS) * q_gain
    kv = kv * lax.rsqrt(jnp.mean(kv * kv, axis=-1, keepdims=True) + EPS) * kv_gain
    turn = rope_tile(turn, cosine, sine)
    lane = lax.broadcasted_iota(jnp.int32, turn.shape, 1)
    turn = jnp.where(lane < RD, turn, 0.0)
    return q, kv, turn


def rope_tile(tile, cosine, sine):
    lane = lax.broadcasted_iota(jnp.int32, tile.shape, 1)
    swapped = jnp.where(lane % RD < RD // 2, pltpu.roll(tile, 96, 1), pltpu.roll(tile, 32, 1))
    return tile * cosine + swapped * sine


def turn_tables(pos, freq):
    turn = pos * freq
    lane = lax.broadcasted_iota(jnp.int32, turn.shape, 1)
    sine = jnp.sin(turn)
    return jnp.cos(turn), jnp.where(lane % RD < RD // 2, -sine, sine)


NT = (((1,), (1,)), ((), ()))
TN = (((0,), (0,)), ((), ()))


def split_query(query, cosine, sine):
    nope, rope = [], []
    lane = lax.broadcasted_iota(jnp.int32, (query.shape[0], 128), 1)
    for pair in range(query.shape[1] // 384):
        t0, t1, t2 = [query[:, 384 * pair + 128 * i : 384 * pair + 128 * i + 128] for i in range(3)]
        nope.append(t0.astype(BF16))
        nope.append(jnp.where(lane < 64, pltpu.roll(t1, 64, 1), pltpu.roll(t2, 64, 1)).astype(BF16))
        rope.append(rope_tile(jnp.where(lane < 64, t1, t2), cosine, sine).astype(BF16))
    return nope, rope


def whole_kernel(
    xt_hbm, xd_hbm, wqa_hbm, wkva_hbm, qg_hbm, kvg_hbm, freq_hbm, len_hbm, docs_hbm, wqb_hbm, wkvb_hbm, wo_hbm,
    out_ref, outd_ref, xt_ref, wqa_ref, wkva_ref, xd_ref, qg_ref, kvg_ref, freq_ref, len_ref, docs_ref,
    wqb, wkvb, wo, wot, wkv_s, p0, p1, c0, c1, near0, near1, far0, far1, q0, q1, in0, in1,
    xd_all, dec, dec_in, tiles, tiles_in, sums_in, rows_in,
    rows_s, square_s, square_in, gain_s,
    zb, zd, qabs_s, qrope_s, pos_s, cos_s, sin_s, kv_s, turn_s, o_s, od_s,
    t0, t1, tc0, tc1, tnear0, tnear1, tfar0, tfar1, tq0, tq1, tqin0, tqin1,
    dt, dc, dn, dz,
    ws, zs, zr, cs, cr, rs, rr, ds, dr, es, er, gs, gr, ks, kr, ms, mr,
    us, ur, vs, vr, fs, fr, hs, hr, ys, yr, qs, qr,
):
    tp, x, y, c = place()
    chip = x * 4 + y
    z, _, _ = z_peer(0)
    peer = {"tp": tp_of(x, y, 1 - c)}
    xp, xm = {"tp": tp_of(next_of(x, 1), y, c)}, {"tp": tp_of(next_of(x, -1), y, c)}
    yp, ym = {"tp": tp_of(x, next_of(y, 1), c)}, {"tp": tp_of(x, next_of(y, -1), c)}
    loads = [
        pltpu.make_async_copy(src, dst, ws.at[i])
        for i, (src, dst) in enumerate(
            (
                (wo_hbm, wo), (wkvb_hbm, wkvb), (wqb_hbm, wqb),
                (xt_hbm, xt_ref), (wqa_hbm, wqa_ref), (wkva_hbm, wkva_ref), (xd_hbm, xd_ref), (qg_hbm, qg_ref),
                (kvg_hbm, kvg_ref), (freq_hbm, freq_ref), (len_hbm, len_ref), (docs_hbm, docs_ref),
            )
        )
    ]
    for load in loads[3:]:
        load.start()
    greet_start(x, y, c)
    for load in loads[3:6]:
        load.wait()

    wkv_s[...] = jnp.zeros_like(wkv_s)
    wkv_s[:, : KL + RD] = wkva_ref[...]
    order = (2, 1, 3, 0)
    cut_q = 1024
    sign = 1 - 2 * c

    def product(s):
        rows = xt_ref[:, 256 * s : 256 * s + 256]
        for cc, w, lo in (
            (0, wqa_ref[:, :cut_q], 0),
            (1, wqa_ref[:, cut_q:], 0),
            (1, wkv_s[...], QL - cut_q),
        ):
            wide = w.shape[1]
            val = lax.dot_general(rows, w, TN, preferred_element_type=F32).reshape(NX, NY, 2, 8, wide)
            p0[s, cc, :, :, :, lo : lo + wide] = val[:, :, 0]
            for yy in range(NY):
                p1[s, cc, yy, :, :, lo : lo + wide] = val[:, yy, 1]
        p0[s, 0, :, :, :, cut_q:] = jnp.zeros((NX, NY, 8, HALF - cut_q), F32)
        p1[s, 0, :, :, :, cut_q:] = jnp.zeros((NX, NY, 8, HALF - cut_q), F32)

    lanes = (slice(0, SPLIT), slice(SPLIT, HALF))
    ka, kb = lanes
    copies = []

    def push(block, device):
        n = len(copies)
        copy = remote(block, block, ks.at[n], kr.at[n], device)
        copy.start()
        copies.append(copy)
        return copy

    def along_x(d):
        return {"tp": tp_of(next_of(x, d), y, c)}

    def along_y(d):
        return {"tp": tp_of(x, next_of(y, d), c)}

    class Front:
        def __init__(self, s):
            self.s = s
            self.core = ([], [])
            self.parts = ((p0, c0, x, self.core[0]), (p1, c1, y, self.core[1]))
            self.rings = (
                Ring(
                    p0.at[s, c], near0.at[s], far0.at[s], lanes, x, along_x(sign), along_x(-sign), rs, rr, 18 * s, sign
                ),
                Ring(
                    p1.at[s, c], near1.at[s], far1.at[s], lanes, y, along_y(sign), along_y(-sign), rs, rr, 18 * s + 6,
                    sign,
                ),
            )
            self.direct = []

        def swap(self):
            for i, d in enumerate(order):
                for h, (p, came, pos_p, list_p) in enumerate(self.parts):
                    k, n = next_of(pos_p, d), 8 * self.s + 2 * i + h
                    copy = remote(p.at[self.s, 1 - c, k], came.at[self.s, k], cs.at[n], cr.at[n], peer)
                    copy.start()
                    list_p.append(copy)

        def take(self, i, h):
            p, came, pos_p, list_p = self.parts[h]
            list_p[i].wait_recv()
            k = next_of(pos_p, order[i])
            p[self.s, c, k] = p[self.s, c, k] + came[self.s, k]

        def far(self):
            for h in range(2):
                self.take(0, h)
                self.rings[h].start_far()

        def near(self):
            for h in range(2):
                self.take(1, h)
                self.take(2, h)
                self.rings[h].start_near()
            for h in range(2):
                self.take(3, h)

        def pass_on(self):
            for ring in self.rings:
                ring.pass_on()

        def second(self):
            for h, (q, box, pos_h, dev) in enumerate(((q0, in0, y, along_y), (q1, in1, x, along_x))):
                for side in range(2):
                    q[self.s, :, :, lanes[side]] = self.rings[h].result(side)
                for d in (2, 1, 3):
                    n = 18 * self.s + 12 + 3 * h + d - 1
                    copy = remote(
                        q.at[self.s, next_of(pos_h, d)], box.at[self.s, d - 1], rs.at[n], rr.at[n], dev(d)
                    )
                    copy.start()
                    self.direct.append(copy)

        def rows(self):
            for copy in self.direct:
                copy.wait_recv()
            s = self.s
            top = q0[s, y] + (in0[s, 0] + in0[s, 1]) + in0[s, 2]
            low = q1[s, x] + (in1[s, 0] + in1[s, 1]) + in1[s, 2]
            rows = jnp.concatenate([top, low], axis=0)
            rows_s[s] = rows
            left = jnp.sum(rows[:, :512] * rows[:, :512], axis=-1, keepdims=True)
            right = jnp.sum(rows[:, 512:cut_q] * rows[:, 512:cut_q], axis=-1, keepdims=True)
            square_s[s, 0] = jnp.broadcast_to(left + jnp.where(c == 0, right, 0.0), (16, 128))
            square_s[s, 1] = jnp.broadcast_to(right, (16, 128))
            self.square = remote(square_s.at[s, 0], square_in.at[s], qs.at[s], qr.at[s], peer)
            self.square.start()

        def norm(self):
            s = self.s
            self.square.wait_recv()
            rows = rows_s[s]
            mean_q = (square_s[s, 0] + square_in[s])[:, 0:1] * (1.0 / QL)
            mean_kv = square_s[s, 1][:, 0:1] * (1.0 / KL)
            scale_q, scale_kv = lax.rsqrt(mean_q + EPS), lax.rsqrt(mean_kv + EPS)
            gain = gain_s[pl.ds(c, 1), :]
            at = pl.ds(pl.multiple_of(256 * s + 16 * chip, 16), 16)
            turn = rope_tile(rows[:, cut_q:], cos_s[at, :], sin_s[at, :])
            lane = lax.broadcasted_iota(jnp.int32, turn.shape, 1)
            zb[s, c, x, y, :, 0:512] = (rows[:, :512] * scale_q * gain[:, :512]).astype(BF16)
            both = jnp.where(c == 0, scale_q, scale_kv)
            zb[s, c, x, y, :, 512:cut_q] = (rows[:, 512:cut_q] * both * gain[:, 512:cut_q]).astype(BF16)
            zb[s, c, x, y, :, cut_q:] = jnp.where(lane < RD, turn, 0.0).astype(BF16)

        def gather_one(self):
            s = self.s
            self.one = []
            for d in (1, 3, 2):
                self.one.append(push(zb.at[s, c, x, y, :, ka], along_x(d)))
                self.one.append(push(zb.at[s, c, x, y, :, kb], along_y(d)))

        def gather_two(self):
            s = self.s
            self.two_a, self.two_b = [], []
            for copy in self.one:
                copy.wait_recv()
            for d in (1, 3, 2):
                self.two_a.append(push(zb.at[s, c, :, y, :, ka], along_y(d)))
                self.two_b.append(push(zb.at[s, c, x, :, :, kb], along_x(d)))

        def gather_mate(self):
            for copy in self.two_a:
                copy.wait_recv()
            self.mates = [push(zb.at[self.s, c, :, :, :, ka], peer)]
            for copy in self.two_b:
                copy.wait_recv()
            self.mates.append(push(zb.at[self.s, c, :, :, :, kb], peer))

        def gather_end(self):
            for copy in self.mates:
                copy.wait_recv()

        def close(self):
            for copy in self.core[0] + self.core[1] + self.direct + [self.square]:
                copy.wait_send()
            for ring in self.rings:
                ring.close()

    f0, f1 = Front(0), Front(1)
    product(0)
    greet_wait()
    f0.swap()
    for load in loads[6:]:
        load.wait()
    xd_all[z] = xd_ref[...]

    def send_z(step, carry):
        zz, _, device = z_peer(step)
        remote(xd_ref, xd_all.at[zz], zs.at[step], zr.at[step], device).start()
        return carry

    lax.fori_loop(1, 8, send_z, 0)
    product(1)
    f0.far()
    f0.near()
    f1.swap()
    for load in loads[1:3]:
        load.start()

    def wait_z(step, carry):
        zz, other, device = z_peer(step)
        remote(xd_ref, xd_all.at[zz], zs.at[step], zr.at[step], device).wait()
        return carry

    f1.far()
    lax.fori_loop(1, 8, wait_z, 0)
    ii = lax.broadcasted_iota(jnp.int32, (16, 128), 0)
    jj = lax.broadcasted_iota(jnp.int32, (16, 128), 1)
    docs = docs_ref[...].reshape(1, 128)
    sel_in = jnp.where(docs == z * 16 + ii, 1.0, 0.0).astype(BF16)
    asked = jnp.dot(sel_in, xd_all[...].reshape(128, -1), preferred_element_type=F32).astype(BF16)
    for w_ref, lo, wide in ((wqa_ref, 0, QL), (wkv_s, QL, W - QL)):
        val = jnp.dot(asked, w_ref[...], preferred_element_type=F32)
        dec[:, :, lo : lo + wide] = val.reshape(2, 8, wide)
    dec_core = remote(dec.at[1 - c], dec_in, ds.at[0], dr.at[0], peer)
    dec_core.start()
    f0.pass_on()
    f1.near()
    loads[0].start()

    q_gain, kv_gain = qg_ref[...].reshape(1, QL), kvg_ref[...].reshape(1, KL)
    gain_s[...] = jnp.zeros_like(gain_s)
    gain_s[0:1, :cut_q] = q_gain[:, :cut_q]
    gain_s[1:2, : QL - cut_q] = q_gain[:, cut_q:]
    gain_s[1:2, QL - cut_q : cut_q] = kv_gain
    lens = len_ref[pl.ds(z, 1), :].astype(F32)
    i16 = lax.broadcasted_iota(jnp.int32, (16, 16), 0)
    j16 = lax.broadcasted_iota(jnp.int32, (16, 16), 1)
    spread = jnp.broadcast_to(lens, (16, 16))
    len_col = jnp.sum(jnp.where(i16 == j16, spread, 0.0), axis=1, keepdims=True)
    end_col = jnp.sum(jnp.where(j16 <= i16, spread, 0.0), axis=1, keepdims=True)
    end_row = jnp.sum(jnp.where(i16 <= j16, jnp.broadcast_to(len_col, (16, 16)), 0.0), axis=0, keepdims=True)
    token = lax.broadcasted_iota(jnp.int32, (512, 16), 0).astype(F32)
    begun = jnp.sum(jnp.where(token >= end_row, jnp.broadcast_to(lens, (512, 16)), 0.0), axis=1, keepdims=True)
    pos = lax.broadcasted_iota(jnp.int32, (512, 128), 0).astype(F32) - begun
    pos_s[...] = pos
    freq = freq_ref[...]
    for i in range(4):
        part = pl.ds(128 * i, 128)
        cos_s[part, :], sin_s[part, :] = turn_tables(pos_s[part, :], freq)
    cosd, sind = turn_tables(jnp.broadcast_to(len_col, (16, 128)), freq)

    f0.second()
    dec_core.wait()
    mine = dec[c] + dec_in[...]
    for j in range(16):
        tiles[j, :, 0:128] = mine[:, 128 * j : 128 * j + 128]
        tiles[j, :, 128:256] = mine[:, QL + KL :]

    def send_tile(step, carry):
        other, device = chip_peer(x, y, c, step)
        remote(tiles.at[other], tiles_in.at[chip], es.at[step], er.at[step], device).start()
        return carry

    lax.fori_loop(1, 16, send_tile, 0)
    tiles_in[chip] = tiles[chip]

    f1.pass_on()

    def turn_wo(k, carry):
        cut = pl.multiple_of(k * 896, 128)
        wot[pl.ds(cut, 896), :] = wo[:, pl.ds(cut, 896)].T
        return carry

    f0.rows()
    f0.norm()
    f0.gather_one()
    f1.second()

    loads[0].wait()
    lax.fori_loop(0, 3, turn_wo, 0)
    f0.gather_two()
    f1.rows()

    f1.norm()
    f1.gather_one()
    def wait_tile(step, carry):
        other, device = chip_peer(x, y, c, step)
        remote(tiles.at[other], tiles_in.at[chip], es.at[step], er.at[step], device).wait()
        return carry

    lax.fori_loop(1, 16, wait_tile, 0)
    total = jnp.sum(tiles_in[...], axis=0)
    sums_in[chip] = total[:, :128]

    def send_sum(step, carry):
        other, device = chip_peer(x, y, c, step)
        remote(sums_in.at[chip], sums_in.at[chip], gs.at[step], gr.at[step], device).start()
        return carry

    lax.fori_loop(1, 16, send_sum, 0)
    lax.fori_loop(3, 5, turn_wo, 0)
    f1.gather_two()
    f0.gather_mate()
    def wait_sum(step, carry):
        other, device = chip_peer(x, y, c, step)
        remote(sums_in.at[chip], sums_in.at[chip], gs.at[step], gr.at[step], device).wait()
        return carry

    lax.fori_loop(1, 16, wait_sum, 0)
    for j in range(16):
        rows_in[c, :, 128 * j : 128 * j + 128] = sums_in[j]
    rows_in[c, :, QL + KL : W] = total[:, 128:]
    dec_mate = remote(rows_in.at[c], rows_in.at[c], ms.at[0], mr.at[0], peer)
    dec_mate.start()
    heads = 4
    scale = 1.0 / float(NOPE + RD) ** 0.5
    wide = NOPE + VD
    for load in loads[1:3]:
        load.wait()
    lax.fori_loop(5, 8, turn_wo, 0)
    f0.gather_end()

    def project(s):
        rows = slice(256 * s, 256 * s + 256)
        latent = zb[s, 1, :, :, :, QL - cut_q : cut_q].reshape(256, KL)
        kv_s[rows, :] = jnp.dot(latent, wkvb[...], preferred_element_type=F32).astype(BF16)
        turn = zb[s, 1, :, :, :, cut_q:].reshape(256, 128)
        turn_s[0, rows, :] = turn
        turn_s[1, rows, :] = pltpu.roll(turn.astype(F32), 64, 1).astype(BF16)

    def block(s):
        for j in range(2):
            first = 256 * s + 128 * j
            begin = max(first - 128, 0)
            rows, keys = slice(first, first + 128), slice(begin, begin + 256)
            chips = slice(2 * j, 2 * j + 2)
            query = jnp.dot(
                zb[s, 0, chips, :, :, :cut_q].reshape(128, cut_q), wqb[:cut_q, :], preferred_element_type=F32
            )
            query = query + jnp.dot(
                zb[s, 1, chips, :, :, : QL - cut_q].reshape(128, QL - cut_q), wqb[cut_q:, :], preferred_element_type=F32
            )
            nope, rope = split_query(query, cos_s[rows, :], sin_s[rows, :])
            own = first + lax.broadcasted_iota(jnp.int32, (128, 256), 0)
            other = begin + lax.broadcasted_iota(jnp.int32, (128, 256), 1)
            back = (own - other).astype(F32)
            keep = (back >= 0) & (back <= jnp.concatenate([pos_s[rows, :]] * 2, axis=1))
            scores = []
            for h in range(heads):
                q = jnp.concatenate([nope[h], rope[h // 2]], axis=1)
                k = jnp.concatenate([kv_s[keys, wide * h : wide * h + NOPE], turn_s[h % 2, keys, :]], axis=1)
                scores.append(lax.dot_general(q, k, NT, preferred_element_type=F32))
            scores = jnp.concatenate(scores, axis=0) * scale
            scores = jnp.where(jnp.concatenate([keep] * heads, axis=0), scores, -1e30)
            e = jnp.exp(scores - jnp.max(scores, axis=-1, keepdims=True))
            p = (e * (1.0 / jnp.sum(e, axis=-1, keepdims=True))).astype(BF16)
            for h in range(heads):
                v = kv_s[keys, wide * h + NOPE : wide * h + wide]
                o = jnp.dot(p[128 * h : 128 * h + 128], v, preferred_element_type=F32)
                o_s[rows, VD * h : VD * h + VD] = o.astype(BF16)

    def decode():
        latent, own_lat = zb[:, 1, :, :, :, QL - cut_q : cut_q].reshape(512, KL), zd[:, QL : QL + KL]
        own_turn = zd[:, QL + KL : W]
        at = lax.broadcasted_iota(jnp.int32, (16, 512), 1).astype(F32)
        keep = (at < end_col) & (at >= end_col - len_col)
        keep = jnp.concatenate([keep] * heads, axis=0)
        diag = jnp.concatenate([i16 == j16] * heads, axis=0)
        q_abs, q_rope = qabs_s[...].reshape(16 * heads, KL), qrope_s[...].reshape(16 * heads, 128)
        s = lax.dot_general(q_abs, latent, NT, preferred_element_type=F32)
        s = (s + lax.dot_general(q_rope, turn_s[0], NT, preferred_element_type=F32)) * scale
        s = jnp.where(keep, s, -1e30)
        t = lax.dot_general(q_abs, own_lat, NT, preferred_element_type=F32)
        t = (t + lax.dot_general(q_rope, own_turn, NT, preferred_element_type=F32)) * scale
        t = jnp.where(diag, t, -1e30)
        top = jnp.maximum(jnp.max(s, axis=-1, keepdims=True), jnp.max(t, axis=-1, keepdims=True))
        e, f = jnp.exp(s - top), jnp.exp(t - top)
        part = 1.0 / (jnp.sum(e, axis=-1, keepdims=True) + jnp.sum(f, axis=-1, keepdims=True))
        lat = jnp.dot((e * part).astype(BF16), latent, preferred_element_type=F32)
        lat = (lat + jnp.dot((f * part).astype(BF16), own_lat, preferred_element_type=F32)).astype(BF16)
        for h in range(heads):
            up_v = wkvb[:, wide * h + NOPE : wide * h + wide]
            o = jnp.dot(lat[16 * h : 16 * h + 16], up_v, preferred_element_type=F32)
            od_s[:, VD * h : VD * h + VD] = o.astype(BF16)

    def decode_out():
        for k in range(8):
            val = jnp.dot(od_s[...], wo[:, 896 * k : 896 * k + 896], preferred_element_type=F32)
            for j in range(4):
                at = 224 * j // 128 * 128
                if at + 384 <= 896:
                    v = val[:, at : at + 384]
                else:
                    v = jnp.concatenate([val[:, at:896], val[:, : at + 384 - 896]], axis=1)
                if 224 * j - at:
                    v = pltpu.roll(v, 384 - (224 * j - at), 1)
                dt[j % 2, 2 * k + j // 2] = v[:, :256].astype(BF16)

    def output(s):
        far_x, far_y = next_of(x, 2), next_of(y, 2) // 2

        def part(n):
            if n < 2:
                k = 2 * far_x + n
            elif n < 5:
                k = 2 * next_of(far_x, n - 1) + far_y
            else:
                k = 2 * next_of(far_x, n - 4) + 1 - far_y
            xx, yy = k // 2, 2 * lax.rem(k, 2)
            w = wot[pl.ds(pl.multiple_of(k * 896, 128), 896), :]
            val = lax.dot_general(w, o_s[256 * s : 256 * s + 256, :], NT, preferred_element_type=F32).astype(BF16)
            for j in range(4):
                t0[s, j % 2, xx, yy + j // 2] = val[224 * j : 224 * j + 112]
                t1[s, j % 2, yy + j // 2, xx] = val[224 * j + 112 : 224 * j + 224]

        return part

    half = (slice(0, 128), slice(128, 256))

    class Stage:
        def __init__(self, s):
            self.s = s
            self.core = ([], [])
            self.rings = (
                Ring(t0.at[s, c], tnear0.at[s], tfar0.at[s], half, x, xp, xm, us, ur, 18 * s),
                Ring(t1.at[s, c], tnear1.at[s], tfar1.at[s], half, y, yp, ym, us, ur, 18 * s + 6),
            )
            self.lasts = [
                (tq0, tqin0, y, lambda d: tp_of(x, next_of(y, d), c)),
                (tq1, tqin1, x, lambda d: tp_of(next_of(x, d), y, c)),
            ]
            self.direct = ([], [])
            self.parts = ((t0, tc0, x, self.core[0]), (t1, tc1, y, self.core[1]))

        def swap(self, which):
            for i in which:
                d = order[i]
                for n, (t, came, pos_t, list_t) in enumerate(self.parts):
                    k, m = next_of(pos_t, d), 8 * self.s + 2 * i + n
                    copy = remote(t.at[self.s, 1 - c, k], came.at[self.s, k], vs.at[m], vr.at[m], peer)
                    copy.start()
                    list_t.append(copy)

        def take(self, i):
            for t, came, pos_t, list_t in self.parts:
                list_t[i].wait_recv()
                k = next_of(pos_t, order[i])
                t[self.s, c, k] = (t[self.s, c, k].astype(F32) + came[self.s, k].astype(F32)).astype(BF16)

        def first(self):
            self.take(0)
            for ring in self.rings:
                ring.start_far()
            self.take(1)
            self.take(2)
            for ring in self.rings:
                ring.start_near()
            self.take(3)

        def pass_on(self):
            for ring in self.rings:
                ring.pass_on()

        def second(self):
            for h, (data, box, pos_q, dev) in enumerate(self.lasts):
                for side in range(2):
                    data[self.s, :, :, half[side]] = self.rings[h].result(side).astype(BF16)
                for d in (2, 1, 3):
                    n = 18 * self.s + 12 + 3 * h + d - 1
                    copy = remote(
                        data.at[self.s, next_of(pos_q, d)], box.at[self.s, d - 1], us.at[n], ur.at[n], {"tp": dev(d)}
                    )
                    copy.start()
                    self.direct[h].append(copy)

        def finish(self):
            for h, (data, box, pos_q, dev) in enumerate(self.lasts):
                for copy in self.direct[h]:
                    copy.wait_recv()
                came = [box[self.s, i].astype(F32) for i in range(3)]
                total = data[self.s, pos_q].astype(F32) + (came[0] + came[1]) + came[2]
                out_ref[112 * h : 112 * h + 112, 256 * self.s : 256 * self.s + 256] = total.astype(BF16)

        def close(self):
            for copy in self.core[0] + self.core[1]:
                copy.wait_send()
            for ring in self.rings:
                ring.close()
            for copy in self.direct[0] + self.direct[1]:
                copy.wait_send()

    s0, s1 = Stage(0), Stage(1)

    def produce(stage):
        part = output(stage.s)
        for n in range(5):
            part(n)
        stage.swap((0,))
        for n in range(5, 8):
            part(n)
        stage.swap((1, 2, 3))

    project(0)
    block(0)
    produce(s0)
    f1.gather_mate()
    s0.first()
    f1.gather_end()
    project(1)
    block(1)
    produce(s1)
    s0.pass_on()
    s1.first()
    dec_mate.wait()
    q, kv, turn = latent_rows(rows_in[...].reshape(16, W), q_gain, kv_gain, cosd, sind)
    zd[:, 0:QL] = q.astype(BF16)
    zd[:, QL : QL + KL] = kv.astype(BF16)
    zd[:, QL + KL : W] = turn.astype(BF16)
    query = jnp.dot(zd[:, :QL], wqb[...], preferred_element_type=F32)
    dec_nope, dec_rope = split_query(query, cosd, sind)
    for h in range(heads):
        up_k = wkvb[:, wide * h : wide * h + NOPE]
        qabs_s[h] = lax.dot_general(dec_nope[h], up_k, NT, preferred_element_type=F32).astype(BF16)
        if h % 2:
            qrope_s[h] = pltpu.roll(dec_rope[h // 2].astype(F32), 64, 1).astype(BF16)
        else:
            qrope_s[h] = dec_rope[h // 2]
    decode()
    decode_out()
    dec_swap = remote(dt.at[1 - c], dc, fs.at[0], fr.at[0], peer)
    dec_swap.start()
    s0.second()
    dec_swap.wait()
    dt[c] = (dt[c].astype(F32) + dc[...].astype(F32)).astype(BF16)

    def send_out(step, carry):
        other, device = chip_peer(x, y, c, step)
        remote(dt.at[c, other], dn.at[chip], hs.at[step], hr.at[step], device).start()
        return carry

    lax.fori_loop(1, 16, send_out, 0)
    dn[chip] = dt[c, chip]
    s1.pass_on()
    s0.finish()

    def wait_out(step, carry):
        other, device = chip_peer(x, y, c, step)
        remote(dt.at[c, other], dn.at[chip], hs.at[step], hr.at[step], device).wait()
        return carry

    lax.fori_loop(1, 16, wait_out, 0)
    dz[z] = jnp.sum(dn[...].astype(F32), axis=0).astype(BF16)

    def send_back(step, carry):
        zz, _, device = z_peer(step)
        remote(dz.at[zz], dz.at[zz], ys.at[step], yr.at[step], device).start()
        return carry

    lax.fori_loop(1, 8, send_back, 0)
    s1.second()

    def wait_back(step, carry):
        zz, _, device = z_peer(step)
        remote(dz.at[zz], dz.at[zz], ys.at[step], yr.at[step], device).wait()
        return carry

    lax.fori_loop(1, 8, wait_back, 0)
    wanted = jnp.sum(jnp.where(jj == z * 16 + ii, docs, 0).astype(F32), axis=1, keepdims=True)
    sel_out = jnp.where(jj.astype(F32) == wanted, 1.0, 0.0).astype(BF16)
    picked = jnp.dot(sel_out, dz[...].reshape(128, 256), preferred_element_type=F32)
    outd_ref[...] = picked[:, :224].astype(BF16)
    s1.finish()
    for copy in copies:
        copy.wait_send()
    f0.close()
    f1.close()
    s0.close()
    s1.close()


def whole(xt, xd, wq_a, wkv_a, q_gain, kv_gain, freq, doc_len, docs, wq_b, wkv_b, wo):
    vm = pl.BlockSpec(memory_space=pltpu.VMEM)
    hbm = pl.BlockSpec(memory_space=pl.ANY)
    dma = pltpu.SemaphoreType.DMA
    shapes = [
        (xt.shape, BF16), (wq_a.shape, BF16), (wkv_a.shape, BF16), (xd.shape, BF16), (q_gain.shape, F32),
        (kv_gain.shape, F32), (freq.shape, F32), (doc_len.shape, jnp.int32), (docs.shape, jnp.int32),
        (wq_b.shape, BF16), (wkv_b.shape, BF16), (wo.shape, BF16), (wo.shape[::-1], BF16),
        ((wq_a.shape[0], W - QL), BF16),
        ((2, 2, 4, 4, 8, HALF), F32), ((2, 2, 4, 4, 8, HALF), F32),
        ((2, 4, 4, 8, HALF), F32), ((2, 4, 4, 8, HALF), F32),
        ((2, 2, 4, 8, HALF), F32), ((2, 2, 4, 8, HALF), F32),
        ((2, 4, 8, HALF), F32), ((2, 4, 8, HALF), F32),
        ((2, 4, 8, HALF), F32), ((2, 4, 8, HALF), F32),
        ((2, 3, 8, HALF), F32), ((2, 3, 8, HALF), F32),
        ((8,) + xd.shape, BF16), ((2, 8, W), F32), ((8, W), F32),
        ((16, 8, 256), F32), ((16, 8, 256), F32), ((16, 8, 128), F32), ((2, 8, W), F32),
        ((2, 16, HALF), F32), ((2, 2, 16, 128), F32), ((2, 16, 128), F32), ((8, HALF), F32),
        ((2, 2, NX, NY, 16, HALF), BF16), ((16, W), BF16), ((4, 16, KL), BF16), ((4, 16, 128), BF16), ((512, 128), F32), ((512, 128), F32), ((512, 128), F32),
        ((512, wkv_b.shape[1]), BF16), ((2, 512, 128), BF16), ((512, 512), BF16), ((16, 512), BF16),
        ((2, 2, 4, 4, 112, 256), BF16), ((2, 2, 4, 4, 112, 256), BF16),
        ((2, 4, 4, 112, 256), BF16), ((2, 4, 4, 112, 256), BF16),
        ((2, 2, 4, 112, 256), BF16), ((2, 2, 4, 112, 256), BF16),
        ((2, 4, 112, 256), BF16), ((2, 4, 112, 256), BF16),
        ((2, 4, 112, 256), BF16), ((2, 4, 112, 256), BF16),
        ((2, 3, 112, 256), BF16), ((2, 3, 112, 256), BF16),
        ((2, 16, 16, 256), BF16), ((16, 16, 256), BF16), ((16, 16, 256), BF16),
        ((8, 16, 256), BF16),
    ]
    counts = (12, 8, 8, 16, 16, 36, 36, 1, 1, 16, 16, 16, 16, 28, 28, 1, 1, 36, 36, 16, 16, 1, 1, 16, 16, 8, 8, 2, 2)
    return pl.pallas_call(
        whole_kernel,
        out_shape=(jax.ShapeDtypeStruct((224, 512), BF16), jax.ShapeDtypeStruct((16, 224), BF16)),
        in_specs=[hbm] * 12,
        out_specs=(vm, vm),
        scratch_shapes=[pltpu.VMEM(shape, kind) for shape, kind in shapes] + [dma((n,)) for n in counts],
        compiler_params=pltpu.CompilerParams(
            collective_id=0, has_side_effects=True, vmem_limit_bytes=VMEM_LIMIT
        ),
        name="whole",
    )(xt, xd, wq_a, wkv_a, q_gain, kv_gain, freq, doc_len, docs, wq_b, wkv_b, wo)


def hand_over_kernel(a_ref, b_ref, out_ref, outd_ref):
    out_ref[...] = a_ref[...]
    outd_ref[...] = b_ref[...]


def hand_over(a, b):
    vm = pl.BlockSpec(memory_space=pltpu.VMEM)
    return pl.pallas_call(
        hand_over_kernel,
        out_shape=(jax.ShapeDtypeStruct(a.shape, a.dtype), jax.ShapeDtypeStruct(b.shape, b.dtype)),
        in_specs=[vm, vm],
        out_specs=(vm, vm),
        name="hand_over",
    )(a, b)


def per_device(x_pre, x_dec, wq_a, wkv_a, q_gain, kv_gain, wq_b, wkv_b, wo, doc_len, request_docs):
    half = RD // 2
    freq = np.tile(10000.0 ** (-np.arange(half) / half), 4).astype(np.float32)[None, :]
    out_t, out_dec = whole(
        x_pre.T, x_dec, wq_a, wkv_a, q_gain, kv_gain, jnp.asarray(freq), doc_len, request_docs, wq_b, wkv_b, wo
    )
    out_t, out_dec = hand_over(out_t, out_dec)
    return out_t.T, out_dec


def solution(mesh):
    placed = (
        P(("role", "grp"), "tp"),
        P(("role", "grp"), "tp"),
        P("tp", None),
        P("tp", None),
        P(),
        P(),
        P(None, "tp"),
        P(None, "tp"),
        P("tp", None),
        P(),
        P(),
    )
    return jax.shard_map(
        per_device,
        mesh=mesh,
        in_specs=placed,
        out_specs=(P(("role", "grp"), "tp"), P(("role", "grp"), "tp")),
        check_vma=False,
    )
```

```python
import jax
import jax.numpy as jnp
import numpy as np
from jax import lax
from jax.experimental import pallas as pl
from jax.experimental.pallas import tpu as pltpu
from jax.sharding import PartitionSpec as P

QL = 1536
KL = 512
RD = 64
NOPE = 128
VD = 128
NX = 4
NY = 4
W = QL + KL + 128
HALF = 1152
SPLIT = 640
EPS = 1e-06
F32 = jnp.float32
BF16 = jnp.bfloat16
MESH = pl.DeviceIdType.MESH
VMEM_LIMIT = 58 * 2**20


def place():
    tp = lax.axis_index("tp")
    return tp, tp // 8, lax.rem(tp // 2, NY), lax.rem(tp, 2)


def tp_of(x, y, c):
    return x * 8 + y * 2 + c


def next_of(p, step):
    return lax.rem(p + step + 4, 4)


def z_peer(step):
    z = lax.axis_index("role") * 2 + lax.axis_index("grp")
    other = lax.rem(z + step, 8)
    return z, other, {"role": other // 2, "grp": lax.rem(other, 2)}


def remote(src, dst, send, recv, device):
    return pltpu.make_async_remote_copy(
        src_ref=src, dst_ref=dst, send_sem=send, recv_sem=recv, device_id=device, device_id_type=MESH
    )


def chip_peer(x, y, c, step):
    other = lax.rem(x * 4 + y + step, 16)
    return other, {"tp": tp_of(other // 4, lax.rem(other, 4), c)}


def greet_start(x, y, c):
    barrier = pltpu.get_barrier_semaphore()
    pl.semaphore_signal(barrier, inc=1, device_id={"tp": tp_of(x, y, 1 - c)}, device_id_type=MESH)

    def chips(step, carry):
        _, device = chip_peer(x, y, c, step)
        pl.semaphore_signal(barrier, inc=1, device_id=device, device_id_type=MESH)
        return carry

    lax.fori_loop(1, 16, chips, 0)

    def planes(step, carry):
        _, _, device = z_peer(step)
        pl.semaphore_signal(barrier, inc=1, device_id=device, device_id_type=MESH)
        return carry

    lax.fori_loop(1, 8, planes, 0)


def greet_wait():
    pl.semaphore_wait(pltpu.get_barrier_semaphore(), 1 + 15 + 7)


class Ring:
    def __init__(self, data, near, far, part, pos, plus, minus, send, recv, base, sign=1):
        self.data, self.near, self.far, self.part = data, near, far, part
        self.pos, self.plus, self.minus = pos, plus, minus
        self.send, self.recv, self.base = send, recv, base
        self.sign = sign
        self.copies = {}

    def cut(self, ref, side):
        return ref.at[(Ellipsis, self.part[side])]

    def go(self, key, number, src, dst, device):
        copy = remote(src, dst, self.send.at[self.base + number], self.recv.at[self.base + number], device)
        copy.start()
        self.copies[key] = copy

    def start_far(self):
        chunk = self.data.at[next_of(self.pos, 2)]
        self.go("far0", 0, self.cut(chunk, 0), self.cut(self.far, 0), self.plus)
        self.go("far1", 1, self.cut(chunk, 1), self.cut(self.far, 1), self.minus)

    def start_near(self):
        up, down = self.data.at[next_of(self.pos, self.sign)], self.data.at[next_of(self.pos, -self.sign)]
        self.go("up1", 2, self.cut(up, 1), self.cut(self.near.at[0], 1), self.plus)
        self.go("down0", 3, self.cut(down, 0), self.cut(self.near.at[1], 0), self.minus)

    def add(self, chunk, side):
        ref, extra = self.cut(chunk, side), self.cut(self.far, side)
        ref[...] = (ref[...].astype(F32) + extra[...].astype(F32)).astype(ref.dtype)

    def pass_on(self):
        up, down = self.data.at[next_of(self.pos, self.sign)], self.data.at[next_of(self.pos, -self.sign)]
        self.copies["far0"].wait_recv()
        self.add(up, 0)
        self.go("up0", 4, self.cut(up, 0), self.cut(self.near.at[0], 0), self.plus)
        self.copies["far1"].wait_recv()
        self.add(down, 1)
        self.go("down1", 5, self.cut(down, 1), self.cut(self.near.at[1], 1), self.minus)

    def result(self, side):
        for key in ("up%d" % side, "down%d" % side):
            self.copies[key].wait_recv()
        own = self.cut(self.data.at[self.pos], side)[...].astype(F32)
        left = self.cut(self.near.at[0], side)[...].astype(F32)
        right = self.cut(self.near.at[1], side)[...].astype(F32)
        return own + (left + right)

    def close(self):
        for copy in self.copies.values():
            copy.wait_send()


def latent_rows(rows, q_gain, kv_gain, cosine, sine):
    q = rows[:, :QL]
    kv = rows[:, QL : QL + KL]
    turn = rows[:, QL + KL :]
    q = q * lax.rsqrt(jnp.mean(q * q, axis=-1, keepdims=True) + EPS) * q_gain
    kv = kv * lax.rsqrt(jnp.mean(kv * kv, axis=-1, keepdims=True) + EPS) * kv_gain
    turn = rope_tile(turn, cosine, sine)
    lane = lax.broadcasted_iota(jnp.int32, turn.shape, 1)
    turn = jnp.where(lane < RD, turn, 0.0)
    return q, kv, turn


def rope_tile(tile, cosine, sine):
    lane = lax.broadcasted_iota(jnp.int32, tile.shape, 1)
    swapped = jnp.where(lane % RD < RD // 2, pltpu.roll(tile, 96, 1), pltpu.roll(tile, 32, 1))
    return tile * cosine + swapped * sine


def turn_tables(pos, freq):
    turn = pos * freq
    lane = lax.broadcasted_iota(jnp.int32, turn.shape, 1)
    sine = jnp.sin(turn)
    return jnp.cos(turn), jnp.where(lane % RD < RD // 2, -sine, sine)


NT = (((1,), (1,)), ((), ()))
TN = (((0,), (0,)), ((), ()))


def split_query(query, cosine, sine):
    nope, rope = [], []
    lane = lax.broadcasted_iota(jnp.int32, (query.shape[0], 128), 1)
    for pair in range(query.shape[1] // 384):
        t0, t1, t2 = [query[:, 384 * pair + 128 * i : 384 * pair + 128 * i + 128] for i in range(3)]
        nope.append(t0.astype(BF16))
        nope.append(jnp.where(lane < 64, pltpu.roll(t1, 64, 1), pltpu.roll(t2, 64, 1)).astype(BF16))
        rope.append(rope_tile(jnp.where(lane < 64, t1, t2), cosine, sine).astype(BF16))
    return nope, rope


def whole_kernel(
    xt_hbm, xd_hbm, wqa_hbm, wkva_hbm, qg_hbm, kvg_hbm, freq_hbm, len_hbm, docs_hbm, wqb_hbm, wkvb_hbm, wo_hbm,
    out_ref, outd_ref, xt_ref, wqa_ref, wkva_ref, xd_ref, qg_ref, kvg_ref, freq_ref, len_ref, docs_ref,
    wqb, wkvb, wo, wot, wkv_s, p0, p1, c0, c1, near0, near1, far0, far1, q0, q1, in0, in1,
    xd_all, dec, dec_in, tiles, tiles_in, sums_in, rows_in,
    rows_s, square_s, square_in, gain_s,
    zb, zd, qabs_s, qrope_s, pos_s, cos_s, sin_s, kv_s, turn_s, o_s, od_s,
    t0, t1, tc0, tc1, tnear0, tnear1, tfar0, tfar1, tq0, tq1, tqin0, tqin1,
    dt, dc, dn, dz,
    ws, zs, zr, cs, cr, rs, rr, ds, dr, es, er, gs, gr, ks, kr, ms, mr,
    us, ur, vs, vr, fs, fr, hs, hr, ys, yr, qs, qr,
):
    tp, x, y, c = place()
    chip = x * 4 + y
    z, _, _ = z_peer(0)
    peer = {"tp": tp_of(x, y, 1 - c)}
    xp, xm = {"tp": tp_of(next_of(x, 1), y, c)}, {"tp": tp_of(next_of(x, -1), y, c)}
    yp, ym = {"tp": tp_of(x, next_of(y, 1), c)}, {"tp": tp_of(x, next_of(y, -1), c)}
    loads = [
        pltpu.make_async_copy(src, dst, ws.at[i])
        for i, (src, dst) in enumerate(
            (
                (wo_hbm, wo), (wkvb_hbm, wkvb), (wqb_hbm, wqb),
                (xt_hbm, xt_ref), (wqa_hbm, wqa_ref), (wkva_hbm, wkva_ref), (xd_hbm, xd_ref), (qg_hbm, qg_ref),
                (kvg_hbm, kvg_ref), (freq_hbm, freq_ref), (len_hbm, len_ref), (docs_hbm, docs_ref),
            )
        )
    ]
    for load in loads[3:]:
        load.start()
    greet_start(x, y, c)
    for load in loads[3:6]:
        load.wait()

    wkv_s[...] = jnp.zeros_like(wkv_s)
    wkv_s[:, : KL + RD] = wkva_ref[...]
    order = (2, 1, 3, 0)
    cut_q = 1024
    sign = 1 - 2 * c

    def product(s):
        rows = xt_ref[:, 256 * s : 256 * s + 256]
        for cc, w, lo in (
            (0, wqa_ref[:, :cut_q], 0),
            (1, wqa_ref[:, cut_q:], 0),
            (1, wkv_s[...], QL - cut_q),
        ):
            wide = w.shape[1]
            val = lax.dot_general(rows, w, TN, preferred_element_type=F32).reshape(NX, NY, 2, 8, wide)
            p0[s, cc, :, :, :, lo : lo + wide] = val[:, :, 0]
            for yy in range(NY):
                p1[s, cc, yy, :, :, lo : lo + wide] = val[:, yy, 1]
        p0[s, 0, :, :, :, cut_q:] = jnp.zeros((NX, NY, 8, HALF - cut_q), F32)
        p1[s, 0, :, :, :, cut_q:] = jnp.zeros((NX, NY, 8, HALF - cut_q), F32)

    lanes = (slice(0, SPLIT), slice(SPLIT, HALF))
    ka, kb = lanes
    copies = []

    def push(block, device):
        n = len(copies)
        copy = remote(block, block, ks.at[n], kr.at[n], device)
        copy.start()
        copies.append(copy)
        return copy

    def along_x(d):
        return {"tp": tp_of(next_of(x, d), y, c)}

    def along_y(d):
        return {"tp": tp_of(x, next_of(y, d), c)}

    class Front:
        def __init__(self, s):
            self.s = s
            self.core = ([], [])
            self.parts = ((p0, c0, x, self.core[0]), (p1, c1, y, self.core[1]))
            self.rings = (
                Ring(
                    p0.at[s, c], near0.at[s], far0.at[s], lanes, x, along_x(sign), along_x(-sign), rs, rr, 18 * s, sign
                ),
                Ring(
                    p1.at[s, c], near1.at[s], far1.at[s], lanes, y, along_y(sign), along_y(-sign), rs, rr, 18 * s + 6,
                    sign,
                ),
            )
            self.direct = []

        def swap(self):
            for i, d in enumerate(order):
                for h, (p, came, pos_p, list_p) in enumerate(self.parts):
                    k, n = next_of(pos_p, d), 8 * self.s + 2 * i + h
                    copy = remote(p.at[self.s, 1 - c, k], came.at[self.s, k], cs.at[n], cr.at[n], peer)
                    copy.start()
                    list_p.append(copy)

        def take(self, i, h):
            p, came, pos_p, list_p = self.parts[h]
            list_p[i].wait_recv()
            k = next_of(pos_p, order[i])
            p[self.s, c, k] = p[self.s, c, k] + came[self.s, k]

        def far(self):
            for h in range(2):
                self.take(0, h)
                self.rings[h].start_far()

        def near(self):
            for h in range(2):
                self.take(1, h)
                self.take(2, h)
                self.rings[h].start_near()
            for h in range(2):
                self.take(3, h)

        def pass_on(self):
            for ring in self.rings:
                ring.pass_on()

        def second(self):
            for h, (q, box, pos_h, dev) in enumerate(((q0, in0, y, along_y), (q1, in1, x, along_x))):
                for side in range(2):
                    q[self.s, :, :, lanes[side]] = self.rings[h].result(side)
                for d in (2, 1, 3):
                    n = 18 * self.s + 12 + 3 * h + d - 1
                    copy = remote(
                        q.at[self.s, next_of(pos_h, d)], box.at[self.s, d - 1], rs.at[n], rr.at[n], dev(d)
                    )
                    copy.start()
                    self.direct.append(copy)

        def rows(self):
            for copy in self.direct:
                copy.wait_recv()
            s = self.s
            top = q0[s, y] + (in0[s, 0] + in0[s, 1]) + in0[s, 2]
            low = q1[s, x] + (in1[s, 0] + in1[s, 1]) + in1[s, 2]
            rows = jnp.concatenate([top, low], axis=0)
            rows_s[s] = rows
            left = jnp.sum(rows[:, :512] * rows[:, :512], axis=-1, keepdims=True)
            right = jnp.sum(rows[:, 512:cut_q] * rows[:, 512:cut_q], axis=-1, keepdims=True)
            square_s[s, 0] = jnp.broadcast_to(left + jnp.where(c == 0, right, 0.0), (16, 128))
            square_s[s, 1] = jnp.broadcast_to(right, (16, 128))
            self.square = remote(square_s.at[s, 0], square_in.at[s], qs.at[s], qr.at[s], peer)
            self.square.start()

        def norm(self):
            s = self.s
            self.square.wait_recv()
            rows = rows_s[s]
            mean_q = (square_s[s, 0] + square_in[s])[:, 0:1] * (1.0 / QL)
            mean_kv = square_s[s, 1][:, 0:1] * (1.0 / KL)
            scale_q, scale_kv = lax.rsqrt(mean_q + EPS), lax.rsqrt(mean_kv + EPS)
            gain = gain_s[pl.ds(c, 1), :]
            at = pl.ds(pl.multiple_of(256 * s + 16 * chip, 16), 16)
            turn = rope_tile(rows[:, cut_q:], cos_s[at, :], sin_s[at, :])
            lane = lax.broadcasted_iota(jnp.int32, turn.shape, 1)
            zb[s, c, x, y, :, 0:512] = (rows[:, :512] * scale_q * gain[:, :512]).astype(BF16)
            both = jnp.where(c == 0, scale_q, scale_kv)
            zb[s, c, x, y, :, 512:cut_q] = (rows[:, 512:cut_q] * both * gain[:, 512:cut_q]).astype(BF16)
            zb[s, c, x, y, :, cut_q:] = jnp.where(lane < RD, turn, 0.0).astype(BF16)

        def gather_one(self):
            s = self.s
            self.one = []
            for d in (1, 3, 2):
                self.one.append(push(zb.at[s, c, x, y, :, ka], along_x(d)))
                self.one.append(push(zb.at[s, c, x, y, :, kb], along_y(d)))

        def gather_two(self):
            s = self.s
            self.two_a, self.two_b = [], []
            for copy in self.one:
                copy.wait_recv()
            for d in (1, 3, 2):
                self.two_a.append(push(zb.at[s, c, :, y, :, ka], along_y(d)))
                self.two_b.append(push(zb.at[s, c, x, :, :, kb], along_x(d)))

        def gather_mate(self):
            for copy in self.two_a:
                copy.wait_recv()
            self.mates = [push(zb.at[self.s, c, :, :, :, ka], peer)]
            for copy in self.two_b:
                copy.wait_recv()
            self.mates.append(push(zb.at[self.s, c, :, :, :, kb], peer))

        def gather_end(self):
            for copy in self.mates:
                copy.wait_recv()

        def close(self):
            for copy in self.core[0] + self.core[1] + self.direct + [self.square]:
                copy.wait_send()
            for ring in self.rings:
                ring.close()

    f0, f1 = Front(0), Front(1)
    product(0)
    greet_wait()
    f0.swap()
    for load in loads[6:]:
        load.wait()
    xd_all[z] = xd_ref[...]

    def send_z(step, carry):
        zz, _, device = z_peer(step)
        remote(xd_ref, xd_all.at[zz], zs.at[step], zr.at[step], device).start()
        return carry

    lax.fori_loop(1, 8, send_z, 0)
    product(1)
    f0.far()
    f0.near()
    f1.swap()
    for load in loads[1:3]:
        load.start()

    def wait_z(step, carry):
        zz, other, device = z_peer(step)
        remote(xd_ref, xd_all.at[zz], zs.at[step], zr.at[step], device).wait()
        return carry

    f1.far()
    lax.fori_loop(1, 8, wait_z, 0)
    ii = lax.broadcasted_iota(jnp.int32, (16, 128), 0)
    jj = lax.broadcasted_iota(jnp.int32, (16, 128), 1)
    docs = docs_ref[...].reshape(1, 128)
    sel_in = jnp.where(docs == z * 16 + ii, 1.0, 0.0).astype(BF16)
    asked = jnp.dot(sel_in, xd_all[...].reshape(128, -1), preferred_element_type=F32).astype(BF16)
    for w_ref, lo, wide in ((wqa_ref, 0, QL), (wkv_s, QL, W - QL)):
        val = jnp.dot(asked, w_ref[...], preferred_element_type=F32)
        dec[:, :, lo : lo + wide] = val.reshape(2, 8, wide)
    dec_core = remote(dec.at[1 - c], dec_in, ds.at[0], dr.at[0], peer)
    dec_core.start()
    f0.pass_on()
    f1.near()
    loads[0].start()

    q_gain, kv_gain = qg_ref[...].reshape(1, QL), kvg_ref[...].reshape(1, KL)
    gain_s[...] = jnp.zeros_like(gain_s)
    gain_s[0:1, :cut_q] = q_gain[:, :cut_q]
    gain_s[1:2, : QL - cut_q] = q_gain[:, cut_q:]
    gain_s[1:2, QL - cut_q : cut_q] = kv_gain
    lens = len_ref[pl.ds(z, 1), :].astype(F32)
    i16 = lax.broadcasted_iota(jnp.int32, (16, 16), 0)
    j16 = lax.broadcasted_iota(jnp.int32, (16, 16), 1)
    spread = jnp.broadcast_to(lens, (16, 16))
    len_col = jnp.sum(jnp.where(i16 == j16, spread, 0.0), axis=1, keepdims=True)
    end_col = jnp.sum(jnp.where(j16 <= i16, spread, 0.0), axis=1, keepdims=True)
    end_row = jnp.sum(jnp.where(i16 <= j16, jnp.broadcast_to(len_col, (16, 16)), 0.0), axis=0, keepdims=True)
    token = lax.broadcasted_iota(jnp.int32, (512, 16), 0).astype(F32)
    begun = jnp.sum(jnp.where(token >= end_row, jnp.broadcast_to(lens, (512, 16)), 0.0), axis=1, keepdims=True)
    pos = lax.broadcasted_iota(jnp.int32, (512, 128), 0).astype(F32) - begun
    pos_s[...] = pos
    freq = freq_ref[...]
    for i in range(4):
        part = pl.ds(128 * i, 128)
        cos_s[part, :], sin_s[part, :] = turn_tables(pos_s[part, :], freq)
    cosd, sind = turn_tables(jnp.broadcast_to(len_col, (16, 128)), freq)

    f0.second()
    dec_core.wait()
    mine = dec[c] + dec_in[...]
    for j in range(16):
        tiles[j, :, 0:128] = mine[:, 128 * j : 128 * j + 128]
        tiles[j, :, 128:256] = mine[:, QL + KL :]

    def send_tile(step, carry):
        other, device = chip_peer(x, y, c, step)
        remote(tiles.at[other], tiles_in.at[chip], es.at[step], er.at[step], device).start()
        return carry

    lax.fori_loop(1, 16, send_tile, 0)
    tiles_in[chip] = tiles[chip]

    f1.pass_on()

    def turn_wo(k, carry):
        cut = pl.multiple_of(k * 896, 128)
        wot[pl.ds(cut, 896), :] = wo[:, pl.ds(cut, 896)].T
        return carry

    f0.rows()
    f0.norm()
    f0.gather_one()
    f1.second()

    loads[0].wait()
    lax.fori_loop(0, 3, turn_wo, 0)
    f0.gather_two()
    f1.rows()

    f1.norm()
    f1.gather_one()
    def wait_tile(step, carry):
        other, device = chip_peer(x, y, c, step)
        remote(tiles.at[other], tiles_in.at[chip], es.at[step], er.at[step], device).wait()
        return carry

    lax.fori_loop(1, 16, wait_tile, 0)
    total = jnp.sum(tiles_in[...], axis=0)
    sums_in[chip] = total[:, :128]

    def send_sum(step, carry):
        other, device = chip_peer(x, y, c, step)
        remote(sums_in.at[chip], sums_in.at[chip], gs.at[step], gr.at[step], device).start()
        return carry

    lax.fori_loop(1, 16, send_sum, 0)
    lax.fori_loop(3, 5, turn_wo, 0)
    f1.gather_two()
    f0.gather_mate()
    def wait_sum(step, carry):
        other, device = chip_peer(x, y, c, step)
        remote(sums_in.at[chip], sums_in.at[chip], gs.at[step], gr.at[step], device).wait()
        return carry

    lax.fori_loop(1, 16, wait_sum, 0)
    for j in range(16):
        rows_in[c, :, 128 * j : 128 * j + 128] = sums_in[j]
    rows_in[c, :, QL + KL : W] = total[:, 128:]
    dec_mate = remote(rows_in.at[c], rows_in.at[c], ms.at[0], mr.at[0], peer)
    dec_mate.start()
    heads = 4
    scale = 1.0 / float(NOPE + RD) ** 0.5
    wide = NOPE + VD
    for load in loads[1:3]:
        load.wait()
    lax.fori_loop(5, 8, turn_wo, 0)
    f0.gather_end()

    def project(s):
        rows = slice(256 * s, 256 * s + 256)
        latent = zb[s, 1, :, :, :, QL - cut_q : cut_q].reshape(256, KL)
        kv_s[rows, :] = jnp.dot(latent, wkvb[...], preferred_element_type=F32).astype(BF16)
        turn = zb[s, 1, :, :, :, cut_q:].reshape(256, 128)
        turn_s[0, rows, :] = turn
        turn_s[1, rows, :] = pltpu.roll(turn.astype(F32), 64, 1).astype(BF16)

    def block(s):
        for j in range(2):
            first = 256 * s + 128 * j
            begin = max(first - 128, 0)
            rows, keys = slice(first, first + 128), slice(begin, begin + 256)
            chips = slice(2 * j, 2 * j + 2)
            query = jnp.dot(
                zb[s, 0, chips, :, :, :cut_q].reshape(128, cut_q), wqb[:cut_q, :], preferred_element_type=F32
            )
            query = query + jnp.dot(
                zb[s, 1, chips, :, :, : QL - cut_q].reshape(128, QL - cut_q), wqb[cut_q:, :], preferred_element_type=F32
            )
            nope, rope = split_query(query, cos_s[rows, :], sin_s[rows, :])
            own = first + lax.broadcasted_iota(jnp.int32, (128, 256), 0)
            other = begin + lax.broadcasted_iota(jnp.int32, (128, 256), 1)
            back = (own - other).astype(F32)
            keep = (back >= 0) & (back <= jnp.concatenate([pos_s[rows, :]] * 2, axis=1))
            scores = []
            for h in range(heads):
                q = jnp.concatenate([nope[h], rope[h // 2]], axis=1)
                k = jnp.concatenate([kv_s[keys, wide * h : wide * h + NOPE], turn_s[h % 2, keys, :]], axis=1)
                scores.append(lax.dot_general(q, k, NT, preferred_element_type=F32))
            scores = jnp.concatenate(scores, axis=0) * scale
            scores = jnp.where(jnp.concatenate([keep] * heads, axis=0), scores, -1e30)
            e = jnp.exp(scores - jnp.max(scores, axis=-1, keepdims=True))
            p = (e * (1.0 / jnp.sum(e, axis=-1, keepdims=True))).astype(BF16)
            for h in range(heads):
                v = kv_s[keys, wide * h + NOPE : wide * h + wide]
                o = jnp.dot(p[128 * h : 128 * h + 128], v, preferred_element_type=F32)
                o_s[rows, VD * h : VD * h + VD] = o.astype(BF16)

    def decode():
        latent, own_lat = zb[:, 1, :, :, :, QL - cut_q : cut_q].reshape(512, KL), zd[:, QL : QL + KL]
        own_turn = zd[:, QL + KL : W]
        at = lax.broadcasted_iota(jnp.int32, (16, 512), 1).astype(F32)
        keep = (at < end_col) & (at >= end_col - len_col)
        keep = jnp.concatenate([keep] * heads, axis=0)
        diag = jnp.concatenate([i16 == j16] * heads, axis=0)
        q_abs, q_rope = qabs_s[...].reshape(16 * heads, KL), qrope_s[...].reshape(16 * heads, 128)
        s = lax.dot_general(q_abs, latent, NT, preferred_element_type=F32)
        s = (s + lax.dot_general(q_rope, turn_s[0], NT, preferred_element_type=F32)) * scale
        s = jnp.where(keep, s, -1e30)
        t = lax.dot_general(q_abs, own_lat, NT, preferred_element_type=F32)
        t = (t + lax.dot_general(q_rope, own_turn, NT, preferred_element_type=F32)) * scale
        t = jnp.where(diag, t, -1e30)
        top = jnp.maximum(jnp.max(s, axis=-1, keepdims=True), jnp.max(t, axis=-1, keepdims=True))
        e, f = jnp.exp(s - top), jnp.exp(t - top)
        part = 1.0 / (jnp.sum(e, axis=-1, keepdims=True) + jnp.sum(f, axis=-1, keepdims=True))
        lat = jnp.dot((e * part).astype(BF16), latent, preferred_element_type=F32)
        lat = (lat + jnp.dot((f * part).astype(BF16), own_lat, preferred_element_type=F32)).astype(BF16)
        for h in range(heads):
            up_v = wkvb[:, wide * h + NOPE : wide * h + wide]
            o = jnp.dot(lat[16 * h : 16 * h + 16], up_v, preferred_element_type=F32)
            od_s[:, VD * h : VD * h + VD] = o.astype(BF16)

    def decode_out():
        for k in range(8):
            val = jnp.dot(od_s[...], wo[:, 896 * k : 896 * k + 896], preferred_element_type=F32)
            for j in range(4):
                at = 224 * j // 128 * 128
                if at + 384 <= 896:
                    v = val[:, at : at + 384]
                else:
                    v = jnp.concatenate([val[:, at:896], val[:, : at + 384 - 896]], axis=1)
                if 224 * j - at:
                    v = pltpu.roll(v, 384 - (224 * j - at), 1)
                dt[j % 2, 2 * k + j // 2] = v[:, :256].astype(BF16)

    def output(s):
        far_x, far_y = next_of(x, 2), next_of(y, 2) // 2

        def part(n):
            if n < 2:
                k = 2 * far_x + n
            elif n < 5:
                k = 2 * next_of(far_x, n - 1) + far_y
            else:
                k = 2 * next_of(far_x, n - 4) + 1 - far_y
            xx, yy = k // 2, 2 * lax.rem(k, 2)
            w = wot[pl.ds(pl.multiple_of(k * 896, 128), 896), :]
            val = lax.dot_general(w, o_s[256 * s : 256 * s + 256, :], NT, preferred_element_type=F32).astype(BF16)
            for j in range(4):
                t0[s, j % 2, xx, yy + j // 2] = val[224 * j : 224 * j + 112]
                t1[s, j % 2, yy + j // 2, xx] = val[224 * j + 112 : 224 * j + 224]

        return part

    half = (slice(0, 128), slice(128, 256))

    class Stage:
        def __init__(self, s):
            self.s = s
            self.core = ([], [])
            self.rings = (
                Ring(t0.at[s, c], tnear0.at[s], tfar0.at[s], half, x, xp, xm, us, ur, 18 * s),
                Ring(t1.at[s, c], tnear1.at[s], tfar1.at[s], half, y, yp, ym, us, ur, 18 * s + 6),
            )
            self.lasts = [
                (tq0, tqin0, y, lambda d: tp_of(x, next_of(y, d), c)),
                (tq1, tqin1, x, lambda d: tp_of(next_of(x, d), y, c)),
            ]
            self.direct = ([], [])
            self.parts = ((t0, tc0, x, self.core[0]), (t1, tc1, y, self.core[1]))

        def swap(self, which):
            for i in which:
                d = order[i]
                for n, (t, came, pos_t, list_t) in enumerate(self.parts):
                    k, m = next_of(pos_t, d), 8 * self.s + 2 * i + n
                    copy = remote(t.at[self.s, 1 - c, k], came.at[self.s, k], vs.at[m], vr.at[m], peer)
                    copy.start()
                    list_t.append(copy)

        def take(self, i):
            for t, came, pos_t, list_t in self.parts:
                list_t[i].wait_recv()
                k = next_of(pos_t, order[i])
                t[self.s, c, k] = (t[self.s, c, k].astype(F32) + came[self.s, k].astype(F32)).astype(BF16)

        def first(self):
            self.take(0)
            for ring in self.rings:
                ring.start_far()
            self.take(1)
            self.take(2)
            for ring in self.rings:
                ring.start_near()
            self.take(3)

        def pass_on(self):
            for ring in self.rings:
                ring.pass_on()

        def second(self):
            for h, (data, box, pos_q, dev) in enumerate(self.lasts):
                for side in range(2):
                    data[self.s, :, :, half[side]] = self.rings[h].result(side).astype(BF16)
                for d in (2, 1, 3):
                    n = 18 * self.s + 12 + 3 * h + d - 1
                    copy = remote(
                        data.at[self.s, next_of(pos_q, d)], box.at[self.s, d - 1], us.at[n], ur.at[n], {"tp": dev(d)}
                    )
                    copy.start()
                    self.direct[h].append(copy)

        def finish(self):
            for h, (data, box, pos_q, dev) in enumerate(self.lasts):
                for copy in self.direct[h]:
                    copy.wait_recv()
                came = [box[self.s, i].astype(F32) for i in range(3)]
                total = data[self.s, pos_q].astype(F32) + (came[0] + came[1]) + came[2]
                out_ref[112 * h : 112 * h + 112, 256 * self.s : 256 * self.s + 256] = total.astype(BF16)

        def close(self):
            for copy in self.core[0] + self.core[1]:
                copy.wait_send()
            for ring in self.rings:
                ring.close()
            for copy in self.direct[0] + self.direct[1]:
                copy.wait_send()

    s0, s1 = Stage(0), Stage(1)

    def produce(stage):
        part = output(stage.s)
        for n in range(5):
            part(n)
        stage.swap((0,))
        for n in range(5, 8):
            part(n)
        stage.swap((1, 2, 3))

    project(0)
    block(0)
    produce(s0)
    f1.gather_mate()
    s0.first()
    f1.gather_end()
    project(1)
    block(1)
    produce(s1)
    s0.pass_on()
    s1.first()
    dec_mate.wait()
    q, kv, turn = latent_rows(rows_in[...].reshape(16, W), q_gain, kv_gain, cosd, sind)
    zd[:, 0:QL] = q.astype(BF16)
    zd[:, QL : QL + KL] = kv.astype(BF16)
    zd[:, QL + KL : W] = turn.astype(BF16)
    query = jnp.dot(zd[:, :QL], wqb[...], preferred_element_type=F32)
    dec_nope, dec_rope = split_query(query, cosd, sind)
    for h in range(heads):
        up_k = wkvb[:, wide * h : wide * h + NOPE]
        qabs_s[h] = lax.dot_general(dec_nope[h], up_k, NT, preferred_element_type=F32).astype(BF16)
        if h % 2:
            qrope_s[h] = pltpu.roll(dec_rope[h // 2].astype(F32), 64, 1).astype(BF16)
        else:
            qrope_s[h] = dec_rope[h // 2]
    decode()
    decode_out()
    dec_swap = remote(dt.at[1 - c], dc, fs.at[0], fr.at[0], peer)
    dec_swap.start()
    s0.second()
    dec_swap.wait()
    dt[c] = (dt[c].astype(F32) + dc[...].astype(F32)).astype(BF16)

    def send_out(step, carry):
        other, device = chip_peer(x, y, c, step)
        remote(dt.at[c, other], dn.at[chip], hs.at[step], hr.at[step], device).start()
        return carry

    lax.fori_loop(1, 16, send_out, 0)
    dn[chip] = dt[c, chip]
    s1.pass_on()
    s0.finish()
    s1.second()

    def wait_out(step, carry):
        other, device = chip_peer(x, y, c, step)
        remote(dt.at[c, other], dn.at[chip], hs.at[step], hr.at[step], device).wait()
        return carry

    lax.fori_loop(1, 16, wait_out, 0)
    dz[z] = jnp.sum(dn[...].astype(F32), axis=0).astype(BF16)

    def send_back(step, carry):
        zz, _, device = z_peer(step)
        remote(dz.at[zz], dz.at[zz], ys.at[step], yr.at[step], device).start()
        return carry

    lax.fori_loop(1, 8, send_back, 0)

    def wait_back(step, carry):
        zz, _, device = z_peer(step)
        remote(dz.at[zz], dz.at[zz], ys.at[step], yr.at[step], device).wait()
        return carry

    lax.fori_loop(1, 8, wait_back, 0)
    wanted = jnp.sum(jnp.where(jj == z * 16 + ii, docs, 0).astype(F32), axis=1, keepdims=True)
    sel_out = jnp.where(jj.astype(F32) == wanted, 1.0, 0.0).astype(BF16)
    picked = jnp.dot(sel_out, dz[...].reshape(128, 256), preferred_element_type=F32)
    outd_ref[...] = picked[:, :224].astype(BF16)
    s1.finish()
    for copy in copies:
        copy.wait_send()
    f0.close()
    f1.close()
    s0.close()
    s1.close()


def whole(xt, xd, wq_a, wkv_a, q_gain, kv_gain, freq, doc_len, docs, wq_b, wkv_b, wo):
    vm = pl.BlockSpec(memory_space=pltpu.VMEM)
    hbm = pl.BlockSpec(memory_space=pl.ANY)
    dma = pltpu.SemaphoreType.DMA
    shapes = [
        (xt.shape, BF16), (wq_a.shape, BF16), (wkv_a.shape, BF16), (xd.shape, BF16), (q_gain.shape, F32),
        (kv_gain.shape, F32), (freq.shape, F32), (doc_len.shape, jnp.int32), (docs.shape, jnp.int32),
        (wq_b.shape, BF16), (wkv_b.shape, BF16), (wo.shape, BF16), (wo.shape[::-1], BF16),
        ((wq_a.shape[0], W - QL), BF16),
        ((2, 2, 4, 4, 8, HALF), F32), ((2, 2, 4, 4, 8, HALF), F32),
        ((2, 4, 4, 8, HALF), F32), ((2, 4, 4, 8, HALF), F32),
        ((2, 2, 4, 8, HALF), F32), ((2, 2, 4, 8, HALF), F32),
        ((2, 4, 8, HALF), F32), ((2, 4, 8, HALF), F32),
        ((2, 4, 8, HALF), F32), ((2, 4, 8, HALF), F32),
        ((2, 3, 8, HALF), F32), ((2, 3, 8, HALF), F32),
        ((8,) + xd.shape, BF16), ((2, 8, W), F32), ((8, W), F32),
        ((16, 8, 256), F32), ((16, 8, 256), F32), ((16, 8, 128), F32), ((2, 8, W), F32),
        ((2, 16, HALF), F32), ((2, 2, 16, 128), F32), ((2, 16, 128), F32), ((8, HALF), F32),
        ((2, 2, NX, NY, 16, HALF), BF16), ((16, W), BF16), ((4, 16, KL), BF16), ((4, 16, 128), BF16), ((512, 128), F32), ((512, 128), F32), ((512, 128), F32),
        ((512, wkv_b.shape[1]), BF16), ((2, 512, 128), BF16), ((512, 512), BF16), ((16, 512), BF16),
        ((2, 2, 4, 4, 112, 256), BF16), ((2, 2, 4, 4, 112, 256), BF16),
        ((2, 4, 4, 112, 256), BF16), ((2, 4, 4, 112, 256), BF16),
        ((2, 2, 4, 112, 256), BF16), ((2, 2, 4, 112, 256), BF16),
        ((2, 4, 112, 256), BF16), ((2, 4, 112, 256), BF16),
        ((2, 4, 112, 256), BF16), ((2, 4, 112, 256), BF16),
        ((2, 3, 112, 256), BF16), ((2, 3, 112, 256), BF16),
        ((2, 16, 16, 256), BF16), ((16, 16, 256), BF16), ((16, 16, 256), BF16),
        ((8, 16, 256), BF16),
    ]
    counts = (12, 8, 8, 16, 16, 36, 36, 1, 1, 16, 16, 16, 16, 28, 28, 1, 1, 36, 36, 16, 16, 1, 1, 16, 16, 8, 8, 2, 2)
    return pl.pallas_call(
        whole_kernel,
        out_shape=(jax.ShapeDtypeStruct((224, 512), BF16), jax.ShapeDtypeStruct((16, 224), BF16)),
        in_specs=[hbm] * 12,
        out_specs=(vm, vm),
        scratch_shapes=[pltpu.VMEM(shape, kind) for shape, kind in shapes] + [dma((n,)) for n in counts],
        compiler_params=pltpu.CompilerParams(
            collective_id=0, has_side_effects=True, vmem_limit_bytes=VMEM_LIMIT
        ),
        name="whole",
    )(xt, xd, wq_a, wkv_a, q_gain, kv_gain, freq, doc_len, docs, wq_b, wkv_b, wo)


def hand_over_kernel(a_ref, b_ref, out_ref, outd_ref):
    out_ref[...] = a_ref[...]
    outd_ref[...] = b_ref[...]


def hand_over(a, b):
    vm = pl.BlockSpec(memory_space=pltpu.VMEM)
    return pl.pallas_call(
        hand_over_kernel,
        out_shape=(jax.ShapeDtypeStruct(a.shape, a.dtype), jax.ShapeDtypeStruct(b.shape, b.dtype)),
        in_specs=[vm, vm],
        out_specs=(vm, vm),
        name="hand_over",
    )(a, b)


def per_device(x_pre, x_dec, wq_a, wkv_a, q_gain, kv_gain, wq_b, wkv_b, wo, doc_len, request_docs):
    half = RD // 2
    freq = np.tile(10000.0 ** (-np.arange(half) / half), 4).astype(np.float32)[None, :]
    out_t, out_dec = whole(
        x_pre.T, x_dec, wq_a, wkv_a, q_gain, kv_gain, jnp.asarray(freq), doc_len, request_docs, wq_b, wkv_b, wo
    )
    out_t, out_dec = hand_over(out_t, out_dec)
    return out_t.T, out_dec


def solution(mesh):
    placed = (
        P(("role", "grp"), "tp"),
        P(("role", "grp"), "tp"),
        P("tp", None),
        P("tp", None),
        P(),
        P(),
        P(None, "tp"),
        P(None, "tp"),
        P("tp", None),
        P(),
        P(),
    )
    return jax.shard_map(
        per_device,
        mesh=mesh,
        in_specs=placed,
        out_specs=(P(("role", "grp"), "tp"), P(("role", "grp"), "tp")),
        check_vma=False,
    )
```
